32 devices in a mesh: dp: 8 (over z, y), seq: 4 (over x, core).
Axes of the slice: x: 2, y: 2, z: 4, core: 2. Of those that a mesh axis runs over, the one named last changes fastest.
Arguments:
- enc_input: bfloat16 [192, 98, 768], P(('dp', 'seq')), may hold values from -6 to 6
- keep_count: int32 [192], P(('dp', 'seq')), may hold values from 40 to 98, as said below
- keep_positions: int32 [192, 98], P(('dp', 'seq')), may hold values from 0 to 195, as said below
- enc_gain_one: bfloat16 [768], replicated, may hold values from 0.099609375 to 1.8984375
- enc_qkv_weight: bfloat16 [768, 2304], replicated, may hold values from -0.21875 to 0.21875
- enc_out_weight: bfloat16 [768, 768], replicated, may hold values from -0.625 to 0.625
- enc_gain_two: bfloat16 [768], replicated, may hold values from 0.099609375 to 1.8984375
- enc_up_weight: bfloat16 [768, 3072], replicated, may hold values from -0.21875 to 0.21875
- enc_down_weight: bfloat16 [3072, 768], replicated, may hold values from -0.15625 to 0.15625
- embed_weight: bfloat16 [768, 512], replicated, may hold values from -0.21875 to 0.21875
- mask_token: bfloat16 [512], replicated, may hold values from -4 to 4
- dec_gain_one: bfloat16 [512], replicated, may hold values from 0.099609375 to 1.8984375
- dec_qkv_weight: bfloat16 [512, 1536], replicated, may hold values from -0.25 to 0.25
- dec_out_weight: bfloat16 [512, 512], replicated, may hold values from -0.75 to 0.75
- dec_gain_two: bfloat16 [512], replicated, may hold values from 0.099609375 to 1.8984375
- dec_up_weight: bfloat16 [512, 2048], replicated, may hold values from -0.25 to 0.25
- dec_down_weight: bfloat16 [2048, 512], replicated, may hold values from -0.1875 to 0.1875
- cotangent: bfloat16 [192, 196, 512], P(('dp', 'seq')), may hold values from -6 to 6
Outputs:
- dec_output: bfloat16 [192, 196, 512], P(('dp', 'seq'))
- enc_input_grad: float32 [192, 98, 768], P(('dp', 'seq'))
- enc_gain_one_grad: float32 [768], P(('dp', 'seq'))
- enc_qkv_grad: float32 [768, 2304], P(('dp', 'seq'))
- enc_out_grad: float32 [768, 768], P(('dp', 'seq'))
- enc_gain_two_grad: float32 [768], P(('dp', 'seq'))
- enc_up_grad: float32 [768, 3072], P(('dp', 'seq'))
- enc_down_grad: float32 [3072, 768], P(('dp', 'seq'))
- embed_grad: float32 [768, 512], P(('dp', 'seq'))
- mask_token_grad: float32 [512], P(('dp', 'seq'))
- dec_gain_one_grad: float32 [512], P(('dp', 'seq'))
- dec_qkv_grad: float32 [512, 1536], P(('dp', 'seq'))
- dec_out_grad: float32 [512, 512], P(('dp', 'seq'))
- dec_gain_two_grad: float32 [512], P(('dp', 'seq'))
- dec_up_grad: float32 [512, 2048], P(('dp', 'seq'))
- dec_down_grad: float32 [2048, 512], P(('dp', 'seq'))
The draws below stay inside these ranges and needn't reach their ends.
Inputs may be any that keep to these rules, and one draw needn't show every extreme that they name: `keep_count`: the number of visible patches of each image; some image has 98 and some image has 40. `keep_positions`: the entries of a row are distinct; the first keep_count entries are the image's visible patch positions, the others are unused.
All inputs are finite; a program needn't handle non-finite values.
Results may differ from the reference program's by a relative error of at most 0.02.
Values sent between devices are 32-bit elements; how exact they have to be, the bound alone decides.
A program may use at most 192 MiB of HBM per device.

```python
import math
import jax
import jax.numpy as jnp
from jax import lax

D = 768
HEADS = 12
FF = 3072
DD = 512
DHEADS = 16
FD = 2048
PATCHES = 196
KEEP = 98
MIN_KEEP = 40
IMAGES = 192


def draw_keep_count(key, part):
    key = jax.random.fold_in(key, 11)
    key_count, key_high, key_low = jax.random.split(key, 3)
    counts = jax.random.randint(key_count, (IMAGES,), MIN_KEEP, KEEP + 1)
    high_place = jax.random.randint(key_high, (), 0, IMAGES)
    low_place = (high_place + 1 + jax.random.randint(key_low, (), 0, IMAGES - 1)) % IMAGES
    counts = counts.at[high_place].set(KEEP)
    counts = counts.at[low_place].set(MIN_KEEP)
    return counts.astype(jnp.int32)


def shuffle_one(one_key):
    return jax.random.permutation(one_key, PATCHES)


def draw_keep_positions(key, part):
    key = jax.random.fold_in(key, 23)
    image_keys = jax.random.split(key, IMAGES)
    shuffled = jax.vmap(shuffle_one)(image_keys)
    return shuffled[:, :KEEP].astype(jnp.int32)


def shard_levels(stream_key, dims, shards, smallest, largest):
    def one(axis_at, shards_of):
        heights = jax.random.uniform(jax.random.fold_in(jax.random.fold_in(stream_key, 6), axis_at), (shards_of,), jnp.float32, smallest / len(shards), largest / len(shards))
        return jnp.repeat(jnp.exp(heights), dims[axis_at] // shards_of).reshape((-1,) + (1,) * (len(dims) - axis_at - 1))

    gain = one(*shards[0])
    for cut in shards[1:]:
        gain = gain * one(*cut)
    return gain


def gaussian(own_key, extent, deviation, limit, cuts=(), dtype=jnp.bfloat16):
    array = jax.random.normal(own_key, extent, jnp.float32) * deviation
    if len(cuts) > 0:
        array = shard_levels(own_key, extent, cuts, -0.22, 0.18) * array
    return jnp.clip(array, min=-limit, max=limit).astype(dtype)


def setup_inputs(seed: int = 0) -> dict:
    key_list = jax.random.split(jax.random.key(seed), 19)
    enc_input = gaussian(key_list[0], (IMAGES, KEEP, D), 1.0, 6.0, ((0, 32),))
    keep_count = draw_keep_count(jax.random.fold_in(key_list[18], 71), 0)
    keep_positions = draw_keep_positions(jax.random.fold_in(key_list[18], 71), 0)
    enc_gain_one = jnp.clip(1.0 + 0.18 * jax.random.normal(key_list[3], (D,), jnp.float32), 0.099609375, 1.8984375).astype(jnp.bfloat16)
    enc_qkv_weight = gaussian(key_list[4], (D, 3 * D), D ** -0.5, 0.21875)
    enc_out_weight = gaussian(key_list[5], (D, D), (D // 8) ** -0.5, 0.625)
    enc_gain_two = jnp.clip(1.0 + 0.18 * jax.random.normal(key_list[6], (D,), jnp.float32), 0.099609375, 1.8984375).astype(jnp.bfloat16)
    enc_up_weight = gaussian(key_list[7], (D, FF), D ** -0.5, 0.21875)
    enc_down_weight = gaussian(key_list[8], (FF, D), (FF // 2) ** -0.5, 0.15625)
    embed_weight = gaussian(key_list[9], (D, DD), D ** -0.5, 0.21875)
    mask_token = gaussian(key_list[10], (DD,), 1.0, 4.0)
    dec_gain_one = jnp.clip(1.0 + 0.18 * jax.random.normal(key_list[11], (DD,), jnp.float32), 0.099609375, 1.8984375).astype(jnp.bfloat16)
    dec_qkv_weight = gaussian(key_list[12], (DD, 3 * DD), DD ** -0.5, 0.25)
    dec_out_weight = gaussian(key_list[13], (DD, DD), (DD // 8) ** -0.5, 0.75)
    dec_gain_two = jnp.clip(1.0 + 0.18 * jax.random.normal(key_list[14], (DD,), jnp.float32), 0.099609375, 1.8984375).astype(jnp.bfloat16)
    dec_up_weight = gaussian(key_list[15], (DD, FD), DD ** -0.5, 0.25)
    dec_down_weight = gaussian(key_list[16], (FD, DD), (FD // 2) ** -0.5, 0.1875)
    cotangent = gaussian(key_list[17], (IMAGES, PATCHES, DD), 1.0, 6.0, ((0, 32),))
    return dict(enc_input=enc_input, keep_count=keep_count, keep_positions=keep_positions, enc_gain_one=enc_gain_one, enc_qkv_weight=enc_qkv_weight, enc_out_weight=enc_out_weight, enc_gain_two=enc_gain_two, enc_up_weight=enc_up_weight, enc_down_weight=enc_down_weight, embed_weight=embed_weight, mask_token=mask_token, dec_gain_one=dec_gain_one, dec_qkv_weight=dec_qkv_weight, dec_out_weight=dec_out_weight, dec_gain_two=dec_gain_two, dec_up_weight=dec_up_weight, dec_down_weight=dec_down_weight, cotangent=cotangent)


@jax.custom_vjp
def low(v):
    return lax.optimization_barrier(v.astype(jnp.bfloat16)).astype(jnp.float32)

@jax.custom_vjp
def low_back(v):
    return v

def low_keep(v):
    return (low(v), None)

def low_pass(kept, grad):
    return (grad,)

def back_keep(v):
    return (v, None)

def back_low(kept, grad):
    return (low(grad),)
low.defvjp(low_keep, low_pass)
low_back.defvjp(back_keep, back_low)
eps = 1e-06
highest = lax.Precision.HIGHEST

def position_table(count, model_width):
    grid_side = math.isqrt(count)
    quarter = model_width // 4
    places = jnp.arange(count)
    across = (places % grid_side).astype(jnp.float32)
    row_place = (places // grid_side).astype(jnp.float32)
    frequency = 1.0 / 10000.0 ** (jnp.arange(quarter).astype(jnp.float32) / quarter)
    return jnp.concatenate([jnp.sin(across[:, None] * frequency), jnp.cos(across[:, None] * frequency), jnp.sin(row_place[:, None] * frequency), jnp.cos(row_place[:, None] * frequency)], axis=1)

def layer_norm(stream, gain_vec):
    row_mean = lax.optimization_barrier(jnp.mean(stream, axis=-1, keepdims=True))
    centered = stream - row_mean
    variance = lax.optimization_barrier(jnp.mean(centered * centered, axis=-1, keepdims=True))
    return centered * lax.rsqrt(variance + eps) * gain_vec

def project(operand, matrix):
    return jnp.einsum('bsi,ij->bsj', operand, matrix, precision=highest)

def attention(hidden, qkv_weight, out_weight, head_count, key_mask):
    batch_size, row_count, model_width = hidden.shape
    head_size = model_width // head_count
    packed = low_back(low(project(low(hidden), qkv_weight)))
    queries = packed[:, :, :model_width].reshape(batch_size, row_count, head_count, head_size)
    key_rows = packed[:, :, model_width:2 * model_width].reshape(batch_size, row_count, head_count, head_size)
    value_rows = packed[:, :, 2 * model_width:].reshape(batch_size, row_count, head_count, head_size)
    scores = jnp.einsum('bqhd,bkhd->bhqk', queries, key_rows, precision=highest) * head_size ** (-0.5)
    if key_mask is not None:
        scores = jnp.where(key_mask[:, None, None, :], scores, -1e+30)
    scores = low_back(scores)
    row_max = lax.optimization_barrier(jnp.max(scores, axis=-1, keepdims=True))
    raised = jnp.exp(scores - row_max)
    attn_weights = raised / lax.optimization_barrier(jnp.sum(raised, axis=-1, keepdims=True))
    mixed_heads = jnp.einsum('bhqk,bkhd->bqhd', low(attn_weights), value_rows, precision=highest)
    mixed_heads = low_back(low(mixed_heads.reshape(batch_size, row_count, model_width)))
    return low_back(project(mixed_heads, out_weight))

def feed_forward(hidden, up_weight, down_weight):
    pre_act = low_back(project(low(hidden), up_weight))
    active = low(jax.nn.gelu(pre_act, approximate=False))
    return low_back(project(active, down_weight))

def block(stream, gain_one, qkv_weight, out_weight, gain_two, up_weight, down_weight, head_count, key_mask):
    middle = stream + attention(layer_norm(stream, gain_one), qkv_weight, out_weight, head_count, key_mask)
    return middle + feed_forward(layer_norm(middle, gain_two), up_weight, down_weight)

def decoder_input(encoded, live_slots, positions, embed_weight, mask_token):
    embedded = project(low(encoded), embed_weight)
    places = jnp.arange(PATCHES)
    matches = (positions[:, :, None] == places[None, None, :]) & live_slots[:, :, None]
    covered = jnp.any(matches, axis=1)
    slot_index = lax.optimization_barrier(jnp.sum(jnp.where(matches, jnp.arange(KEEP)[None, :, None], 0), axis=1)).astype(jnp.int32)
    picked = jnp.take_along_axis(embedded, slot_index[:, :, None], axis=1)
    filled = jnp.where(covered[:, :, None], picked, mask_token) + position_table(PATCHES, embedded.shape[-1])
    return low_back(low(filled))

def reference(enc_input, keep_count, keep_positions, enc_gain_one, enc_qkv_weight, enc_out_weight, enc_gain_two, enc_up_weight, enc_down_weight, embed_weight, mask_token, dec_gain_one, dec_qkv_weight, dec_out_weight, dec_gain_two, dec_up_weight, dec_down_weight, cotangent):
    weights = tuple((weight_array.astype(jnp.float32) for weight_array in (enc_gain_one, enc_qkv_weight, enc_out_weight, enc_gain_two, enc_up_weight, enc_down_weight, embed_weight, mask_token, dec_gain_one, dec_qkv_weight, dec_out_weight, dec_gain_two, dec_up_weight, dec_down_weight)))
    group_size = 16
    image_total = enc_input.shape[0]

    def forward(enc_rows, *params):

        def one_group(pieces):
            stream, counts, positions = pieces
            live_slots = jnp.arange(KEEP)[None, :] < counts[:, None]
            encoded = block(stream, params[0], params[1], params[2], params[3], params[4], params[5], HEADS, live_slots)
            decoded = decoder_input(encoded, live_slots, positions, params[6], params[7])
            return block(decoded, params[8], params[9], params[10], params[11], params[12], params[13], DHEADS, None)
        stacked = lax.map(jax.checkpoint(one_group), (enc_rows.reshape(image_total // group_size, group_size, KEEP, D), keep_count.reshape(image_total // group_size, group_size), keep_positions.reshape(image_total // group_size, group_size, KEEP)))
        return stacked.reshape(image_total, PATCHES, DD)
    output, pullback = jax.vjp(forward, enc_input.astype(jnp.float32), *weights)
    gradients = pullback(cotangent.astype(jnp.float32))
    return (output.astype(jnp.bfloat16), gradients[0], gradients[1], gradients[2], gradients[3], gradients[4], gradients[5], gradients[6], gradients[7], gradients[8], gradients[9], gradients[10], gradients[11], gradients[12], gradients[13], gradients[14])
```

```python
import functools
import math

import jax
import jax.numpy as jnp
from jax import lax
from jax.experimental import pallas as pl
from jax.experimental.pallas import tpu as pltpu
from jax.sharding import PartitionSpec as P

HEADS = 12
DHEADS = 16
PATCHES = 196


eps = 1e-06


def position_table(count, model_width):
    grid_side = math.isqrt(count)
    quarter = model_width // 4
    places = jnp.arange(count)
    across = (places % grid_side).astype(jnp.float32)
    row_place = (places // grid_side).astype(jnp.float32)
    frequency = 1.0 / 10000.0 ** (jnp.arange(quarter).astype(jnp.float32) / quarter)
    return jnp.concatenate(
        [
            jnp.sin(across[:, None] * frequency),
            jnp.cos(across[:, None] * frequency),
            jnp.sin(row_place[:, None] * frequency),
            jnp.cos(row_place[:, None] * frequency),
        ],
        axis=1,
    )


def contract(operand, matrix):
    return jnp.einsum("...i,ij->...j", operand, matrix, preferred_element_type=jnp.float32)


def contract_back(gradient, matrix):
    return jnp.einsum("...j,ij->...i", gradient, matrix, preferred_element_type=jnp.float32)


def outer_sum(operand, gradient):
    flat_left = operand.reshape(-1, operand.shape[-1])
    flat_right = gradient.reshape(-1, gradient.shape[-1])
    return lax.dot_general(
        flat_left, flat_right, (((0,), (0,)), ((), ())), preferred_element_type=jnp.float32
    )


def exact_gelu(values):
    return jax.nn.gelu(values, approximate=False)


def gelu_back(pre_act, grad_active):
    unused, pullback = jax.vjp(exact_gelu, pre_act)
    return pullback(grad_active)[0]


def layer_norm(stream, gain_vec):
    row_mean = jnp.mean(stream, axis=-1, keepdims=True)
    centered = stream - row_mean
    inverse = lax.rsqrt(jnp.mean(centered * centered, axis=-1, keepdims=True) + eps)
    unit_rows = centered * inverse
    return (unit_rows * gain_vec, unit_rows, inverse)


def layer_norm_back(grad_normed, unit_rows, inverse, gain_vec):
    grad_gain = jnp.sum((grad_normed * unit_rows).reshape(-1, unit_rows.shape[-1]), axis=0)
    grad_unit = grad_normed * gain_vec
    grad_stream = inverse * (
        grad_unit
        - jnp.mean(grad_unit, axis=-1, keepdims=True)
        - unit_rows * jnp.mean(grad_unit * unit_rows, axis=-1, keepdims=True)
    )
    return (grad_stream, grad_gain)


def attend(packed, head_count, key_mask):
    batch_size, row_count, triple_width = packed.shape
    model_width = triple_width // 3
    head_size = model_width // head_count
    queries = packed[:, :, :model_width].reshape(batch_size, row_count, head_count, head_size)
    key_heads = packed[:, :, model_width : 2 * model_width].reshape(
        batch_size, row_count, head_count, head_size
    )
    value_heads = packed[:, :, 2 * model_width :].reshape(
        batch_size, row_count, head_count, head_size
    )
    scores = jnp.einsum(
        "bqhd,bkhd->bhqk", queries, key_heads, preferred_element_type=jnp.float32
    ) * head_size ** (-0.5)
    if key_mask is not None:
        scores = jnp.where(key_mask[:, None, None, :], scores, -1e30)
    row_max = jnp.max(scores, axis=-1, keepdims=True)
    raised = jnp.exp(scores - row_max)
    attn_weights = raised / jnp.sum(raised, axis=-1, keepdims=True)
    attn_low = attn_weights.astype(jnp.bfloat16)
    mixed_heads = jnp.einsum(
        "bhqk,bkhd->bqhd", attn_low, value_heads, preferred_element_type=jnp.float32
    )
    mixed_heads = mixed_heads.reshape(batch_size, row_count, model_width).astype(jnp.bfloat16)
    return (mixed_heads, attn_weights, attn_low)


def attend_back(packed, attn_weights, attn_low, grad_mixed, head_count):
    batch_size, row_count, triple_width = packed.shape
    model_width = triple_width // 3
    head_size = model_width // head_count
    factor = head_size ** (-0.5)
    queries = packed[:, :, :model_width].reshape(batch_size, row_count, head_count, head_size)
    key_heads = packed[:, :, model_width : 2 * model_width].reshape(
        batch_size, row_count, head_count, head_size
    )
    value_heads = packed[:, :, 2 * model_width :].reshape(
        batch_size, row_count, head_count, head_size
    )
    grad_heads = grad_mixed.reshape(batch_size, row_count, head_count, head_size)
    grad_values = jnp.einsum(
        "bhqk,bqhd->bkhd", attn_low, grad_heads, preferred_element_type=jnp.float32
    )
    grad_attn = jnp.einsum(
        "bqhd,bkhd->bhqk", grad_heads, value_heads, preferred_element_type=jnp.float32
    )
    grad_scores = attn_weights * (
        grad_attn - jnp.sum(attn_weights * grad_attn, axis=-1, keepdims=True)
    )
    grad_scores = grad_scores.astype(jnp.bfloat16)
    grad_queries = (
        jnp.einsum("bhqk,bkhd->bqhd", grad_scores, key_heads, preferred_element_type=jnp.float32)
        * factor
    )
    grad_keys = (
        jnp.einsum("bhqk,bqhd->bkhd", grad_scores, queries, preferred_element_type=jnp.float32)
        * factor
    )
    grad_packed = jnp.concatenate(
        [
            grad_queries.reshape(batch_size, row_count, model_width),
            grad_keys.reshape(batch_size, row_count, model_width),
            grad_values.reshape(batch_size, row_count, model_width),
        ],
        axis=-1,
    )
    return grad_packed.astype(jnp.bfloat16)


def mlp_forward(middle, gain_two, up_weight, down_weight):
    normed_two, unit_two, inverse_two = layer_norm(middle, gain_two.astype(jnp.float32))
    second_low = normed_two.astype(jnp.bfloat16)
    pre_act = contract(second_low, up_weight)
    active_low = exact_gelu(pre_act).astype(jnp.bfloat16)
    result = middle + contract(active_low, down_weight)
    return (
        result,
        {
            "unit_two": unit_two,
            "inverse_two": inverse_two,
            "second_low": second_low,
            "pre_act": pre_act,
            "active_low": active_low,
        },
    )


def mlp_backward(grad_result, kept_values, gain_two, up_weight, down_weight):
    grad_branch = grad_result.astype(jnp.bfloat16)
    grad_down = outer_sum(kept_values["active_low"], grad_branch)
    grad_active = contract_back(grad_branch, down_weight)
    grad_pre = gelu_back(kept_values["pre_act"], grad_active).astype(jnp.bfloat16)
    grad_up = outer_sum(kept_values["second_low"], grad_pre)
    grad_second = contract_back(grad_pre, up_weight)
    grad_middle, grad_gain_two = layer_norm_back(
        grad_second,
        kept_values["unit_two"],
        kept_values["inverse_two"],
        gain_two.astype(jnp.float32),
    )
    return (grad_middle + grad_result, grad_gain_two, grad_up, grad_down)


def block_forward(stream, weights, head_count, key_mask):
    gain_one, qkv_weight, out_weight, gain_two, up_weight, down_weight = weights
    normed_one, unit_one, inverse_one = layer_norm(stream, gain_one.astype(jnp.float32))
    normed_low = normed_one.astype(jnp.bfloat16)
    packed = contract(normed_low, qkv_weight).astype(jnp.bfloat16)
    mixed_heads, attn_weights, attn_low = attend(packed, head_count, key_mask)
    middle = stream + contract(mixed_heads, out_weight)
    result, mlp_kept = mlp_forward(middle, gain_two, up_weight, down_weight)
    kept_values = {
        "unit_one": unit_one,
        "inverse_one": inverse_one,
        "normed_low": normed_low,
        "packed": packed,
        "attn_weights": attn_weights,
        "attn_low": attn_low,
        "mixed_heads": mixed_heads,
        "mlp": mlp_kept,
    }
    return (result, kept_values)


def block_backward(grad_result, kept_values, weights, head_count):
    gain_one, qkv_weight, out_weight, gain_two, up_weight, down_weight = weights
    grad_middle, grad_gain_two, grad_up, grad_down = mlp_backward(
        grad_result, kept_values["mlp"], gain_two, up_weight, down_weight
    )
    grad_attend = grad_middle.astype(jnp.bfloat16)
    grad_out = outer_sum(kept_values["mixed_heads"], grad_attend)
    grad_mixed = contract_back(grad_attend, out_weight).astype(jnp.bfloat16)
    grad_packed = attend_back(
        kept_values["packed"],
        kept_values["attn_weights"],
        kept_values["attn_low"],
        grad_mixed,
        head_count,
    )
    grad_qkv = outer_sum(kept_values["normed_low"], grad_packed)
    grad_normed = contract_back(grad_packed, qkv_weight)
    grad_stream, grad_gain_one = layer_norm_back(
        grad_normed,
        kept_values["unit_one"],
        kept_values["inverse_one"],
        gain_one.astype(jnp.float32),
    )
    return (
        grad_stream + grad_middle,
        grad_gain_one,
        grad_qkv,
        grad_out,
        grad_gain_two,
        grad_up,
        grad_down,
    )


def micro_step(
    enc_rows, counts, positions, cot_rows, enc_weights, embed_weight, mask_token, dec_weights
):
    slot_total = enc_rows.shape[1]
    live_slots = jnp.arange(slot_total)[None, :] < counts[:, None]
    encoded, enc_kept = block_forward(enc_rows.astype(jnp.float32), enc_weights, HEADS, live_slots)
    encoded_low = encoded.astype(jnp.bfloat16)
    embedded = contract(encoded_low, embed_weight)
    places = jnp.arange(PATCHES)
    matches = (positions[:, :, None] == places[None, None, :]) & live_slots[:, :, None]
    covered = jnp.any(matches, axis=1)
    pick = matches.astype(jnp.bfloat16)
    high = embedded.astype(jnp.bfloat16)
    low = (embedded - high.astype(jnp.float32)).astype(jnp.bfloat16)
    picked = jnp.einsum("bjp,bjw->bpw", pick, high, preferred_element_type=jnp.float32)
    picked = picked + jnp.einsum("bjp,bjw->bpw", pick, low, preferred_element_type=jnp.float32)
    filled = jnp.where(covered[:, :, None], picked, mask_token.astype(jnp.float32))
    filled = filled + position_table(PATCHES, embedded.shape[-1])
    filled_low = filled.astype(jnp.bfloat16)
    decoded, dec_kept = block_forward(filled_low.astype(jnp.float32), dec_weights, DHEADS, None)
    dec_piece = decoded.astype(jnp.bfloat16)
    dec_back = block_backward(cot_rows.astype(jnp.float32), dec_kept, dec_weights, DHEADS)
    dec_terms = dec_back[1:]
    grad_filled = dec_back[0].astype(jnp.bfloat16).astype(jnp.float32)
    mask_term = jnp.sum(
        jnp.where(covered[:, :, None], 0.0, grad_filled).reshape(-1, grad_filled.shape[-1]), axis=0
    )
    grad_embedded = jnp.einsum(
        "bjp,bpw->bjw", pick, grad_filled.astype(jnp.bfloat16), preferred_element_type=jnp.float32
    ).astype(jnp.bfloat16)
    embed_term = outer_sum(encoded_low, grad_embedded)
    grad_encoded = contract_back(grad_embedded, embed_weight)
    enc_back = block_backward(grad_encoded, enc_kept, enc_weights, HEADS)
    grad_input = enc_back[0]
    enc_terms = enc_back[1:] + (embed_term, mask_term)
    return (dec_piece, grad_input, tuple(enc_terms) + tuple(dec_terms))


MESH = pl.DeviceIdType.MESH
W = 256
STEP = 64
FLOWS = ((0, 24, "xyls"), (24, 24, "yxls"), (48, 8, "lsxy"), (56, 8, "lsyx"))
DIMS = "slyx"

def coords():
    seq = lax.axis_index("seq"); dp = lax.axis_index("dp")
    return {"s": dp // 4, "l": (dp // 2) % 2, "y": dp % 2, "x": seq // 2, "c": seq % 2}

def partner(here, dim):
    other = dict(here); other[dim] = 1 - here[dim]
    return (other["s"] * 4 + other["l"] * 2 + other["y"], other["x"] * 2 + other["c"])

def comm_scratch(nt):
    sc = [pltpu.VMEM((nt, 2, 2, 2, 2, STEP, W), jnp.float32)]
    for _, rows, order in FLOWS:
        for k in range(1, 5):
            sc.append(pltpu.VMEM((nt,) + (2,) * (4 - k) + (rows, W), jnp.float32))
    sc.append(pltpu.VMEM((2, 2, 2, 2, 2, STEP, W), jnp.float32))
    sc += [pltpu.SemaphoreType.DMA((nt, 17)), pltpu.SemaphoreType.DMA((nt, 17)), pltpu.SemaphoreType.DMA((2,))]
    return sc

class Comm:
    def __init__(self, g_ref, out_ref, scratch, nt):
        self.g, self.out, self.nt = g_ref, out_ref, nt
        self.land0 = scratch[0]
        self.lands = [scratch[1 + 4 * f: 5 + 4 * f] for f in range(4)]
        self.own, self.ssem, self.rsem, self.lsem = scratch[17:21]
        self.here = coords()

    def barrier(self):
        bar = pltpu.get_barrier_semaphore()
        for d in "c" + DIMS:
            pl.semaphore_signal(bar, inc=1, device_id=partner(self.here, d), device_id_type=MESH)
        pl.semaphore_wait(bar, 5)

    def core_copy(self, t):
        rows = pl.ds(pl.multiple_of(t * STEP, STEP), STEP)
        return pltpu.make_async_remote_copy(
            src_ref=self.g.at[:, :, :, :, 1 - self.here["c"], rows], dst_ref=self.land0.at[t],
            send_sem=self.ssem.at[t, 16], recv_sem=self.rsem.at[t, 16],
            device_id=partner(self.here, "c"), device_id_type=MESH)

    def own_copy(self, t):
        rows = pl.ds(pl.multiple_of(t * STEP, STEP), STEP)
        return pltpu.make_async_copy(self.g.at[:, :, :, :, self.here["c"], rows], self.own.at[t % 2], self.lsem.at[t % 2])

    def source(self, t, f, k, mine):
        off, rows, order = FLOWS[f]
        left = "".join(d for d in DIMS if d not in order[:k])
        d = order[k]
        pick = tuple((self.here[d] if mine else 1 - self.here[d]) if e == d else slice(None) for e in left)
        if k == 0:
            return self.land0.at[(t,) + pick + (pl.ds(off, rows),)]
        return self.lands[f][k - 1].at[(t,) + pick]

    def copy(self, t, f, k):
        d = FLOWS[f][2][k]
        i = f * 4 + k
        return pltpu.make_async_remote_copy(
            src_ref=self.source(t, f, k, False), dst_ref=self.lands[f][k].at[t],
            send_sem=self.ssem.at[t, i], recv_sem=self.rsem.at[t, i],
            device_id=partner(self.here, d), device_id_type=MESH)

    def stage(self, k, t):
        if k == 0:
            self.core_copy(t).start()
            self.own_copy(t).start()
        elif k == 1:
            self.own_copy(t).wait()
            self.core_copy(t).wait()
            self.land0[t] += self.own[t % 2]
            for f in range(4):
                self.copy(t, f, 0).start()
        else:
            for f in range(4):
                self.copy(t, f, k - 2).wait()
                land = self.lands[f][k - 2]
                kept = self.source(t, f, k - 2, True)
                if k < 5:
                    land[t] += kept[...]
                    self.copy(t, f, k - 1).start()
                else:
                    off, rows, _ = FLOWS[f]
                    at = pl.ds(pl.multiple_of(t * STEP + off, 8), rows)
                    self.out[at] = land[t] + kept[...]

    def step(self, t):
        for k in range(6):
            p = t - k
            @pl.when((p >= 0) & (p < self.nt))
            def _():
                self.stage(k, p)

def comm_only_kernel(nt, g_ref, out_ref, *scratch):
    comm = Comm(g_ref, out_ref, scratch, nt)
    comm.barrier()
    def body(t, _):
        comm.step(t); return 0
    lax.fori_loop(0, nt + 5, body, 0)

def reduce_scatter(g, nt, cid):
    return pl.pallas_call(functools.partial(comm_only_kernel, nt),
        out_shape=jax.ShapeDtypeStruct((nt * STEP, W), jnp.float32),
        in_specs=[pl.BlockSpec(memory_space=pl.ANY)], out_specs=pl.BlockSpec(memory_space=pltpu.VMEM),
        scratch_shapes=comm_scratch(nt), name="comm",
        compiler_params=pltpu.CompilerParams(collective_id=cid, has_side_effects=True, vmem_limit_bytes=60 * 2**20))(g)


GROUPS = (((13, 12, 10, 9), (8, 11)), ((6, 5, 4, 2, 1), (0, 3, 7)))


def reduce_group(totals, matrices, vectors, call):
    parts = lax.axis_size("dp") * lax.axis_size("seq")
    blocks = []
    for i in matrices:
        rows, columns = totals[i].shape
        block = totals[i].reshape(parts, rows // parts, columns // W, W)
        blocks.append(block.transpose(0, 2, 1, 3).reshape(parts, -1, W))
    vector = jnp.concatenate([totals[i].reshape(parts, -1) for i in vectors], axis=1)
    blocks.append(jnp.pad(vector, ((0, 0), (0, 8 * W - vector.shape[1]))).reshape(parts, 8, W))
    used = sum(block.shape[1] for block in blocks)
    steps = -(-used // STEP)
    blocks.append(jnp.zeros((parts, steps * STEP - used, W), jnp.float32))
    whole = jnp.concatenate(blocks, axis=1).reshape(2, 2, 2, 2, 2, steps * STEP, W)
    mine = reduce_scatter(whole, steps, call)
    out = {}
    at = 0
    for i in matrices:
        rows, columns = totals[i].shape[0] // parts, totals[i].shape[1]
        size = rows * columns // W
        out[i] = mine[at : at + size].reshape(columns // W, rows, W).transpose(1, 0, 2).reshape(rows, columns)
        at += size
    vector = mine[at]
    at = 0
    for i in vectors:
        size = totals[i].shape[0] // parts
        out[i] = vector[at : at + size]
        at += size
    return out


def reduce_all(totals):
    if (lax.axis_size("dp"), lax.axis_size("seq")) != (8, 4):
        return tuple(
            lax.psum_scatter(total, ("dp", "seq"), scatter_dimension=0, tiled=True) for total in totals
        )
    out = {}
    for call, (matrices, vectors) in enumerate(GROUPS):
        out.update(reduce_group(totals, matrices, vectors, call))
    return tuple(out[i] for i in range(len(totals)))


def local(
    enc_input,
    keep_count,
    keep_positions,
    enc_gain_one,
    enc_qkv_weight,
    enc_out_weight,
    enc_gain_two,
    enc_up_weight,
    enc_down_weight,
    embed_weight,
    mask_token,
    dec_gain_one,
    dec_qkv_weight,
    dec_out_weight,
    dec_gain_two,
    dec_up_weight,
    dec_down_weight,
    cotangent,
):
    enc_weights = (
        enc_gain_one,
        enc_qkv_weight,
        enc_out_weight,
        enc_gain_two,
        enc_up_weight,
        enc_down_weight,
    )
    dec_weights = (
        dec_gain_one,
        dec_qkv_weight,
        dec_out_weight,
        dec_gain_two,
        dec_up_weight,
        dec_down_weight,
    )
    all_params = (
        enc_gain_one,
        enc_qkv_weight,
        enc_out_weight,
        enc_gain_two,
        enc_up_weight,
        enc_down_weight,
        embed_weight,
        mask_token,
        dec_gain_one,
        dec_qkv_weight,
        dec_out_weight,
        dec_gain_two,
        dec_up_weight,
        dec_down_weight,
    )
    dec_pieces, input_grads, totals = micro_step(
        enc_input, keep_count, keep_positions, cotangent, enc_weights, embed_weight, mask_token, dec_weights
    )
    totals = reduce_all(totals)
    dec_output = dec_pieces.reshape(cotangent.shape)
    enc_input_grad = input_grads.reshape(enc_input.shape)
    return (
        dec_output,
        enc_input_grad,
        totals[0],
        totals[1],
        totals[2],
        totals[3],
        totals[4],
        totals[5],
        totals[6],
        totals[7],
        totals[8],
        totals[9],
        totals[10],
        totals[11],
        totals[12],
        totals[13],
    )


def solution(mesh):
    placed = (
        P(("dp", "seq"), None, None),
        P(("dp", "seq")),
        P(("dp", "seq"), None),
        P(),
        P(),
        P(),
        P(),
        P(),
        P(),
        P(),
        P(),
        P(),
        P(),
        P(),
        P(),
        P(),
        P(),
        P(("dp", "seq"), None, None),
    )
    return jax.shard_map(
        local,
        mesh=mesh,
        in_specs=placed,
        out_specs=(
            P(("dp", "seq"), None, None),
            P(("dp", "seq"), None, None),
            P(("dp", "seq")),
            P(("dp", "seq"), None),
            P(("dp", "seq"), None),
            P(("dp", "seq")),
            P(("dp", "seq"), None),
            P(("dp", "seq"), None),
            P(("dp", "seq"), None),
            P(("dp", "seq")),
            P(("dp", "seq")),
            P(("dp", "seq"), None),
            P(("dp", "seq"), None),
            P(("dp", "seq")),
            P(("dp", "seq"), None),
            P(("dp", "seq"), None),
        ),
        check_vma=False,
    )
```

```python
import functools
import math

import jax
import jax.numpy as jnp
import numpy as np
from jax import lax
from jax.experimental import pallas as pl
from jax.experimental.pallas import tpu as pltpu
from jax.sharding import PartitionSpec as P

HEADS = 12
DHEADS = 16
PATCHES = 196


eps = 1e-06


def position_table(count, model_width):
    grid_side = math.isqrt(count)
    quarter = model_width // 4
    places = jnp.arange(count)
    across = (places % grid_side).astype(jnp.float32)
    row_place = (places // grid_side).astype(jnp.float32)
    frequency = 1.0 / 10000.0 ** (jnp.arange(quarter).astype(jnp.float32) / quarter)
    return jnp.concatenate(
        [
            jnp.sin(across[:, None] * frequency),
            jnp.cos(across[:, None] * frequency),
            jnp.sin(row_place[:, None] * frequency),
            jnp.cos(row_place[:, None] * frequency),
        ],
        axis=1,
    )


def contract(operand, matrix):
    return jnp.einsum("...i,ij->...j", operand, matrix, preferred_element_type=jnp.float32)


def contract_back(gradient, matrix):
    return jnp.einsum("...j,ij->...i", gradient, matrix, preferred_element_type=jnp.float32)


def outer_sum(operand, gradient):
    flat_left = operand.reshape(-1, operand.shape[-1])
    flat_right = gradient.reshape(-1, gradient.shape[-1])
    return lax.dot_general(
        flat_left, flat_right, (((0,), (0,)), ((), ())), preferred_element_type=jnp.float32
    )


def exact_gelu(values):
    return jax.nn.gelu(values, approximate=False)


def gelu_back(pre_act, grad_active):
    unused, pullback = jax.vjp(exact_gelu, pre_act)
    return pullback(grad_active)[0]


def layer_norm(stream, gain_vec):
    row_mean = jnp.mean(stream, axis=-1, keepdims=True)
    centered = stream - row_mean
    inverse = lax.rsqrt(jnp.mean(centered * centered, axis=-1, keepdims=True) + eps)
    unit_rows = centered * inverse
    return (unit_rows * gain_vec, unit_rows, inverse)


def layer_norm_back(grad_normed, unit_rows, inverse, gain_vec):
    grad_gain = jnp.sum((grad_normed * unit_rows).reshape(-1, unit_rows.shape[-1]), axis=0)
    grad_unit = grad_normed * gain_vec
    grad_stream = inverse * (
        grad_unit
        - jnp.mean(grad_unit, axis=-1, keepdims=True)
        - unit_rows * jnp.mean(grad_unit * unit_rows, axis=-1, keepdims=True)
    )
    return (grad_stream, grad_gain)


def attend(packed, head_count, key_mask):
    batch_size, row_count, triple_width = packed.shape
    model_width = triple_width // 3
    head_size = model_width // head_count
    queries = packed[:, :, :model_width].reshape(batch_size, row_count, head_count, head_size)
    key_heads = packed[:, :, model_width : 2 * model_width].reshape(
        batch_size, row_count, head_count, head_size
    )
    value_heads = packed[:, :, 2 * model_width :].reshape(
        batch_size, row_count, head_count, head_size
    )
    scores = jnp.einsum(
        "bqhd,bkhd->bhqk", queries, key_heads, preferred_element_type=jnp.float32
    ) * head_size ** (-0.5)
    if key_mask is not None:
        scores = jnp.where(key_mask[:, None, None, :], scores, -1e30)
    row_max = jnp.max(scores, axis=-1, keepdims=True)
    raised = jnp.exp(scores - row_max)
    attn_weights = raised / jnp.sum(raised, axis=-1, keepdims=True)
    attn_low = attn_weights.astype(jnp.bfloat16)
    mixed_heads = jnp.einsum(
        "bhqk,bkhd->bqhd", attn_low, value_heads, preferred_element_type=jnp.float32
    )
    mixed_heads = mixed_heads.reshape(batch_size, row_count, model_width).astype(jnp.bfloat16)
    return (mixed_heads, attn_weights, attn_low)


def attend_back(packed, attn_weights, attn_low, grad_mixed, head_count):
    batch_size, row_count, triple_width = packed.shape
    model_width = triple_width // 3
    head_size = model_width // head_count
    factor = head_size ** (-0.5)
    queries = packed[:, :, :model_width].reshape(batch_size, row_count, head_count, head_size)
    key_heads = packed[:, :, model_width : 2 * model_width].reshape(
        batch_size, row_count, head_count, head_size
    )
    value_heads = packed[:, :, 2 * model_width :].reshape(
        batch_size, row_count, head_count, head_size
    )
    grad_heads = grad_mixed.reshape(batch_size, row_count, head_count, head_size)
    grad_values = jnp.einsum(
        "bhqk,bqhd->bkhd", attn_low, grad_heads, preferred_element_type=jnp.float32
    )
    grad_attn = jnp.einsum(
        "bqhd,bkhd->bhqk", grad_heads, value_heads, preferred_element_type=jnp.float32
    )
    grad_scores = attn_weights * (
        grad_attn - jnp.sum(attn_weights * grad_attn, axis=-1, keepdims=True)
    )
    grad_scores = grad_scores.astype(jnp.bfloat16)
    grad_queries = (
        jnp.einsum("bhqk,bkhd->bqhd", grad_scores, key_heads, preferred_element_type=jnp.float32)
        * factor
    )
    grad_keys = (
        jnp.einsum("bhqk,bqhd->bkhd", grad_scores, queries, preferred_element_type=jnp.float32)
        * factor
    )
    grad_packed = jnp.concatenate(
        [
            grad_queries.reshape(batch_size, row_count, model_width),
            grad_keys.reshape(batch_size, row_count, model_width),
            grad_values.reshape(batch_size, row_count, model_width),
        ],
        axis=-1,
    )
    return grad_packed.astype(jnp.bfloat16)


def mlp_forward(middle, gain_two, up_weight, down_weight):
    normed_two, unit_two, inverse_two = layer_norm(middle, gain_two.astype(jnp.float32))
    second_low = normed_two.astype(jnp.bfloat16)
    pre_act = contract(second_low, up_weight)
    active_low = exact_gelu(pre_act).astype(jnp.bfloat16)
    result = middle + contract(active_low, down_weight)
    return (
        result,
        {
            "unit_two": unit_two,
            "inverse_two": inverse_two,
            "second_low": second_low,
            "pre_act": pre_act,
            "active_low": active_low,
        },
    )


def mlp_backward(grad_result, kept_values, gain_two, up_weight, down_weight):
    grad_branch = grad_result.astype(jnp.bfloat16)
    grad_down = outer_sum(kept_values["active_low"], grad_branch)
    grad_active = contract_back(grad_branch, down_weight)
    grad_pre = gelu_back(kept_values["pre_act"], grad_active).astype(jnp.bfloat16)
    grad_up = outer_sum(kept_values["second_low"], grad_pre)
    grad_second = contract_back(grad_pre, up_weight)
    grad_middle, grad_gain_two = layer_norm_back(
        grad_second,
        kept_values["unit_two"],
        kept_values["inverse_two"],
        gain_two.astype(jnp.float32),
    )
    return (grad_middle + grad_result, grad_gain_two, grad_up, grad_down)


def block_forward(stream, weights, head_count, key_mask):
    gain_one, qkv_weight, out_weight, gain_two, up_weight, down_weight = weights
    normed_one, unit_one, inverse_one = layer_norm(stream, gain_one.astype(jnp.float32))
    normed_low = normed_one.astype(jnp.bfloat16)
    packed = contract(normed_low, qkv_weight).astype(jnp.bfloat16)
    mixed_heads, attn_weights, attn_low = attend(packed, head_count, key_mask)
    middle = stream + contract(mixed_heads, out_weight)
    result, mlp_kept = mlp_forward(middle, gain_two, up_weight, down_weight)
    kept_values = {
        "unit_one": unit_one,
        "inverse_one": inverse_one,
        "normed_low": normed_low,
        "packed": packed,
        "attn_weights": attn_weights,
        "attn_low": attn_low,
        "mixed_heads": mixed_heads,
        "mlp": mlp_kept,
    }
    return (result, kept_values)


def block_backward(grad_result, kept_values, weights, head_count):
    gain_one, qkv_weight, out_weight, gain_two, up_weight, down_weight = weights
    grad_middle, grad_gain_two, grad_up, grad_down = mlp_backward(
        grad_result, kept_values["mlp"], gain_two, up_weight, down_weight
    )
    grad_attend = grad_middle.astype(jnp.bfloat16)
    grad_out = outer_sum(kept_values["mixed_heads"], grad_attend)
    grad_mixed = contract_back(grad_attend, out_weight).astype(jnp.bfloat16)
    grad_packed = attend_back(
        kept_values["packed"],
        kept_values["attn_weights"],
        kept_values["attn_low"],
        grad_mixed,
        head_count,
    )
    grad_qkv = outer_sum(kept_values["normed_low"], grad_packed)
    grad_normed = contract_back(grad_packed, qkv_weight)
    grad_stream, grad_gain_one = layer_norm_back(
        grad_normed,
        kept_values["unit_one"],
        kept_values["inverse_one"],
        gain_one.astype(jnp.float32),
    )
    return (
        grad_stream + grad_middle,
        grad_gain_one,
        grad_qkv,
        grad_out,
        grad_gain_two,
        grad_up,
        grad_down,
    )


def micro_step(
    enc_rows, counts, positions, cot_rows, enc_weights, embed_weight, mask_token, dec_weights
):
    slot_total = enc_rows.shape[1]
    live_slots = jnp.arange(slot_total)[None, :] < counts[:, None]
    encoded, enc_kept = block_forward(enc_rows.astype(jnp.float32), enc_weights, HEADS, live_slots)
    encoded_low = encoded.astype(jnp.bfloat16)
    embedded = contract(encoded_low, embed_weight)
    places = jnp.arange(PATCHES)
    matches = (positions[:, :, None] == places[None, None, :]) & live_slots[:, :, None]
    covered = jnp.any(matches, axis=1)
    slot_index = jnp.sum(jnp.where(matches, jnp.arange(slot_total)[None, :, None], 0), axis=1)
    picked = jnp.take_along_axis(embedded, slot_index[:, :, None], axis=1)
    filled = jnp.where(covered[:, :, None], picked, mask_token.astype(jnp.float32))
    filled = filled + position_table(PATCHES, embedded.shape[-1])
    filled_low = filled.astype(jnp.bfloat16)
    decoded, dec_kept = block_forward(filled_low.astype(jnp.float32), dec_weights, DHEADS, None)
    dec_piece = decoded.astype(jnp.bfloat16)
    dec_back = block_backward(cot_rows.astype(jnp.float32), dec_kept, dec_weights, DHEADS)
    dec_terms = dec_back[1:]
    grad_filled = dec_back[0].astype(jnp.bfloat16).astype(jnp.float32)
    mask_term = jnp.sum(
        jnp.where(covered[:, :, None], 0.0, grad_filled).reshape(-1, grad_filled.shape[-1]), axis=0
    )
    grad_embedded = jnp.take_along_axis(grad_filled, positions[:, :, None], axis=1)
    grad_embedded = jnp.where(live_slots[:, :, None], grad_embedded, 0.0).astype(jnp.bfloat16)
    embed_term = outer_sum(encoded_low, grad_embedded)
    grad_encoded = contract_back(grad_embedded, embed_weight)
    enc_back = block_backward(grad_encoded, enc_kept, enc_weights, HEADS)
    grad_input = enc_back[0]
    enc_terms = enc_back[1:] + (embed_term, mask_term)
    return (dec_piece, grad_input, tuple(enc_terms) + tuple(dec_terms))


def local(
    enc_input,
    keep_count,
    keep_positions,
    enc_gain_one,
    enc_qkv_weight,
    enc_out_weight,
    enc_gain_two,
    enc_up_weight,
    enc_down_weight,
    embed_weight,
    mask_token,
    dec_gain_one,
    dec_qkv_weight,
    dec_out_weight,
    dec_gain_two,
    dec_up_weight,
    dec_down_weight,
    cotangent,
):
    enc_weights = (
        enc_gain_one,
        enc_qkv_weight,
        enc_out_weight,
        enc_gain_two,
        enc_up_weight,
        enc_down_weight,
    )
    dec_weights = (
        dec_gain_one,
        dec_qkv_weight,
        dec_out_weight,
        dec_gain_two,
        dec_up_weight,
        dec_down_weight,
    )
    all_params = (
        enc_gain_one,
        enc_qkv_weight,
        enc_out_weight,
        enc_gain_two,
        enc_up_weight,
        enc_down_weight,
        embed_weight,
        mask_token,
        dec_gain_one,
        dec_qkv_weight,
        dec_out_weight,
        dec_gain_two,
        dec_up_weight,
        dec_down_weight,
    )
    dec_pieces, input_grads, totals = micro_step(
        enc_input, keep_count, keep_positions, cotangent, enc_weights, embed_weight, mask_token, dec_weights
    )
    totals = (
        lax.psum_scatter(totals[0], ("dp", "seq"), scatter_dimension=0, tiled=True),
        lax.psum_scatter(totals[1], ("dp", "seq"), scatter_dimension=0, tiled=True),
        lax.psum_scatter(totals[2], ("dp", "seq"), scatter_dimension=0, tiled=True),
        lax.psum_scatter(totals[3], ("dp", "seq"), scatter_dimension=0, tiled=True),
        lax.psum_scatter(totals[4], ("dp", "seq"), scatter_dimension=0, tiled=True),
        lax.psum_scatter(totals[5], ("dp", "seq"), scatter_dimension=0, tiled=True),
        lax.psum_scatter(totals[6], ("dp", "seq"), scatter_dimension=0, tiled=True),
        lax.psum_scatter(totals[7], ("dp", "seq"), scatter_dimension=0, tiled=True),
        lax.psum_scatter(totals[8], ("dp", "seq"), scatter_dimension=0, tiled=True),
        lax.psum_scatter(totals[9], ("dp", "seq"), scatter_dimension=0, tiled=True),
        lax.psum_scatter(totals[10], ("dp", "seq"), scatter_dimension=0, tiled=True),
        lax.psum_scatter(totals[11], ("dp", "seq"), scatter_dimension=0, tiled=True),
        lax.psum_scatter(totals[12], ("dp", "seq"), scatter_dimension=0, tiled=True),
        lax.psum_scatter(totals[13], ("dp", "seq"), scatter_dimension=0, tiled=True),
    )
    dec_output = dec_pieces.reshape(cotangent.shape)
    enc_input_grad = input_grads.reshape(enc_input.shape)
    return (
        dec_output,
        enc_input_grad,
        totals[0],
        totals[1],
        totals[2],
        totals[3],
        totals[4],
        totals[5],
        totals[6],
        totals[7],
        totals[8],
        totals[9],
        totals[10],
        totals[11],
        totals[12],
        totals[13],
    )


MESH = pl.DeviceIdType.MESH
BF = jnp.bfloat16
F32 = jnp.float32
LANES = 128
TILE = 256
CHUNK = 48
VMEM_BYTES = 62 * 2**20
STEP = 72
FLOWS = ((0, 32, "xyls"), (32, 24, "yxls"), (56, 8, "lsxy"), (64, 8, "lsyx"))
DIMS = "slyx"


def padded(count, multiple):
    return -(-count // multiple) * multiple


def nn(left, right):
    return lax.dot_general(left, right, (((1,), (0,)), ((), ())), preferred_element_type=F32)


def nt(left, right):
    return lax.dot_general(left, right, (((1,), (1,)), ((), ())), preferred_element_type=F32)


def tn(left, right):
    return lax.dot_general(left, right, (((0,), (0,)), ((), ())), preferred_element_type=F32)


def columns(tile):
    return pl.ds(pl.multiple_of(tile * TILE, TILE), TILE)


def each(count, body):
    lax.fori_loop(0, count, lambda index, carry: (body(index), carry)[1], 0)


def gelu_pair(values):
    reach = jnp.abs(values)
    point = 1.0 / (1.0 + 0.23164189 * reach)
    decay = jnp.exp(-0.5 * values * values)
    tail = 0.5307027145 * point - 0.7265760135
    tail = tail * point + 0.710706870
    tail = tail * point - 0.142248368
    tail = tail * point + 0.127414796
    tail = tail * point * decay
    below = jnp.where(values < 0.0, tail, 1.0 - tail)
    return values * below, below + values * decay * 0.3989422804014327


def norm_rows(total, source, gain, normed, inverse):
    width = gain.shape[-1]

    def body(chunk):
        rows = pl.ds(pl.multiple_of(chunk * CHUNK, CHUNK), CHUNK)
        stream = source[rows, :].astype(F32)
        centered = stream - jnp.sum(stream, axis=-1, keepdims=True) * (1.0 / width)
        scale = lax.rsqrt(jnp.sum(centered * centered, axis=-1, keepdims=True) * (1.0 / width) + eps)
        inverse[rows, :] = scale
        normed[rows, :] = (centered * scale * gain).astype(BF)

    each(total // CHUNK, body)


def norm_back(total, grad_normed, normed, inverse, gain, added, emit, partial):
    width = gain.shape[-1]
    over = 1.0 / gain
    partial[...] = jnp.zeros_like(partial)

    def body(chunk):
        rows = pl.ds(pl.multiple_of(chunk * CHUNK, CHUNK), CHUNK)
        grad = grad_normed[rows, :]
        unit = normed[rows, :].astype(F32)
        both = grad * unit
        scaled = grad * gain
        first = jnp.sum(scaled, axis=-1, keepdims=True) * (1.0 / width)
        second = jnp.sum(both, axis=-1, keepdims=True) * (1.0 / width)
        emit(rows, inverse[rows, :] * (scaled - first - unit * over * second) + added[rows, :].astype(F32))
        partial[...] += jnp.sum(both.reshape(CHUNK // 8, 8, width), axis=0)

    each(total // CHUNK, body)
    return jnp.sum(partial[...], axis=0, keepdims=True) * over


def head_masks(size):
    lane = lax.broadcasted_iota(jnp.int32, (1, LANES), 1)
    return [((lane >= h * size) & (lane < (h + 1) * size)).astype(F32) for h in range(LANES // size)]


def split_heads(block, masks):
    return jnp.concatenate([block * mask.astype(BF) for mask in masks], axis=0)


def merge_heads(stacked, masks, rows):
    total = stacked[:rows] * masks[0]
    for h in range(1, len(masks)):
        total = total + stacked[h * rows : (h + 1) * rows] * masks[h]
    return total


def attend_block(packed, width, rows, size, image, group, limit, kept, mixed):
    masks = head_masks(size)
    heads = len(masks)
    at = pl.ds(pl.multiple_of(image * rows, 16), rows)
    queries = packed[at, group * LANES : (group + 1) * LANES]
    keys = packed[at, width + group * LANES : width + (group + 1) * LANES]
    values = packed[at, 2 * width + group * LANES : 2 * width + (group + 1) * LANES]
    scores = (nt(split_heads(keys, masks), queries) * size**-0.5).reshape(heads, rows, rows)
    live = lax.broadcasted_iota(jnp.int32, (1, rows, 1), 1) < limit
    scores = jnp.where(live, scores, -1e30)
    raised = jnp.exp(scores - jnp.max(scores, axis=1, keepdims=True))
    weights = raised * (1.0 / jnp.sum(raised, axis=1, keepdims=True))
    low = weights.reshape(heads * rows, rows).astype(BF)
    kept[image, group] = low
    mixed[at, group * LANES : (group + 1) * LANES] = tn(low, split_heads(values, masks)).astype(BF)


def attend_back_block(packed, width, rows, size, image, group, kept, grad_mixed, grad_packed):
    masks = head_masks(size)
    heads = len(masks)
    at = pl.ds(pl.multiple_of(image * rows, 16), rows)
    queries = packed[at, group * LANES : (group + 1) * LANES]
    keys = packed[at, width + group * LANES : width + (group + 1) * LANES]
    values = packed[at, 2 * width + group * LANES : 2 * width + (group + 1) * LANES]
    grad_out = grad_mixed[at, group * LANES : (group + 1) * LANES]
    low = kept[image, group]
    weights = low.astype(F32)
    both = weights * nt(split_heads(values, masks), grad_out)
    inner = jnp.sum(both.reshape(heads, rows, rows), axis=1, keepdims=True)
    grad_scores = both - (weights.reshape(heads, rows, rows) * inner).reshape(heads * rows, rows)
    grad_scores = grad_scores.astype(BF)
    grad_values = merge_heads(nn(low, grad_out), masks, rows)
    grad_keys = merge_heads(nn(grad_scores, queries), masks, rows) * size**-0.5
    grad_queries = tn(grad_scores, split_heads(keys, masks)) * size**-0.5
    grad_packed[at, group * LANES : (group + 1) * LANES] = grad_queries.astype(BF)
    grad_packed[at, width + group * LANES : width + (group + 1) * LANES] = grad_keys.astype(BF)
    grad_packed[at, 2 * width + group * LANES : 2 * width + (group + 1) * LANES] = grad_values.astype(BF)


def pad_images(source, target, rows):
    images, count = source.shape[0], source.shape[1]
    whole = count // 16 * 16
    for image in range(images):
        target[image * rows + whole : (image + 1) * rows, :] = jnp.zeros((rows - whole, target.shape[1]), target.dtype)
        target[image * rows : image * rows + count, :] = source[image]


def enc_forward_kernel(
    rows, counts, stream, gain_one, qkv, out, gain_two, up, down,
    normed_one, inverse_one, packed, kept, mixed, normed_two, inverse_two, active, slope, encoded,
    padded_in, middle,
):
    images = stream.shape[0]
    total = images * rows
    width = stream.shape[-1]
    pad_images(stream, padded_in, rows)
    norm_rows(total, padded_in, gain_one[...].astype(F32), normed_one, inverse_one)

    def project(tile):
        packed[:, columns(tile)] = nn(normed_one[...], qkv[:, columns(tile)]).astype(BF)

    each(qkv.shape[1] // TILE, project)

    def mix(image):
        for group in range(width // LANES):
            attend_block(packed, width, rows, width // HEADS, image, group, counts[image], kept, mixed)

    each(images, mix)

    def add_out(tile):
        middle[:, columns(tile)] = padded_in[:, columns(tile)].astype(F32) + nn(mixed[...], out[:, columns(tile)])

    each(width // TILE, add_out)
    norm_rows(total, middle, gain_two[...].astype(F32), normed_two, inverse_two)
    feed_up(normed_two, up, active, slope)

    def add_down(tile):
        encoded[:, columns(tile)] = (middle[:, columns(tile)] + nn(active[...], down[:, columns(tile)])).astype(BF)

    each(width // TILE, add_down)


def feed_up(normed, up, active, slope):
    def body(tile):
        value, derivative = gelu_pair(nn(normed[...], up[:, columns(tile)]))
        active[:, columns(tile)] = value.astype(BF)
        slope[:, columns(tile)] = derivative.astype(BF)

    each(up.shape[1] // TILE, body)


def feed_back(grad_low, down, slope, grad_pre):
    def body(tile):
        grad = nt(grad_low[...], down[columns(tile), :]) * slope[:, columns(tile)].astype(F32)
        grad_pre[:, columns(tile)] = grad.astype(BF)

    each(down.shape[0] // TILE, body)


def times_back(grad, matrix, result):
    def body(tile):
        result[:, columns(tile)] = nt(grad[...], matrix[columns(tile), :]).astype(result.dtype)

    each(matrix.shape[0] // TILE, body)


def one_hot(positions, image, limit, slots, places):
    place = lax.broadcasted_iota(jnp.int32, (places, slots), 0)
    slot = lax.broadcasted_iota(jnp.int32, (places, slots), 1)
    return jnp.where((positions[image : image + 1, :slots] == place) & (slot < limit), 1.0, 0.0)


def send_tiles(count, first, rows, gathered, place, sems, tile, slots=2):
    def copy(slot, at):
        return pltpu.make_async_copy(place(slot), gathered.at[:, pl.ds(at, rows), :], sems.at[slot])

    def body(n):
        slot = lax.rem(n, slots)

        @pl.when(n >= slots)
        def _():
            copy(slot, first).wait()

        place(slot)[...] = tile(n).reshape(32, rows, TILE)
        copy(slot, pl.multiple_of(first + n * rows, 8)).start()

    each(count, body)
    for n in range(max(count - slots, 0), count):
        copy(n % slots, first).wait()


def dec_kernel(
    erows, drows, counts, positions, encoded, embed, mask_token, table,
    gain_one, qkv, out, gain_two, up, down, cotangent,
    result, grad_encoded, grad_embedded, vectors, gathered,
    filled, normed_one, inverse_one, packed, kept, mixed, middle, normed_two, inverse_two, active, slope,
    grad_wide, wide, partial, stage_down, stage_up, sem_down, sem_up, sem_embed,
):
    images, places = cotangent.shape[0], cotangent.shape[1]
    total = images * drows
    width = cotangent.shape[-1]
    high, rest = mixed, grad_wide
    embedded_rows = images * erows

    def embed_tile(tile):
        value = nn(encoded[...], embed[:, columns(tile)])
        top = value.astype(BF)
        high[pl.ds(0, embedded_rows), columns(tile)] = top
        rest[pl.ds(0, embedded_rows), columns(tile)] = (value - top.astype(F32)).astype(BF)

    each(width // TILE, embed_tile)
    row = lax.broadcasted_iota(jnp.int32, (drows, 1), 0)
    for image in range(images):
        pick = one_hot(positions, image, counts[image], erows, drows)
        low_pick = pick.astype(BF)
        slots = pl.ds(image * erows, erows)
        picked = nn(low_pick, high[slots, :]) + nn(low_pick, rest[slots, :])
        covered = jnp.sum(pick, axis=1, keepdims=True) > 0.5
        value = jnp.where(covered, picked, mask_token[...].astype(F32)) + table[...]
        filled[pl.ds(image * drows, drows), :] = jnp.where(row < places, value, 0.0).astype(BF)

    norm_rows(total, filled, gain_one[...].astype(F32), normed_one, inverse_one)

    def project(tile):
        packed[:, columns(tile)] = nn(normed_one[...], qkv[:, columns(tile)]).astype(BF)

    each(qkv.shape[1] // TILE, project)

    def mix(image):
        for group in range(width // LANES):
            attend_block(packed, width, drows, width // DHEADS, image, group, places, kept, mixed)

    each(images, mix)

    def add_out(tile):
        middle[:, columns(tile)] = filled[:, columns(tile)].astype(F32) + nn(mixed[...], out[:, columns(tile)])

    each(width // TILE, add_out)
    norm_rows(total, middle, gain_two[...].astype(F32), normed_two, inverse_two)
    feed_up(normed_two, up, active, slope)

    for tile in range(width // TILE):
        at = slice(tile * TILE, (tile + 1) * TILE)
        value = (middle[:, at] + nn(active[...], down[:, at])).astype(BF)
        for image in range(images):
            result[image, :, at] = value[image * drows : image * drows + places]

    grad_low = grad_wide
    pad_images(cotangent, grad_low, drows)
    at = 0
    block = down.shape[0] // 32
    send_tiles(width // TILE, at, block, gathered, lambda slot: stage_down, sem_down, lambda n: tn(active[...], grad_low[:, columns(n)]), 1)
    at += width // TILE * block
    block = width // 32
    feed_back(grad_low, down, slope, slope)
    send_tiles(up.shape[1] // TILE, at, block, gathered, lambda slot: stage_up.at[slot], sem_up, lambda n: tn(normed_two[...], slope[:, columns(n)]))
    at += up.shape[1] // TILE * block
    times_back(slope, up, middle)
    grad_attend = grad_wide

    def keep_middle(rows, grad):
        middle[rows, :] = grad
        grad_attend[rows, :] = grad.astype(BF)

    vectors[...] = jnp.zeros_like(vectors)
    vectors[1:2, :] = norm_back(total, middle, normed_two, inverse_two, gain_two[...].astype(F32), grad_low, keep_middle, partial)
    send_tiles(width // TILE, at, block, gathered, lambda slot: stage_up.at[slot], sem_up, lambda n: tn(mixed[...], grad_attend[:, columns(n)]))
    at += width // TILE * block
    grad_mixed = normed_two
    times_back(grad_attend, out, grad_mixed)

    def mix_back(image):
        for group in range(width // LANES):
            attend_back_block(packed, width, drows, width // DHEADS, image, group, kept, grad_mixed, packed)

    each(images, mix_back)
    send_tiles(qkv.shape[1] // TILE, at, block, gathered, lambda slot: stage_up.at[slot], sem_up, lambda n: tn(normed_one[...], packed[:, columns(n)]))
    at += qkv.shape[1] // TILE * block
    times_back(packed, qkv, wide)

    def keep_filled(rows, grad):
        filled[rows, :] = grad.astype(BF)

    vectors[0:1, :] = norm_back(total, wide, normed_one, inverse_one, gain_one[...].astype(F32), middle, keep_filled, partial)
    token = jnp.zeros((1, width), F32)
    for image in range(images):
        pick = one_hot(positions, image, counts[image], erows, drows)
        covered = jnp.sum(pick, axis=1, keepdims=True) > 0.5
        grad = filled[pl.ds(image * drows, drows), :]
        token = token + jnp.sum(jnp.where(covered | (row >= places), 0.0, grad.astype(F32)), axis=0, keepdims=True)
        grad_embedded[pl.ds(image * erows, erows), :] = tn(pick.astype(BF), grad).astype(BF)
    vectors[2:3, :] = token
    block = embed.shape[0] // 32

    def embed_place(slot):
        return stage_down.at[:, pl.ds(pl.multiple_of(slot * block, 8), block), :]

    send_tiles(width // TILE, at, block, gathered, embed_place, sem_embed, lambda n: tn(encoded[...], grad_embedded[:, columns(n)]))
    times_back(grad_embedded, embed, grad_encoded)


def coords():
    seq, dp = lax.axis_index("seq"), lax.axis_index("dp")
    return {"s": dp // 4, "l": (dp // 2) % 2, "y": dp % 2, "x": seq // 2, "c": seq % 2}


def partner(here, dim):
    other = dict(here)
    other[dim] = 1 - here[dim]
    return (other["s"] * 4 + other["l"] * 2 + other["y"], other["x"] * 2 + other["c"])


class Reduction:
    def __init__(self, steps, result, scratch):
        self.steps, self.result = steps, result
        self.stage, self.land = scratch[0], scratch[1]
        self.lands = [scratch[2 + 4 * f : 6 + 4 * f] for f in range(4)]
        self.send_sem, self.recv_sem = scratch[18:20]
        self.here = coords()

    @staticmethod
    def scratch(steps):
        shapes = [pltpu.VMEM((2, 2, 2, 2, 2, 2, STEP, TILE), F32), pltpu.VMEM((steps, 2, 2, 2, 2, STEP, TILE), F32)]
        for _, rows, _ in FLOWS:
            for k in range(1, 5):
                shapes.append(pltpu.VMEM((steps,) + (2,) * (4 - k) + (rows, TILE), F32))
        return shapes + [pltpu.SemaphoreType.DMA((steps, 17)), pltpu.SemaphoreType.DMA((steps, 17))]

    def enter(self):
        barrier = pltpu.get_barrier_semaphore()
        for dim in "c" + DIMS:
            pl.semaphore_signal(barrier, inc=1, device_id=partner(self.here, dim), device_id_type=MESH)
        pl.semaphore_wait(barrier, 5)

    def core_copy(self, t):
        return pltpu.make_async_remote_copy(
            src_ref=self.stage.at[lax.rem(t, 2), :, :, :, :, 1 - self.here["c"]],
            dst_ref=self.land.at[t],
            send_sem=self.send_sem.at[t, 16],
            recv_sem=self.recv_sem.at[t, 16],
            device_id=partner(self.here, "c"),
            device_id_type=MESH,
        )

    def half(self, t, flow, k, kept):
        first, rows, order = FLOWS[flow]
        left = [dim for dim in DIMS if dim not in order[:k]]
        side = self.here[order[k]] if kept else 1 - self.here[order[k]]
        at = (t,) + tuple(side if dim == order[k] else slice(None) for dim in left)
        if k == 0:
            return self.land.at[at + (pl.ds(first, rows),)]
        return self.lands[flow][k - 1].at[at]

    def copy(self, t, flow, k):
        return pltpu.make_async_remote_copy(
            src_ref=self.half(t, flow, k, False),
            dst_ref=self.lands[flow][k].at[t],
            send_sem=self.send_sem.at[t, flow * 4 + k],
            recv_sem=self.recv_sem.at[t, flow * 4 + k],
            device_id=partner(self.here, FLOWS[flow][2][k]),
            device_id_type=MESH,
        )

    def advance(self, k, t):
        if k == 1:
            self.core_copy(t).wait()
            self.land[t] += self.stage[lax.rem(t, 2), :, :, :, :, self.here["c"]]
            for flow in range(4):
                self.copy(t, flow, 0).start()
            return
        for flow in range(4):
            self.copy(t, flow, k - 2).wait()
            kept = self.half(t, flow, k - 2, True)
            if k < 5:
                self.lands[flow][k - 2][t] += kept[...]
                self.copy(t, flow, k - 1).start()
            else:
                first, rows, _ = FLOWS[flow]
                at = pl.ds(pl.multiple_of(t * STEP + first, 8), rows)
                self.result[at, :] = self.lands[flow][3][t] + kept[...]

    def step(self, t, fill=None):
        if fill is not None:
            fill(t)
            self.core_copy(t).start()
        for k in range(1, 6):
            @pl.when((t >= k) & (t < self.steps + k))
            def _():
                self.advance(k, t - k)


def staged_load(reduction, gathered, sems):
    def load(t):
        rows = pl.ds(pl.multiple_of(t * STEP, 8), STEP)
        return pltpu.make_async_copy(gathered.at[:, :, :, :, :, rows, :], reduction.stage.at[lax.rem(t, 2)], sems.at[lax.rem(t, 2)])

    return load


def enc_back_kernel(
    rows, steps,
    grad_encoded, active, slope, normed_two, inverse_two, gain_two, packed, kept, normed_one, inverse_one, gain_one,
    qkv, out, up, down, gathered,
    grad_low, grad_pre, grad_attend, grad_packed, input_grad, vectors, gathered_down, reduced,
    middle, wide, grad_mixed, partial, stage_down, weight, sem_down, sem_in, sem_load, *scratch,
):
    images, slots = input_grad.shape[0], input_grad.shape[1]
    total = images * rows
    width = middle.shape[-1]
    reduction = Reduction(steps, reduced, scratch)
    load = staged_load(reduction, gathered, sem_load)
    into_pre = pltpu.make_async_copy(slope, grad_pre, sem_in.at[0])
    into_packed = pltpu.make_async_copy(packed, grad_packed, sem_in.at[1])
    into_wide = pltpu.make_async_copy(grad_encoded, wide, sem_in.at[2])
    into_up = pltpu.make_async_copy(up, weight, sem_in.at[3])
    into_qkv = pltpu.make_async_copy(qkv, weight.at[:, : qkv.shape[1]], sem_in.at[4])
    into_wide.start()
    into_pre.start()
    load(0).start()
    into_packed.start()
    into_up.start()
    reduction.enter()

    def communicate(t):
        load(t).wait()
        reduction.step(t, lambda _: None)

        @pl.when(t + 1 < steps)
        def _():
            load(t + 1).start()

    def low_chunk(chunk):
        at = pl.ds(pl.multiple_of(chunk * CHUNK, CHUNK), CHUNK)
        grad_low[at, :] = wide[at, :].astype(BF)

    into_wide.wait()
    each(total // CHUNK, low_chunk)
    into_pre.wait()
    block = down.shape[0] // 32

    def down_tile(n):
        return tn(active[...], grad_low[:, columns(n)])

    def copy_down(n):
        return pltpu.make_async_copy(stage_down.at[0], gathered_down.at[:, pl.ds(pl.multiple_of(n * block, 8), block), :], sem_down.at[0])

    def send_down(n):
        @pl.when(n > 0)
        def _():
            copy_down(n - 1).wait()

        stage_down[0] = down_tile(n).reshape(stage_down.shape[1:])
        copy_down(n).start()
        communicate(n)

    each(width // TILE, send_down)
    copy_down(width // TILE - 1).wait()
    feed_back(grad_low, down, grad_pre, grad_pre)
    into_up.wait()
    times_back(grad_pre, weight, middle)
    into_qkv.start()

    def keep_middle(at, grad):
        middle[at, :] = grad
        grad_attend[at, :] = grad.astype(BF)

    vectors[...] = jnp.zeros_like(vectors)
    vectors[1:2, :] = norm_back(total, middle, normed_two, inverse_two, gain_two[...].astype(F32), wide, keep_middle, partial)
    times_back(grad_attend, out, grad_mixed)
    into_packed.wait()
    first = width // TILE

    def mix_back(image):
        for group in range(width // LANES):
            attend_back_block(grad_packed, width, rows, width // HEADS, image, group, kept, grad_mixed, grad_packed)

        @pl.when(first + image < steps)
        def _():
            communicate(first + image)

    each(images, mix_back)
    into_qkv.wait()
    times_back(grad_packed, weight.at[:, : qkv.shape[1]], wide)

    def keep_input(at, grad):
        wide[at, :] = grad

    vectors[0:1, :] = norm_back(total, wide, normed_one, inverse_one, gain_one[...].astype(F32), middle, keep_input, partial)
    for image in range(images):
        input_grad[image] = wide[image * rows : image * rows + slots, :]
    each(5, lambda k: reduction.step(steps + k))


def enc_weights_kernel(
    steps,
    normed_two, grad_pre, mixed, grad_attend, normed_one, grad_packed, gathered_down, vector,
    reduced, vector_sum,
    vector_part, vector_land, vector_send, vector_recv, sem_load, *scratch,
):
    reduction = Reduction(steps, reduced, scratch)
    load = staged_load(reduction, gathered_down, sem_load)
    ready = gathered_down.shape[-2] // STEP
    load(0).start()
    reduction.enter()
    order = "c" + DIMS

    def vector_copy(k):
        return pltpu.make_async_remote_copy(
            src_ref=vector_part.at[k],
            dst_ref=vector_land.at[k],
            send_sem=vector_send.at[k],
            recv_sem=vector_recv.at[k],
            device_id=partner(reduction.here, order[k]),
            device_id_type=MESH,
        )

    def vector_step(t):
        for k in range(6):
            @pl.when(t == k)
            def _():
                if k == 0:
                    vector_part[0] = vector[...]
                else:
                    vector_copy(k - 1).wait()
                    vector_part[k] = vector_part[k - 1] + vector_land[k - 1]
                if k < 5:
                    vector_copy(k).start()

    def from_memory(t):
        load(t).wait()
        reduction.step(t, lambda _: None)
        vector_step(t)

        @pl.when(t + 1 < ready)
        def _():
            load(t + 1).start()

    each(ready, from_memory)

    def from_product(first, left, right):
        block = left.shape[1] // 32
        count = STEP // block

        def fill(t):
            for i in range(count):
                tile = tn(left[...], right[:, columns((t - first) * count + i)])
                reduction.stage[lax.rem(t, 2), :, :, :, :, :, i * block : (i + 1) * block, :] = tile.reshape(2, 2, 2, 2, 2, block, TILE)

        def body(s):
            reduction.step(first + s, fill)
            vector_step(first + s)

        number = right.shape[1] // TILE // count
        each(number, body)
        return first + number

    at = from_product(ready, normed_two, grad_pre)
    at = from_product(at, normed_one, grad_packed)
    at = from_product(at, mixed, grad_attend)
    each(5, lambda k: reduction.step(steps + k))
    here = reduction.here
    index = (here["s"] * 4 + here["l"] * 2 + here["y"]) * 4 + here["x"] * 2 + here["c"]
    vector_sum[...] = vector_part[5, pl.ds(index, 1), :]


def unpack_kernel(layout, *refs):
    sources, targets = refs[:2], refs[2:]
    at = [0, 0]
    for (which, _), target in zip(layout, targets):
        block, width = target.shape
        for n in range(width // TILE):
            target[:, n * TILE : (n + 1) * TILE] = sources[which][at[which] : at[which] + block, :]
            at[which] += block


def vmem(count):
    return [pl.BlockSpec(memory_space=pltpu.VMEM)] * count


def anywhere(count):
    return [pl.BlockSpec(memory_space=pl.ANY)] * count


def shapes(*pairs):
    return [jax.ShapeDtypeStruct(shape, dtype) for shape, dtype in pairs]


def scratches(*pairs):
    return [pltpu.VMEM(shape, dtype) for shape, dtype in pairs]


def cost(flops, bytes_accessed):
    return pl.CostEstimate(flops=flops, bytes_accessed=bytes_accessed, transcendentals=0)


def fast_local(
    enc_input, keep_count, keep_positions,
    enc_gain_one, enc_qkv_weight, enc_out_weight, enc_gain_two, enc_up_weight, enc_down_weight,
    embed_weight, mask_token,
    dec_gain_one, dec_qkv_weight, dec_out_weight, dec_gain_two, dec_up_weight, dec_down_weight,
    cotangent,
):
    images, slots, width = enc_input.shape
    places, dwidth = cotangent.shape[1:]
    hidden, dhidden = enc_up_weight.shape[1], dec_up_weight.shape[1]
    erows, drows = padded(slots, 16), padded(places, 16)
    etotal, dtotal = images * erows, images * drows
    egroups, dgroups = width // LANES, dwidth // LANES
    eheads, dheads = HEADS // egroups, DHEADS // dgroups
    smem = [pl.BlockSpec(memory_space=pltpu.SMEM)]
    settings = functools.partial(pltpu.CompilerParams, vmem_limit_bytes=VMEM_BYTES)
    row = lambda vector: vector.reshape(1, -1)

    normed_one, inverse_one, packed, kept, mixed, normed_two, inverse_two, active, slope, encoded = pl.pallas_call(
        functools.partial(enc_forward_kernel, erows),
        name="enc_forward",
        out_shape=shapes(
            ((etotal, width), BF), ((etotal, 1), F32), ((etotal, 3 * width), BF), ((images, egroups, eheads * erows, erows), BF),
            ((etotal, width), BF), ((etotal, width), BF), ((etotal, 1), F32), ((etotal, hidden), BF), ((etotal, hidden), BF), ((etotal, width), BF),
        ),
        in_specs=smem + vmem(7),
        out_specs=vmem(10),
        scratch_shapes=scratches(((etotal, width), BF), ((etotal, width), F32)),
        compiler_params=settings(),
    )(keep_count, enc_input, row(enc_gain_one), enc_qkv_weight, enc_out_weight, row(enc_gain_two), enc_up_weight, enc_down_weight)

    table = jnp.asarray(position_rows(places, dwidth, drows))
    block_down, block, block_embed = dhidden // 32, dwidth // 32, width // 32
    dec_rows = dwidth // TILE * (block_down + block + block_embed) + (dhidden + 3 * dwidth) // TILE * block
    dec_output, grad_encoded, grad_embedded, dec_vectors, gathered = pl.pallas_call(
        functools.partial(dec_kernel, erows, drows),
        name="decoder",
        out_shape=shapes(
            (cotangent.shape, BF), ((etotal, width), F32), ((etotal, dwidth), BF), ((8, dwidth), F32), ((32, dec_rows, TILE), F32),
        ),
        in_specs=smem + vmem(12),
        out_specs=vmem(4) + anywhere(1),
        scratch_shapes=scratches(
            ((dtotal, dwidth), BF), ((dtotal, dwidth), BF), ((dtotal, 1), F32), ((dtotal, 3 * dwidth), BF),
            ((images, dgroups, dheads * drows, drows), BF), ((dtotal, dwidth), BF), ((dtotal, dwidth), F32), ((dtotal, dwidth), BF),
            ((dtotal, 1), F32), ((dtotal, dhidden), BF), ((dtotal, dhidden), BF), ((dtotal, dwidth), BF), ((dtotal, dwidth), F32),
            ((8, dwidth), F32), ((32, block_down, TILE), F32), ((2, 32, block, TILE), F32),
        ) + [pltpu.SemaphoreType.DMA((2,))] * 3,
        compiler_params=settings(),
    )(
        keep_count, jnp.pad(keep_positions, ((0, 0), (0, erows - slots))), encoded, embed_weight, row(mask_token), table,
        row(dec_gain_one), dec_qkv_weight, dec_out_weight, row(dec_gain_two), dec_up_weight, dec_down_weight, cotangent,
    )

    dec_steps = dec_rows // STEP
    down_rows = width // TILE * (hidden // 32)
    grad_low, grad_pre, grad_attend, grad_packed, input_grad, enc_vectors, gathered_down, dec_reduced = pl.pallas_call(
        functools.partial(enc_back_kernel, erows, dec_steps),
        name="enc_back",
        out_shape=shapes(
            ((etotal, width), BF), ((etotal, hidden), BF), ((etotal, width), BF), ((etotal, 3 * width), BF),
            (enc_input.shape, F32), ((8, width), F32), ((32, down_rows, TILE), F32), ((dec_rows, TILE), F32),
        ),
        in_specs=anywhere(1) + vmem(1) + anywhere(1) + vmem(3) + anywhere(1) + vmem(4) + anywhere(1) + vmem(1) + anywhere(1) + vmem(1) + anywhere(1),
        out_specs=vmem(6) + anywhere(1) + vmem(1),
        scratch_shapes=scratches(
            ((etotal, width), F32), ((etotal, width), F32), ((etotal, width), BF), ((8, width), F32), ((1, 32, hidden // 32, TILE), F32), (enc_up_weight.shape, BF),
        ) + [pltpu.SemaphoreType.DMA((1,)), pltpu.SemaphoreType.DMA((5,)), pltpu.SemaphoreType.DMA((2,))] + Reduction.scratch(dec_steps),
        compiler_params=settings(collective_id=0, has_side_effects=True),
    )(
        grad_encoded, active, slope, normed_two, inverse_two, row(enc_gain_two), packed, kept, normed_one, inverse_one, row(enc_gain_one),
        enc_qkv_weight, enc_out_weight, enc_up_weight, enc_down_weight, gathered.reshape(2, 2, 2, 2, 2, dec_rows, TILE),
    )

    share = lambda vector: vector.reshape(32, -1)
    vector = jnp.concatenate(
        [share(enc_vectors[0]), share(enc_vectors[1]), share(dec_vectors[2]), share(dec_vectors[0]), share(dec_vectors[1])], axis=1
    )
    vector = jnp.pad(vector, ((0, 0), (0, LANES - vector.shape[1])))
    enc_rows = down_rows + (hidden + 4 * width) // TILE * block_embed
    enc_steps = enc_rows // STEP
    enc_reduced, vector_sum = pl.pallas_call(
        functools.partial(enc_weights_kernel, enc_steps),
        name="enc_weights",
        out_shape=shapes(((enc_rows, TILE), F32), ((1, LANES), F32)),
        in_specs=vmem(6) + anywhere(1) + vmem(1),
        out_specs=vmem(2),
        scratch_shapes=scratches(((6, 32, LANES), F32), ((5, 32, LANES), F32))
        + [pltpu.SemaphoreType.DMA((5,)), pltpu.SemaphoreType.DMA((5,)), pltpu.SemaphoreType.DMA((2,))]
        + Reduction.scratch(enc_steps),
        compiler_params=settings(collective_id=1, has_side_effects=True),
    )(normed_two, grad_pre, mixed, grad_attend, normed_one, grad_packed, gathered_down.reshape(2, 2, 2, 2, 2, down_rows, TILE), vector)

    layout = (
        (0, (block_down, dwidth)), (0, (block, dhidden)), (0, (block, dwidth)), (0, (block, 3 * dwidth)), (0, (block_embed, dwidth)),
        (1, (hidden // 32, width)), (1, (block_embed, hidden)), (1, (block_embed, 3 * width)), (1, (block_embed, width)),
    )
    dec_down, dec_up, dec_out, dec_qkv, embed, enc_down, enc_up, enc_qkv, enc_out = pl.pallas_call(
        functools.partial(unpack_kernel, layout),
        name="unpack",
        out_shape=shapes(*((shape, F32) for _, shape in layout)),
        in_specs=vmem(2),
        out_specs=vmem(9),
    )(dec_reduced, enc_reduced)
    cuts = []
    at = 0
    for size in (width // 32, width // 32, dwidth // 32, dwidth // 32, dwidth // 32):
        cuts.append(vector_sum[0, at : at + size])
        at += size
    return (
        dec_output, input_grad, cuts[0], enc_qkv, enc_out, cuts[1], enc_up, enc_down, embed, cuts[2],
        cuts[3], dec_qkv, dec_out, cuts[4], dec_up, dec_down,
    )


def position_rows(places, width, rows):
    side = math.isqrt(places)
    quarter = width // 4
    place = np.arange(places)
    rate = 1.0 / 10000.0 ** (np.arange(quarter) / quarter)
    across, down = place[:, None] % side * rate, place[:, None] // side * rate
    table = np.concatenate([np.sin(across), np.cos(across), np.sin(down), np.cos(down)], axis=1)
    return np.pad(table, ((0, rows - places), (0, 0))).astype(np.float32)


def solution(mesh):
    placed = (
        P(("dp", "seq"), None, None),
        P(("dp", "seq")),
        P(("dp", "seq"), None),
        P(),
        P(),
        P(),
        P(),
        P(),
        P(),
        P(),
        P(),
        P(),
        P(),
        P(),
        P(),
        P(),
        P(),
        P(("dp", "seq"), None, None),
    )
    fast = (mesh.shape["dp"], mesh.shape["seq"]) == (8, 4)
    return jax.shard_map(
        fast_local if fast else local,
        mesh=mesh,
        in_specs=placed,
        out_specs=(
            P(("dp", "seq"), None, None),
            P(("dp", "seq"), None, None),
            P(("dp", "seq")),
            P(("dp", "seq"), None),
            P(("dp", "seq"), None),
            P(("dp", "seq")),
            P(("dp", "seq"), None),
            P(("dp", "seq"), None),
            P(("dp", "seq"), None),
            P(("dp", "seq")),
            P(("dp", "seq")),
            P(("dp", "seq"), None),
            P(("dp", "seq"), None),
            P(("dp", "seq")),
            P(("dp", "seq"), None),
            P(("dp", "seq"), None),
        ),
        check_vma=False,
    )
```

```python
import functools
import math

import jax
import jax.numpy as jnp
import numpy as np
from jax import lax
from jax.experimental import pallas as pl
from jax.experimental.pallas import tpu as pltpu
from jax.sharding import PartitionSpec as P

HEADS = 12
DHEADS = 16
PATCHES = 196


eps = 1e-06


def position_table(count, model_width):
    grid_side = math.isqrt(count)
    quarter = model_width // 4
    places = jnp.arange(count)
    across = (places % grid_side).astype(jnp.float32)
    row_place = (places // grid_side).astype(jnp.float32)
    frequency = 1.0 / 10000.0 ** (jnp.arange(quarter).astype(jnp.float32) / quarter)
    return jnp.concatenate(
        [
            jnp.sin(across[:, None] * frequency),
            jnp.cos(across[:, None] * frequency),
            jnp.sin(row_place[:, None] * frequency),
            jnp.cos(row_place[:, None] * frequency),
        ],
        axis=1,
    )


def contract(operand, matrix):
    return jnp.einsum("...i,ij->...j", operand, matrix, preferred_element_type=jnp.float32)


def contract_back(gradient, matrix):
    return jnp.einsum("...j,ij->...i", gradient, matrix, preferred_element_type=jnp.float32)


def outer_sum(operand, gradient):
    flat_left = operand.reshape(-1, operand.shape[-1])
    flat_right = gradient.reshape(-1, gradient.shape[-1])
    return lax.dot_general(
        flat_left, flat_right, (((0,), (0,)), ((), ())), preferred_element_type=jnp.float32
    )


def exact_gelu(values):
    return jax.nn.gelu(values, approximate=False)


def gelu_back(pre_act, grad_active):
    unused, pullback = jax.vjp(exact_gelu, pre_act)
    return pullback(grad_active)[0]


def layer_norm(stream, gain_vec):
    row_mean = jnp.mean(stream, axis=-1, keepdims=True)
    centered = stream - row_mean
    inverse = lax.rsqrt(jnp.mean(centered * centered, axis=-1, keepdims=True) + eps)
    unit_rows = centered * inverse
    return (unit_rows * gain_vec, unit_rows, inverse)


def layer_norm_back(grad_normed, unit_rows, inverse, gain_vec):
    grad_gain = jnp.sum((grad_normed * unit_rows).reshape(-1, unit_rows.shape[-1]), axis=0)
    grad_unit = grad_normed * gain_vec
    grad_stream = inverse * (
        grad_unit
        - jnp.mean(grad_unit, axis=-1, keepdims=True)
        - unit_rows * jnp.mean(grad_unit * unit_rows, axis=-1, keepdims=True)
    )
    return (grad_stream, grad_gain)


def attend(packed, head_count, key_mask):
    batch_size, row_count, triple_width = packed.shape
    model_width = triple_width // 3
    head_size = model_width // head_count
    queries = packed[:, :, :model_width].reshape(batch_size, row_count, head_count, head_size)
    key_heads = packed[:, :, model_width : 2 * model_width].reshape(
        batch_size, row_count, head_count, head_size
    )
    value_heads = packed[:, :, 2 * model_width :].reshape(
        batch_size, row_count, head_count, head_size
    )
    scores = jnp.einsum(
        "bqhd,bkhd->bhqk", queries, key_heads, preferred_element_type=jnp.float32
    ) * head_size ** (-0.5)
    if key_mask is not None:
        scores = jnp.where(key_mask[:, None, None, :], scores, -1e30)
    row_max = jnp.max(scores, axis=-1, keepdims=True)
    raised = jnp.exp(scores - row_max)
    attn_weights = raised / jnp.sum(raised, axis=-1, keepdims=True)
    attn_low = attn_weights.astype(jnp.bfloat16)
    mixed_heads = jnp.einsum(
        "bhqk,bkhd->bqhd", attn_low, value_heads, preferred_element_type=jnp.float32
    )
    mixed_heads = mixed_heads.reshape(batch_size, row_count, model_width).astype(jnp.bfloat16)
    return (mixed_heads, attn_weights, attn_low)


def attend_back(packed, attn_weights, attn_low, grad_mixed, head_count):
    batch_size, row_count, triple_width = packed.shape
    model_width = triple_width // 3
    head_size = model_width // head_count
    factor = head_size ** (-0.5)
    queries = packed[:, :, :model_width].reshape(batch_size, row_count, head_count, head_size)
    key_heads = packed[:, :, model_width : 2 * model_width].reshape(
        batch_size, row_count, head_count, head_size
    )
    value_heads = packed[:, :, 2 * model_width :].reshape(
        batch_size, row_count, head_count, head_size
    )
    grad_heads = grad_mixed.reshape(batch_size, row_count, head_count, head_size)
    grad_values = jnp.einsum(
        "bhqk,bqhd->bkhd", attn_low, grad_heads, preferred_element_type=jnp.float32
    )
    grad_attn = jnp.einsum(
        "bqhd,bkhd->bhqk", grad_heads, value_heads, preferred_element_type=jnp.float32
    )
    grad_scores = attn_weights * (
        grad_attn - jnp.sum(attn_weights * grad_attn, axis=-1, keepdims=True)
    )
    grad_scores = grad_scores.astype(jnp.bfloat16)
    grad_queries = (
        jnp.einsum("bhqk,bkhd->bqhd", grad_scores, key_heads, preferred_element_type=jnp.float32)
        * factor
    )
    grad_keys = (
        jnp.einsum("bhqk,bqhd->bkhd", grad_scores, queries, preferred_element_type=jnp.float32)
        * factor
    )
    grad_packed = jnp.concatenate(
        [
            grad_queries.reshape(batch_size, row_count, model_width),
            grad_keys.reshape(batch_size, row_count, model_width),
            grad_values.reshape(batch_size, row_count, model_width),
        ],
        axis=-1,
    )
    return grad_packed.astype(jnp.bfloat16)


def mlp_forward(middle, gain_two, up_weight, down_weight):
    normed_two, unit_two, inverse_two = layer_norm(middle, gain_two.astype(jnp.float32))
    second_low = normed_two.astype(jnp.bfloat16)
    pre_act = contract(second_low, up_weight)
    active_low = exact_gelu(pre_act).astype(jnp.bfloat16)
    result = middle + contract(active_low, down_weight)
    return (
        result,
        {
            "unit_two": unit_two,
            "inverse_two": inverse_two,
            "second_low": second_low,
            "pre_act": pre_act,
            "active_low": active_low,
        },
    )


def mlp_backward(grad_result, kept_values, gain_two, up_weight, down_weight):
    grad_branch = grad_result.astype(jnp.bfloat16)
    grad_down = outer_sum(kept_values["active_low"], grad_branch)
    grad_active = contract_back(grad_branch, down_weight)
    grad_pre = gelu_back(kept_values["pre_act"], grad_active).astype(jnp.bfloat16)
    grad_up = outer_sum(kept_values["second_low"], grad_pre)
    grad_second = contract_back(grad_pre, up_weight)
    grad_middle, grad_gain_two = layer_norm_back(
        grad_second,
        kept_values["unit_two"],
        kept_values["inverse_two"],
        gain_two.astype(jnp.float32),
    )
    return (grad_middle + grad_result, grad_gain_two, grad_up, grad_down)


def block_forward(stream, weights, head_count, key_mask):
    gain_one, qkv_weight, out_weight, gain_two, up_weight, down_weight = weights
    normed_one, unit_one, inverse_one = layer_norm(stream, gain_one.astype(jnp.float32))
    normed_low = normed_one.astype(jnp.bfloat16)
    packed = contract(normed_low, qkv_weight).astype(jnp.bfloat16)
    mixed_heads, attn_weights, attn_low = attend(packed, head_count, key_mask)
    middle = stream + contract(mixed_heads, out_weight)
    result, mlp_kept = mlp_forward(middle, gain_two, up_weight, down_weight)
    kept_values = {
        "unit_one": unit_one,
        "inverse_one": inverse_one,
        "normed_low": normed_low,
        "packed": packed,
        "attn_weights": attn_weights,
        "attn_low": attn_low,
        "mixed_heads": mixed_heads,
        "mlp": mlp_kept,
    }
    return (result, kept_values)


def block_backward(grad_result, kept_values, weights, head_count):
    gain_one, qkv_weight, out_weight, gain_two, up_weight, down_weight = weights
    grad_middle, grad_gain_two, grad_up, grad_down = mlp_backward(
        grad_result, kept_values["mlp"], gain_two, up_weight, down_weight
    )
    grad_attend = grad_middle.astype(jnp.bfloat16)
    grad_out = outer_sum(kept_values["mixed_heads"], grad_attend)
    grad_mixed = contract_back(grad_attend, out_weight).astype(jnp.bfloat16)
    grad_packed = attend_back(
        kept_values["packed"],
        kept_values["attn_weights"],
        kept_values["attn_low"],
        grad_mixed,
        head_count,
    )
    grad_qkv = outer_sum(kept_values["normed_low"], grad_packed)
    grad_normed = contract_back(grad_packed, qkv_weight)
    grad_stream, grad_gain_one = layer_norm_back(
        grad_normed,
        kept_values["unit_one"],
        kept_values["inverse_one"],
        gain_one.astype(jnp.float32),
    )
    return (
        grad_stream + grad_middle,
        grad_gain_one,
        grad_qkv,
        grad_out,
        grad_gain_two,
        grad_up,
        grad_down,
    )


def micro_step(
    enc_rows, counts, positions, cot_rows, enc_weights, embed_weight, mask_token, dec_weights
):
    slot_total = enc_rows.shape[1]
    live_slots = jnp.arange(slot_total)[None, :] < counts[:, None]
    encoded, enc_kept = block_forward(enc_rows.astype(jnp.float32), enc_weights, HEADS, live_slots)
    encoded_low = encoded.astype(jnp.bfloat16)
    embedded = contract(encoded_low, embed_weight)
    places = jnp.arange(PATCHES)
    matches = (positions[:, :, None] == places[None, None, :]) & live_slots[:, :, None]
    covered = jnp.any(matches, axis=1)
    slot_index = jnp.sum(jnp.where(matches, jnp.arange(slot_total)[None, :, None], 0), axis=1)
    picked = jnp.take_along_axis(embedded, slot_index[:, :, None], axis=1)
    filled = jnp.where(covered[:, :, None], picked, mask_token.astype(jnp.float32))
    filled = filled + position_table(PATCHES, embedded.shape[-1])
    filled_low = filled.astype(jnp.bfloat16)
    decoded, dec_kept = block_forward(filled_low.astype(jnp.float32), dec_weights, DHEADS, None)
    dec_piece = decoded.astype(jnp.bfloat16)
    dec_back = block_backward(cot_rows.astype(jnp.float32), dec_kept, dec_weights, DHEADS)
    dec_terms = dec_back[1:]
    grad_filled = dec_back[0].astype(jnp.bfloat16).astype(jnp.float32)
    mask_term = jnp.sum(
        jnp.where(covered[:, :, None], 0.0, grad_filled).reshape(-1, grad_filled.shape[-1]), axis=0
    )
    grad_embedded = jnp.take_along_axis(grad_filled, positions[:, :, None], axis=1)
    grad_embedded = jnp.where(live_slots[:, :, None], grad_embedded, 0.0).astype(jnp.bfloat16)
    embed_term = outer_sum(encoded_low, grad_embedded)
    grad_encoded = contract_back(grad_embedded, embed_weight)
    enc_back = block_backward(grad_encoded, enc_kept, enc_weights, HEADS)
    grad_input = enc_back[0]
    enc_terms = enc_back[1:] + (embed_term, mask_term)
    return (dec_piece, grad_input, tuple(enc_terms) + tuple(dec_terms))


def local(
    enc_input,
    keep_count,
    keep_positions,
    enc_gain_one,
    enc_qkv_weight,
    enc_out_weight,
    enc_gain_two,
    enc_up_weight,
    enc_down_weight,
    embed_weight,
    mask_token,
    dec_gain_one,
    dec_qkv_weight,
    dec_out_weight,
    dec_gain_two,
    dec_up_weight,
    dec_down_weight,
    cotangent,
):
    enc_weights = (
        enc_gain_one,
        enc_qkv_weight,
        enc_out_weight,
        enc_gain_two,
        enc_up_weight,
        enc_down_weight,
    )
    dec_weights = (
        dec_gain_one,
        dec_qkv_weight,
        dec_out_weight,
        dec_gain_two,
        dec_up_weight,
        dec_down_weight,
    )
    all_params = (
        enc_gain_one,
        enc_qkv_weight,
        enc_out_weight,
        enc_gain_two,
        enc_up_weight,
        enc_down_weight,
        embed_weight,
        mask_token,
        dec_gain_one,
        dec_qkv_weight,
        dec_out_weight,
        dec_gain_two,
        dec_up_weight,
        dec_down_weight,
    )
    dec_pieces, input_grads, totals = micro_step(
        enc_input, keep_count, keep_positions, cotangent, enc_weights, embed_weight, mask_token, dec_weights
    )
    totals = (
        lax.psum_scatter(totals[0], ("dp", "seq"), scatter_dimension=0, tiled=True),
        lax.psum_scatter(totals[1], ("dp", "seq"), scatter_dimension=0, tiled=True),
        lax.psum_scatter(totals[2], ("dp", "seq"), scatter_dimension=0, tiled=True),
        lax.psum_scatter(totals[3], ("dp", "seq"), scatter_dimension=0, tiled=True),
        lax.psum_scatter(totals[4], ("dp", "seq"), scatter_dimension=0, tiled=True),
        lax.psum_scatter(totals[5], ("dp", "seq"), scatter_dimension=0, tiled=True),
        lax.psum_scatter(totals[6], ("dp", "seq"), scatter_dimension=0, tiled=True),
        lax.psum_scatter(totals[7], ("dp", "seq"), scatter_dimension=0, tiled=True),
        lax.psum_scatter(totals[8], ("dp", "seq"), scatter_dimension=0, tiled=True),
        lax.psum_scatter(totals[9], ("dp", "seq"), scatter_dimension=0, tiled=True),
        lax.psum_scatter(totals[10], ("dp", "seq"), scatter_dimension=0, tiled=True),
        lax.psum_scatter(totals[11], ("dp", "seq"), scatter_dimension=0, tiled=True),
        lax.psum_scatter(totals[12], ("dp", "seq"), scatter_dimension=0, tiled=True),
        lax.psum_scatter(totals[13], ("dp", "seq"), scatter_dimension=0, tiled=True),
    )
    dec_output = dec_pieces.reshape(cotangent.shape)
    enc_input_grad = input_grads.reshape(enc_input.shape)
    return (
        dec_output,
        enc_input_grad,
        totals[0],
        totals[1],
        totals[2],
        totals[3],
        totals[4],
        totals[5],
        totals[6],
        totals[7],
        totals[8],
        totals[9],
        totals[10],
        totals[11],
        totals[12],
        totals[13],
    )


MESH = pl.DeviceIdType.MESH
BF = jnp.bfloat16
F32 = jnp.float32
LANES = 128
TILE = 256
CHUNK = 48
VMEM_BYTES = 62 * 2**20
STEP = 40
FLOWS = ((0, 16, "xyls"), (16, 16, "yxls"), (32, 8, "lsxy"))
COPIES = 4 * len(FLOWS) + 1
SLOTS = 7
DIMS = "slyx"


def padded(count, multiple):
    return -(-count // multiple) * multiple


def nn(left, right):
    return lax.dot_general(left, right, (((1,), (0,)), ((), ())), preferred_element_type=F32)


def nt(left, right):
    return lax.dot_general(left, right, (((1,), (1,)), ((), ())), preferred_element_type=F32)


def tn(left, right):
    return lax.dot_general(left, right, (((0,), (0,)), ((), ())), preferred_element_type=F32)


def columns(tile):
    return pl.ds(pl.multiple_of(tile * TILE, TILE), TILE)


def each(count, body):
    lax.fori_loop(0, count, lambda index, carry: (body(index), carry)[1], 0)


def gelu_pair(values):
    reach = jnp.abs(values)
    point = 1.0 / (1.0 + 0.23164189 * reach)
    decay = jnp.exp(-0.5 * values * values)
    tail = 0.5307027145 * point - 0.7265760135
    tail = tail * point + 0.710706870
    tail = tail * point - 0.142248368
    tail = tail * point + 0.127414796
    tail = tail * point * decay
    below = jnp.where(values < 0.0, tail, 1.0 - tail)
    return values * below, below + values * decay * 0.3989422804014327


def norm_rows(total, source, gain, normed, inverse):
    width = gain.shape[-1]

    def body(chunk):
        rows = pl.ds(pl.multiple_of(chunk * CHUNK, CHUNK), CHUNK)
        stream = source[rows, :].astype(F32)
        centered = stream - jnp.sum(stream, axis=-1, keepdims=True) * (1.0 / width)
        scale = lax.rsqrt(jnp.sum(centered * centered, axis=-1, keepdims=True) * (1.0 / width) + eps)
        inverse[rows, :] = scale
        normed[rows, :] = (centered * scale * gain).astype(BF)

    each(total // CHUNK, body)


def norm_back(total, grad_normed, normed, inverse, gain, added, emit, partial):
    width = gain.shape[-1]
    over = 1.0 / gain
    partial[...] = jnp.zeros_like(partial)

    def body(chunk):
        rows = pl.ds(pl.multiple_of(chunk * CHUNK, CHUNK), CHUNK)
        grad = grad_normed[rows, :]
        unit = normed[rows, :].astype(F32)
        both = grad * unit
        scaled = grad * gain
        first = jnp.sum(scaled, axis=-1, keepdims=True) * (1.0 / width)
        second = jnp.sum(both, axis=-1, keepdims=True) * (1.0 / width)
        emit(rows, inverse[rows, :] * (scaled - first - unit * over * second) + added[rows, :].astype(F32))
        partial[...] += jnp.sum(both.reshape(CHUNK // 8, 8, width), axis=0)

    each(total // CHUNK, body)
    return jnp.sum(partial[...], axis=0, keepdims=True) * over


def head_masks(size):
    lane = lax.broadcasted_iota(jnp.int32, (1, LANES), 1)
    return [((lane >= h * size) & (lane < (h + 1) * size)).astype(F32) for h in range(LANES // size)]


def split_heads(block, masks):
    return jnp.concatenate([block * mask.astype(BF) for mask in masks], axis=0)


def merge_heads(stacked, masks, rows):
    total = stacked[:rows] * masks[0]
    for h in range(1, len(masks)):
        total = total + stacked[h * rows : (h + 1) * rows] * masks[h]
    return total


def attend_block(packed, width, rows, size, image, group, limit, kept, mixed):
    masks = head_masks(size)
    heads = len(masks)
    at = pl.ds(pl.multiple_of(image * rows, 16), rows)
    queries = packed[at, group * LANES : (group + 1) * LANES]
    keys = packed[at, width + group * LANES : width + (group + 1) * LANES]
    values = packed[at, 2 * width + group * LANES : 2 * width + (group + 1) * LANES]
    scores = (nt(split_heads(keys, masks), queries) * size**-0.5).reshape(heads, rows, rows)
    live = lax.broadcasted_iota(jnp.int32, (1, rows, 1), 1) < limit
    scores = jnp.where(live, scores, -1e30)
    raised = jnp.exp(scores - jnp.max(scores, axis=1, keepdims=True))
    weights = raised * (1.0 / jnp.sum(raised, axis=1, keepdims=True))
    low = weights.reshape(heads * rows, rows).astype(BF)
    kept[image, group] = low
    mixed[at, group * LANES : (group + 1) * LANES] = tn(low, split_heads(values, masks)).astype(BF)


def attend_back_block(packed, width, rows, size, image, group, kept, grad_mixed, grad_packed):
    masks = head_masks(size)
    heads = len(masks)
    at = pl.ds(pl.multiple_of(image * rows, 16), rows)
    queries = packed[at, group * LANES : (group + 1) * LANES]
    keys = packed[at, width + group * LANES : width + (group + 1) * LANES]
    values = packed[at, 2 * width + group * LANES : 2 * width + (group + 1) * LANES]
    grad_out = grad_mixed[at, group * LANES : (group + 1) * LANES]
    low = kept[image, group]
    weights = low.astype(F32)
    both = weights * nt(split_heads(values, masks), grad_out)
    inner = jnp.sum(both.reshape(heads, rows, rows), axis=1, keepdims=True)
    grad_scores = both - (weights.reshape(heads, rows, rows) * inner).reshape(heads * rows, rows)
    grad_scores = grad_scores.astype(BF)
    grad_values = merge_heads(nn(low, grad_out), masks, rows)
    grad_keys = merge_heads(nn(grad_scores, queries), masks, rows) * size**-0.5
    grad_queries = tn(grad_scores, split_heads(keys, masks)) * size**-0.5
    grad_packed[at, group * LANES : (group + 1) * LANES] = grad_queries.astype(BF)
    grad_packed[at, width + group * LANES : width + (group + 1) * LANES] = grad_keys.astype(BF)
    grad_packed[at, 2 * width + group * LANES : 2 * width + (group + 1) * LANES] = grad_values.astype(BF)


def pad_images(source, target, rows):
    images, count = source.shape[0], source.shape[1]
    whole = count // 16 * 16
    for image in range(images):
        target[image * rows + whole : (image + 1) * rows, :] = jnp.zeros((rows - whole, target.shape[1]), target.dtype)
        target[image * rows : image * rows + count, :] = source[image]


def enc_forward_kernel(
    rows, counts, stream, gains, qkv, out, up, down,
    normed_one_out, inverse_one_out, packed_out, kept_out, mixed_out, normed_two_out, inverse_two_out, active_out, slope_out, encoded_out,
    qkv_in, out_in, up_in, down_in, padded_in, middle,
    normed_one, inverse_one, packed, kept, mixed, normed_two, inverse_two, active, slope, encoded, in_sems, out_sems,
):
    images = stream.shape[0]
    total = images * rows
    width = stream.shape[-1]
    weights = [(qkv, qkv_in), (out, out_in), (up, up_in), (down, down_in)]
    loads = [pltpu.make_async_copy(source, target, in_sems.at[i]) for i, (source, target) in enumerate(weights)]
    for load in loads:
        load.start()
    results = [
        (normed_one, normed_one_out), (inverse_one, inverse_one_out), (packed, packed_out), (kept, kept_out), (mixed, mixed_out),
        (normed_two, normed_two_out), (inverse_two, inverse_two_out), (active, active_out), (slope, slope_out), (encoded, encoded_out),
    ]
    stores = [pltpu.make_async_copy(source, target, out_sems.at[i]) for i, (source, target) in enumerate(results)]
    pad_images(stream, padded_in, rows)
    norm_rows(total, padded_in, gains[0:1, :], normed_one, inverse_one)
    loads[0].wait()

    def project(tile):
        packed[:, columns(tile)] = nn(normed_one[...], qkv_in[:, columns(tile)]).astype(BF)

    each(qkv.shape[1] // TILE, project)
    for store in stores[:3]:
        store.start()

    def mix(image):
        for group in range(width // LANES):
            attend_block(packed, width, rows, width // HEADS, image, group, counts[image], kept, mixed)

    each(images, mix)
    for store in stores[3:5]:
        store.start()
    loads[1].wait()

    def add_out(tile):
        middle[:, columns(tile)] = padded_in[:, columns(tile)].astype(F32) + nn(mixed[...], out_in[:, columns(tile)])

    each(width // TILE, add_out)
    norm_rows(total, middle, gains[1:2, :], normed_two, inverse_two)
    loads[2].wait()
    feed_up(normed_two, up_in, active, slope)
    for store in stores[5:9]:
        store.start()
    loads[3].wait()

    def add_down(tile):
        encoded[:, columns(tile)] = (middle[:, columns(tile)] + nn(active[...], down_in[:, columns(tile)])).astype(BF)

    each(width // TILE, add_down)
    stores[9].start()
    for store in stores:
        store.wait()


def feed_up(normed, up, active, slope):
    def body(tile):
        value, derivative = gelu_pair(nn(normed[...], up[:, columns(tile)]))
        active[:, columns(tile)] = value.astype(BF)
        slope[:, columns(tile)] = derivative.astype(BF)

    each(up.shape[1] // TILE, body)


def feed_back(grad_low, down, slope, grad_pre):
    def body(tile):
        grad = nt(grad_low[...], down[columns(tile), :]) * slope[:, columns(tile)].astype(F32)
        grad_pre[:, columns(tile)] = grad.astype(BF)

    each(down.shape[0] // TILE, body)


def times_back(grad, matrix, result):
    def body(tile):
        result[:, columns(tile)] = nt(grad[...], matrix[columns(tile), :]).astype(result.dtype)

    each(matrix.shape[0] // TILE, body)


def one_hot(positions, image, limit, slots, places):
    place = lax.broadcasted_iota(jnp.int32, (places, slots), 0)
    slot = lax.broadcasted_iota(jnp.int32, (places, slots), 1)
    return jnp.where((positions[image : image + 1, :slots] == place) & (slot < limit), 1.0, 0.0)


def coords():
    seq, dp = lax.axis_index("seq"), lax.axis_index("dp")
    return {"s": dp // 4, "l": (dp // 2) % 2, "y": dp % 2, "x": seq // 2, "c": seq % 2}


def partner(here, dim):
    other = dict(here)
    other[dim] = 1 - here[dim]
    return (other["s"] * 4 + other["l"] * 2 + other["y"], other["x"] * 2 + other["c"])


class Reduction:
    def __init__(self, gathered, result, scratch):
        self.gathered, self.result = gathered, result
        self.steps = gathered.shape[1] // STEP
        self.stage, self.land = scratch[0], scratch[1]
        self.lands = [scratch[2 + 4 * f : 6 + 4 * f] for f in range(len(FLOWS))]
        self.send_sem, self.recv_sem, self.load_sem = scratch[-3:]
        self.here = coords()
        self.next, self.ready, self.loading = 0, 0, False

    @staticmethod
    def scratch():
        shapes = [pltpu.VMEM((2, 2, 2, 2, 2, 2, STEP, TILE), F32), pltpu.VMEM((SLOTS, 2, 2, 2, 2, STEP, TILE), F32)]
        for _, rows, _ in FLOWS:
            for k in range(1, 5):
                shapes.append(pltpu.VMEM((SLOTS,) + (2,) * (4 - k) + (rows, TILE), F32))
        return shapes + [pltpu.SemaphoreType.DMA((SLOTS, COPIES)), pltpu.SemaphoreType.DMA((SLOTS, COPIES)), pltpu.SemaphoreType.DMA((2,))]

    def enter(self):
        barrier = pltpu.get_barrier_semaphore()
        for dim in "c" + DIMS:
            pl.semaphore_signal(barrier, inc=1, device_id=partner(self.here, dim), device_id_type=MESH)
        pl.semaphore_wait(barrier, 5)

    def load(self, t):
        rows = pl.ds(pl.multiple_of(t * STEP, 8), STEP)
        whole = self.gathered.reshape(2, 2, 2, 2, 2, self.gathered.shape[1], TILE)
        return pltpu.make_async_copy(whole.at[:, :, :, :, :, rows, :], self.stage.at[lax.rem(t, 2)], self.load_sem.at[lax.rem(t, 2)])

    def core_copy(self, t):
        slot = lax.rem(t, SLOTS)
        return pltpu.make_async_remote_copy(
            src_ref=self.stage.at[lax.rem(t, 2), :, :, :, :, 1 - self.here["c"]],
            dst_ref=self.land.at[slot],
            send_sem=self.send_sem.at[slot, COPIES - 1],
            recv_sem=self.recv_sem.at[slot, COPIES - 1],
            device_id=partner(self.here, "c"),
            device_id_type=MESH,
        )

    def half(self, t, flow, k, kept):
        first, rows, order = FLOWS[flow]
        left = [dim for dim in DIMS if dim not in order[:k]]
        side = self.here[order[k]] if kept else 1 - self.here[order[k]]
        at = (lax.rem(t, SLOTS),) + tuple(side if dim == order[k] else slice(None) for dim in left)
        if k == 0:
            return self.land.at[at + (pl.ds(first, rows),)]
        return self.lands[flow][k - 1].at[at]

    def copy(self, t, flow, k):
        slot = lax.rem(t, SLOTS)
        return pltpu.make_async_remote_copy(
            src_ref=self.half(t, flow, k, False),
            dst_ref=self.lands[flow][k].at[slot],
            send_sem=self.send_sem.at[slot, flow * 4 + k],
            recv_sem=self.recv_sem.at[slot, flow * 4 + k],
            device_id=partner(self.here, FLOWS[flow][2][k]),
            device_id_type=MESH,
        )

    def advance(self, k, t):
        slot = lax.rem(t, SLOTS)
        if k == 1:
            self.core_copy(t).wait()
            self.land[slot] += self.stage[lax.rem(t, 2), :, :, :, :, self.here["c"]]
            for flow in range(len(FLOWS)):
                self.copy(t, flow, 0).start()
            return
        for flow in range(len(FLOWS)):
            self.copy(t, flow, k - 2).wait()
            kept = self.half(t, flow, k - 2, True)
            if k < 5:
                self.lands[flow][k - 2][slot] += kept[...]
                self.copy(t, flow, k - 1).start()
            else:
                first, rows, _ = FLOWS[flow]
                at = pl.ds(pl.multiple_of(t * STEP + first, 8), rows)
                self.result[at, :] = self.lands[flow][3][slot] + kept[...]

    def step(self, t, fresh):
        @pl.when(t < fresh)
        def _():
            self.load(t).wait()
            self.core_copy(t).start()

        for k in range(1, 6):
            @pl.when((t >= k) & (t < self.steps + k))
            def _():
                self.advance(k, t - k)

        @pl.when(t + 1 < fresh)
        def _():
            self.load(t + 1).start()

    def run(self, count, body, every=1):
        first, fresh = self.next, self.ready // STEP
        pumps = min(count // every, fresh - first)
        if pumps <= 0:
            each(count, body)
            return
        if not self.loading:
            self.load(first).start()

        def one(index):
            body(index)

            @pl.when((lax.rem(index, every) == every - 1) & (index < pumps * every))
            def _():
                self.step(first + lax.div(index, every), fresh)

        each(count, one)
        self.next = first + pumps
        self.loading = self.next < fresh

    def pump(self, count=1):
        self.run(count, lambda index: None)

    def finish(self, beside):
        first, fresh = self.next, self.ready // STEP
        if not self.loading and first < fresh:
            self.load(first).start()

        def one(index):
            self.step(first + index, fresh)
            beside(index)

        each(self.steps + 5 - first, one)

    def send(self, place, sems, tile, rows, count, every=0, slots=2):
        start = self.ready

        def copy(slot, at):
            return pltpu.make_async_copy(place(slot), self.gathered.at[:, pl.ds(at, rows), :], sems.at[slot])

        def body(n):
            slot = lax.rem(n, slots)

            @pl.when(n >= slots)
            def _():
                copy(slot, start).wait()

            place(slot)[...] = tile(n).reshape(32, rows, TILE)
            copy(slot, pl.multiple_of(start + n * rows, 8)).start()

        if every:
            self.run(count, body, every)
        else:
            each(count, body)
        for n in range(max(count - slots, 0), count):
            copy(n % slots, start).wait()
        self.ready = start + count * rows


def backward_kernel(
    erows, drows,
    counts, positions, gains, table, encoded, embed, dec_qkv, dec_out, dec_up, dec_down, cotangent,
    enc_qkv, enc_out, enc_up, enc_down,
    enc_normed_one, enc_inverse_one, enc_packed, enc_kept, enc_mixed, enc_normed_two, enc_inverse_two, enc_active, enc_slope,
    result, input_grad, gathered, reduced, vector_sum,
    padded_positions, grad_embedded, vector_part, vector_land, vector_send, vector_recv, dec_sems, enc_sems, tile_sems, *scratch,
):
    images, places, dwidth = cotangent.shape
    slots, width = input_grad.shape[1:]
    dhidden, hidden = dec_up.shape[1], enc_up.shape[1]
    dtotal, etotal = images * drows, images * erows
    reduction = Reduction(gathered, reduced, scratch)
    mask_token, dec_gain_one, dec_gain_two = gains[2:3, :dwidth], gains[3:4, :dwidth], gains[4:5, :dwidth]
    row = lax.broadcasted_iota(jnp.int32, (drows, 1), 0)
    padded_positions[:images, :slots] = positions[...]
    vector_part[...] = jnp.zeros_like(vector_part)

    def pick_of(image):
        place = lax.broadcasted_iota(jnp.int32, (drows, erows), 0)
        slot = lax.broadcasted_iota(jnp.int32, (drows, erows), 1)
        named = (padded_positions[image : image + 1, :erows] == place) & (slot < counts[image])
        return jnp.where(named, 1.0, 0.0)

    def decoder(
        qkv, out, up, down, filled, normed_one, inverse_one, packed, kept, mixed, middle, normed_two, inverse_two, slope, wide_low, stage
    ):
        into_result = pltpu.make_async_copy(cotangent, result, dec_sems.at[0])
        weights = [(dec_qkv, qkv), (dec_out, out), (dec_up, up), (dec_down, down)]
        loads = [pltpu.make_async_copy(source, target, dec_sems.at[1 + i]) for i, (source, target) in enumerate(weights)]

        def fill(table_in, encoded_in, embed_in):
            starts = [(encoded, encoded_in), (embed, embed_in), (table, table_in)]
            starts = [pltpu.make_async_copy(source, target, dec_sems.at[5 + i]) for i, (source, target) in enumerate(starts)]
            for copy in starts + loads + [into_result]:
                copy.start()
            reduction.enter()
            starts[0].wait()
            starts[1].wait()
            high, rest = mixed, wide_low

            def embed_tile(tile):
                value = nn(encoded_in[...], embed_in[:, columns(tile)])
                top = value.astype(BF)
                high[pl.ds(0, etotal), columns(tile)] = top
                rest[pl.ds(0, etotal), columns(tile)] = (value - top.astype(F32)).astype(BF)

            each(dwidth // TILE, embed_tile)
            starts[2].wait()
            for image in range(images):
                pick = pick_of(image)
                low_pick = pick.astype(BF)
                at = pl.ds(image * erows, erows)
                picked = nn(low_pick, high[at, :]) + nn(low_pick, rest[at, :])
                covered = jnp.sum(pick, axis=1, keepdims=True) > 0.5
                value = jnp.where(covered, picked, mask_token) + table_in[...]
                filled[pl.ds(image * drows, drows), :] = jnp.where(row < places, value, 0.0).astype(BF)

        pl.run_scoped(
            fill, pltpu.VMEM(table.shape, F32), pltpu.VMEM(encoded.shape, BF), pltpu.VMEM(embed.shape, BF)
        )
        norm_rows(dtotal, filled, dec_gain_one, normed_one, inverse_one)
        loads[0].wait()

        def project(tile):
            packed[:, columns(tile)] = nn(normed_one[...], qkv[:, columns(tile)]).astype(BF)

        each(qkv.shape[1] // TILE, project)

        def mix(image):
            for group in range(dwidth // LANES):
                attend_block(packed, dwidth, drows, dwidth // DHEADS, image, group, places, kept, mixed)

        each(images, mix)
        loads[1].wait()

        def add_out(tile):
            middle[:, columns(tile)] = filled[:, columns(tile)].astype(F32) + nn(mixed[...], out[:, columns(tile)])

        each(dwidth // TILE, add_out)
        norm_rows(dtotal, middle, dec_gain_two, normed_two, inverse_two)
        loads[2].wait()
        grad_low = wide_low
        into_result.wait()
        pad_images(result, grad_low, drows)
        block = dwidth // 32

        def place(slot):
            return stage.at[:, pl.ds(pl.multiple_of(slot * block, 8), block), :]

        def feed(active):
            feed_up(normed_two, up, active, slope)
            reduction.send(lambda slot: stage, tile_sems, lambda n: tn(active[...], grad_low[:, columns(n)]), dhidden // 32, dwidth // TILE, slots=1)
            reduction.pump()
            loads[3].wait()
            for tile in range(dwidth // TILE):
                at = slice(tile * TILE, (tile + 1) * TILE)
                value = (middle[:, at] + nn(active[...], down[:, at])).astype(BF)
                for image in range(images):
                    result[image, :, at] = value[image * drows : image * drows + places]

        pl.run_scoped(feed, pltpu.VMEM((dtotal, dhidden), BF))
        reduction.pump()
        feed_back(grad_low, down, slope, slope)
        reduction.pump()
        reduction.send(place, tile_sems, lambda n: tn(normed_two[...], slope[:, columns(n)]), block, dhidden // TILE)
        reduction.pump()
        times_back(slope, up, middle)
        reduction.pump()
        grad_attend = wide_low

        def keep_middle(at, grad):
            middle[at, :] = grad
            grad_attend[at, :] = grad.astype(BF)

        def late(wide, partial):
            vector_part[0, 4:5, :dwidth] = norm_back(
                dtotal, middle, normed_two, inverse_two, dec_gain_two, grad_low, keep_middle, partial
            )
            reduction.pump()
            reduction.send(place, tile_sems, lambda n: tn(mixed[...], grad_attend[:, columns(n)]), block, dwidth // TILE)
            grad_mixed = normed_two
            times_back(grad_attend, out, grad_mixed)

            def mix_back(image):
                for group in range(dwidth // LANES):
                    attend_back_block(packed, dwidth, drows, dwidth // DHEADS, image, group, kept, grad_mixed, packed)

            reduction.run(images, mix_back, 3)
            reduction.send(place, tile_sems, lambda n: tn(normed_one[...], packed[:, columns(n)]), block, 3 * dwidth // TILE)
            reduction.pump()
            times_back(packed, qkv, wide)

            def keep_filled(at, grad):
                filled[at, :] = grad.astype(BF)

            vector_part[0, 3:4, :dwidth] = norm_back(
                dtotal, wide, normed_one, inverse_one, dec_gain_one, middle, keep_filled, partial
            )
            reduction.pump()

        pl.run_scoped(late, pltpu.VMEM((dtotal, dwidth), F32), pltpu.VMEM((8, dwidth), F32))
        token = jnp.zeros((1, dwidth), F32)
        for image in range(images):
            pick = pick_of(image)
            covered = jnp.sum(pick, axis=1, keepdims=True) > 0.5
            grad = filled[pl.ds(image * drows, drows), :]
            token = token + jnp.sum(jnp.where(covered | (row >= places), 0.0, grad.astype(F32)), axis=0, keepdims=True)
            grad_embedded[pl.ds(image * erows, erows), :] = tn(pick.astype(BF), grad).astype(BF)
        vector_part[0, 2:3, :dwidth] = token

    dgroups, dheads = dwidth // LANES, DHEADS * LANES // dwidth
    wide_shape = (dtotal, dwidth)
    pl.run_scoped(
        decoder,
        *[pltpu.VMEM(ref.shape, BF) for ref in (dec_qkv, dec_out, dec_up, dec_down)],
        pltpu.VMEM(wide_shape, BF), pltpu.VMEM(wide_shape, BF), pltpu.VMEM((dtotal, 1), F32), pltpu.VMEM((dtotal, 3 * dwidth), BF),
        pltpu.VMEM((images, dgroups, dheads * drows, drows), BF), pltpu.VMEM(wide_shape, BF), pltpu.VMEM(wide_shape, F32),
        pltpu.VMEM(wide_shape, BF), pltpu.VMEM((dtotal, 1), F32), pltpu.VMEM((dtotal, dhidden), BF), pltpu.VMEM(wide_shape, BF),
        pltpu.VMEM((32, dhidden // 32, TILE), F32),
    )

    def encoder(
        embed_in, out, weight, down, normed_one, inverse_one, packed, kept, mixed, normed_two, inverse_two, grad_pre,
        grad_low, grad_attend, middle, wide, stage,
    ):
        sources = [
            (embed, embed_in), (enc_down, down), (enc_slope, grad_pre), (enc_normed_two, normed_two), (enc_up, weight),
            (enc_inverse_two, inverse_two), (enc_out, out), (enc_mixed, mixed), (enc_packed, packed), (enc_kept, kept),
            (enc_normed_one, normed_one), (enc_inverse_one, inverse_one),
        ]
        loads = [pltpu.make_async_copy(source, target, enc_sems.at[i]) for i, (source, target) in enumerate(sources)]
        block = width // 32

        def place(slot):
            return stage.at[:, pl.ds(pl.multiple_of(slot * block, 8), block), :]

        def feed(active, encoded_in):
            starts = [(encoded, encoded_in), (enc_active, active)]
            starts = [pltpu.make_async_copy(source, target, enc_sems.at[len(loads) + i]) for i, (source, target) in enumerate(starts)]
            for copy in starts + loads:
                copy.start()
            starts[0].wait()
            reduction.send(place, tile_sems, lambda n: tn(encoded_in[...], grad_embedded[:, columns(n)]), block, dwidth // TILE)
            loads[0].wait()
            times_back(grad_embedded, embed_in, wide)

            def low_chunk(chunk):
                at = pl.ds(pl.multiple_of(chunk * CHUNK, CHUNK), CHUNK)
                grad_low[at, :] = wide[at, :].astype(BF)

            each(etotal // CHUNK, low_chunk)
            reduction.pump()
            starts[1].wait()
            reduction.send(lambda slot: stage, tile_sems, lambda n: tn(active[...], grad_low[:, columns(n)]), hidden // 32, width // TILE, slots=1)

        pl.run_scoped(feed, pltpu.VMEM(enc_active.shape, BF), pltpu.VMEM(encoded.shape, BF))
        reduction.pump()
        loads[1].wait()
        loads[2].wait()
        feed_back(grad_low, down, grad_pre, grad_pre)
        reduction.pump()
        loads[3].wait()
        reduction.send(place, tile_sems, lambda n: tn(normed_two[...], grad_pre[:, columns(n)]), block, hidden // TILE, every=6)
        loads[4].wait()
        times_back(grad_pre, weight, middle)
        reduction.pump()
        into_qkv = pltpu.make_async_copy(enc_qkv, weight.at[:, : enc_qkv.shape[1]], enc_sems.at[len(loads) + 2])
        into_qkv.start()
        loads[5].wait()

        def late(grad_mixed, partial, input_stage):
            def keep_middle(at, grad):
                middle[at, :] = grad
                grad_attend[at, :] = grad.astype(BF)

            vector_part[0, 1:2, :] = norm_back(etotal, middle, normed_two, inverse_two, gains[1:2, :], wide, keep_middle, partial)
            loads[6].wait()
            loads[7].wait()
            reduction.pump()
            reduction.send(place, tile_sems, lambda n: tn(mixed[...], grad_attend[:, columns(n)]), block, width // TILE)
            times_back(grad_attend, out, grad_mixed)
            for load in loads[8:]:
                load.wait()

            def mix_back(image):
                for group in range(width // LANES):
                    attend_back_block(packed, width, erows, width // HEADS, image, group, kept, grad_mixed, packed)

            reduction.run(images, mix_back, 3)
            reduction.send(place, tile_sems, lambda n: tn(normed_one[...], packed[:, columns(n)]), block, 3 * width // TILE, every=9)
            left = gathered.shape[1] - reduction.ready
            if left:
                stage[:, :left, :] = jnp.zeros((32, left, TILE), F32)
                rest = pltpu.make_async_copy(
                    stage.at[:, pl.ds(0, left), :], gathered.at[:, pl.ds(reduction.ready, left), :], tile_sems.at[0]
                )
                rest.start()
                rest.wait()
                reduction.ready += left
            into_qkv.wait()
            times_back(packed, weight.at[:, : enc_qkv.shape[1]], wide)
            reduction.pump()

            def keep_input(at, grad):
                wide[at, :] = grad

            vector_part[0, 0:1, :] = norm_back(etotal, wide, normed_one, inverse_one, gains[0:1, :], middle, keep_input, partial)
            for image in range(images):
                input_stage[image] = wide[image * erows : image * erows + slots, :]
            store = pltpu.make_async_copy(input_stage, input_grad, tile_sems.at[0])
            store.start()
            reduction.pump()
            store.wait()

        pl.run_scoped(
            late, pltpu.VMEM((etotal, width), BF), pltpu.VMEM((8, width), F32), pltpu.VMEM(input_grad.shape, F32)
        )

    pl.run_scoped(
        encoder,
        pltpu.VMEM(embed.shape, BF), pltpu.VMEM(enc_out.shape, BF), pltpu.VMEM(enc_up.shape, BF), pltpu.VMEM(enc_down.shape, BF),
        pltpu.VMEM(enc_normed_one.shape, BF), pltpu.VMEM(enc_inverse_one.shape, F32), pltpu.VMEM(enc_packed.shape, BF),
        pltpu.VMEM(enc_kept.shape, BF), pltpu.VMEM(enc_mixed.shape, BF), pltpu.VMEM(enc_normed_two.shape, BF),
        pltpu.VMEM(enc_inverse_two.shape, F32), pltpu.VMEM(enc_slope.shape, BF),
        pltpu.VMEM((etotal, width), BF), pltpu.VMEM((etotal, width), BF), pltpu.VMEM((etotal, width), F32), pltpu.VMEM((etotal, width), F32),
        pltpu.VMEM((32, hidden // 32, TILE), F32),
    )
    order = "c" + DIMS

    def vector_copy(k):
        return pltpu.make_async_remote_copy(
            src_ref=vector_part.at[k],
            dst_ref=vector_land.at[k],
            send_sem=vector_send.at[k],
            recv_sem=vector_recv.at[k],
            device_id=partner(reduction.here, order[k]),
            device_id_type=MESH,
        )

    def vector_step(index):
        for k in range(6):
            @pl.when(index == k)
            def _():
                if k:
                    vector_copy(k - 1).wait()
                    vector_part[k] = vector_part[k - 1] + vector_land[k - 1]
                if k < 5:
                    vector_copy(k).start()

    reduction.finish(vector_step)
    vector_sum[...] = vector_part[5]


def unpack_kernel(source, *targets):
    at = 0
    for target in targets:
        block, width = target.shape
        for n in range(width // TILE):
            target[:, n * TILE : (n + 1) * TILE] = source[at : at + block, :]
            at += block


def vmem(count):
    return [pl.BlockSpec(memory_space=pltpu.VMEM)] * count


def anywhere(count):
    return [pl.BlockSpec(memory_space=pl.ANY)] * count


def shapes(*pairs):
    return [jax.ShapeDtypeStruct(shape, dtype) for shape, dtype in pairs]


def scratches(*pairs):
    return [pltpu.VMEM(shape, dtype) for shape, dtype in pairs]


def fast_local(
    enc_input, keep_count, keep_positions,
    enc_gain_one, enc_qkv_weight, enc_out_weight, enc_gain_two, enc_up_weight, enc_down_weight,
    embed_weight, mask_token,
    dec_gain_one, dec_qkv_weight, dec_out_weight, dec_gain_two, dec_up_weight, dec_down_weight,
    cotangent,
):
    images, slots, width = enc_input.shape
    places, dwidth = cotangent.shape[1:]
    hidden, dhidden = enc_up_weight.shape[1], dec_up_weight.shape[1]
    erows, drows = padded(slots, 16), padded(places, 16)
    etotal, dtotal = images * erows, images * drows
    egroups, dgroups = width // LANES, dwidth // LANES
    eheads, dheads = HEADS // egroups, DHEADS // dgroups
    smem = [pl.BlockSpec(memory_space=pltpu.SMEM)]
    settings = functools.partial(pltpu.CompilerParams, vmem_limit_bytes=VMEM_BYTES)
    vectors = (enc_gain_one, enc_gain_two, mask_token, dec_gain_one, dec_gain_two)
    gains = jnp.stack([jnp.pad(vector, (0, width - vector.shape[0])) for vector in vectors]).astype(F32)
    gains = jnp.pad(gains, ((0, 8 - len(vectors)), (0, 0)))

    saved = shapes(
        ((etotal, width), BF), ((etotal, 1), F32), ((etotal, 3 * width), BF), ((images, egroups, eheads * erows, erows), BF),
        ((etotal, width), BF), ((etotal, width), BF), ((etotal, 1), F32), ((etotal, hidden), BF), ((etotal, hidden), BF), ((etotal, width), BF),
    )
    normed_one, inverse_one, packed, kept, mixed, normed_two, inverse_two, active, slope, encoded = pl.pallas_call(
        functools.partial(enc_forward_kernel, erows),
        name="enc_forward",
        out_shape=saved,
        in_specs=smem + vmem(2) + anywhere(4),
        out_specs=anywhere(10),
        scratch_shapes=scratches(
            *((weight.shape, BF) for weight in (enc_qkv_weight, enc_out_weight, enc_up_weight, enc_down_weight)),
            ((etotal, width), BF), ((etotal, width), F32), *((array.shape, array.dtype) for array in saved),
        ) + [pltpu.SemaphoreType.DMA((4,)), pltpu.SemaphoreType.DMA((10,))],
        compiler_params=settings(),
    )(keep_count, enc_input, gains, enc_qkv_weight, enc_out_weight, enc_up_weight, enc_down_weight)

    table = jnp.asarray(position_rows(places, dwidth, drows))
    block = dwidth // 32
    eblock = width // 32
    layout = (
        (dhidden // 32, dwidth), (block, dhidden), (block, dwidth), (block, 3 * dwidth), (eblock, dwidth),
        (hidden // 32, width), (eblock, hidden), (eblock, width), (eblock, 3 * width),
    )
    share_rows = padded(sum(rows * columns // TILE for rows, columns in layout), STEP)
    dec_output, input_grad, _, reduced, vector_sum = pl.pallas_call(
        functools.partial(backward_kernel, erows, drows),
        name="backward",
        out_shape=shapes(
            (cotangent.shape, BF), (enc_input.shape, F32), ((32, share_rows, TILE), F32), ((share_rows, TILE), F32), ((8, width), F32),
        ),
        in_specs=smem + vmem(2) + anywhere(21),
        out_specs=vmem(1) + anywhere(2) + vmem(2),
        scratch_shapes=scratches(
            ((8, LANES), jnp.int32), ((etotal, dwidth), BF), ((6, 8, width), F32), ((5, 8, width), F32),
        ) + [pltpu.SemaphoreType.DMA((count,)) for count in (5, 5, 8, 15, 2)] + Reduction.scratch(),
        compiler_params=settings(collective_id=0, has_side_effects=True),
    )(
        keep_count, keep_positions, gains, table, encoded, embed_weight, dec_qkv_weight, dec_out_weight, dec_up_weight, dec_down_weight,
        cotangent, enc_qkv_weight, enc_out_weight, enc_up_weight, enc_down_weight,
        normed_one, inverse_one, packed, kept, mixed, normed_two, inverse_two, active, slope,
    )
    dec_down, dec_up, dec_out, dec_qkv, embed, enc_down, enc_up, enc_out, enc_qkv = pl.pallas_call(
        unpack_kernel,
        name="unpack",
        out_shape=shapes(*((shape, F32) for shape in layout)),
        in_specs=vmem(1),
        out_specs=vmem(9),
    )(reduced)
    index = lax.axis_index("dp") * lax.axis_size("seq") + lax.axis_index("seq")
    cuts = []
    for at, vector in enumerate(vectors):
        size = vector.shape[0] // 32
        cuts.append(lax.dynamic_slice(vector_sum, (at, index * size), (1, size))[0])
    return (
        dec_output, input_grad, cuts[0], enc_qkv, enc_out, cuts[1], enc_up, enc_down, embed, cuts[2],
        cuts[3], dec_qkv, dec_out, cuts[4], dec_up, dec_down,
    )


def position_rows(places, width, rows):
    side = math.isqrt(places)
    quarter = width // 4
    place = np.arange(places)
    rate = 1.0 / 10000.0 ** (np.arange(quarter) / quarter)
    across, down = place[:, None] % side * rate, place[:, None] // side * rate
    table = np.concatenate([np.sin(across), np.cos(across), np.sin(down), np.cos(down)], axis=1)
    return np.pad(table, ((0, rows - places), (0, 0))).astype(np.float32)


def solution(mesh):
    placed = (
        P(("dp", "seq"), None, None),
        P(("dp", "seq")),
        P(("dp", "seq"), None),
        P(),
        P(),
        P(),
        P(),
        P(),
        P(),
        P(),
        P(),
        P(),
        P(),
        P(),
        P(),
        P(),
        P(),
        P(("dp", "seq"), None, None),
    )
    fast = (mesh.shape["dp"], mesh.shape["seq"]) == (8, 4)
    return jax.shard_map(
        fast_local if fast else local,
        mesh=mesh,
        in_specs=placed,
        out_specs=(
            P(("dp", "seq"), None, None),
            P(("dp", "seq"), None, None),
            P(("dp", "seq")),
            P(("dp", "seq"), None),
            P(("dp", "seq"), None),
            P(("dp", "seq")),
            P(("dp", "seq"), None),
            P(("dp", "seq"), None),
            P(("dp", "seq"), None),
            P(("dp", "seq")),
            P(("dp", "seq")),
            P(("dp", "seq"), None),
            P(("dp", "seq"), None),
            P(("dp", "seq")),
            P(("dp", "seq"), None),
            P(("dp", "seq"), None),
        ),
        check_vma=False,
    )
```

```python
import functools
import math

import jax
import jax.numpy as jnp
import numpy as np
from jax import lax
from jax.experimental import pallas as pl
from jax.experimental.pallas import tpu as pltpu
from jax.sharding import PartitionSpec as P

HEADS = 12
DHEADS = 16
PATCHES = 196


eps = 1e-06


def position_table(count, model_width):
    grid_side = math.isqrt(count)
    quarter = model_width // 4
    places = jnp.arange(count)
    across = (places % grid_side).astype(jnp.float32)
    row_place = (places // grid_side).astype(jnp.float32)
    frequency = 1.0 / 10000.0 ** (jnp.arange(quarter).astype(jnp.float32) / quarter)
    return jnp.concatenate(
        [
            jnp.sin(across[:, None] * frequency),
            jnp.cos(across[:, None] * frequency),
            jnp.sin(row_place[:, None] * frequency),
            jnp.cos(row_place[:, None] * frequency),
        ],
        axis=1,
    )


def contract(operand, matrix):
    return jnp.einsum("...i,ij->...j", operand, matrix, preferred_element_type=jnp.float32)


def contract_back(gradient, matrix):
    return jnp.einsum("...j,ij->...i", gradient, matrix, preferred_element_type=jnp.float32)


def outer_sum(operand, gradient):
    flat_left = operand.reshape(-1, operand.shape[-1])
    flat_right = gradient.reshape(-1, gradient.shape[-1])
    return lax.dot_general(
        flat_left, flat_right, (((0,), (0,)), ((), ())), preferred_element_type=jnp.float32
    )


def exact_gelu(values):
    return jax.nn.gelu(values, approximate=False)


def gelu_back(pre_act, grad_active):
    unused, pullback = jax.vjp(exact_gelu, pre_act)
    return pullback(grad_active)[0]


def layer_norm(stream, gain_vec):
    row_mean = jnp.mean(stream, axis=-1, keepdims=True)
    centered = stream - row_mean
    inverse = lax.rsqrt(jnp.mean(centered * centered, axis=-1, keepdims=True) + eps)
    unit_rows = centered * inverse
    return (unit_rows * gain_vec, unit_rows, inverse)


def layer_norm_back(grad_normed, unit_rows, inverse, gain_vec):
    grad_gain = jnp.sum((grad_normed * unit_rows).reshape(-1, unit_rows.shape[-1]), axis=0)
    grad_unit = grad_normed * gain_vec
    grad_stream = inverse * (
        grad_unit
        - jnp.mean(grad_unit, axis=-1, keepdims=True)
        - unit_rows * jnp.mean(grad_unit * unit_rows, axis=-1, keepdims=True)
    )
    return (grad_stream, grad_gain)


def attend(packed, head_count, key_mask):
    batch_size, row_count, triple_width = packed.shape
    model_width = triple_width // 3
    head_size = model_width // head_count
    queries = packed[:, :, :model_width].reshape(batch_size, row_count, head_count, head_size)
    key_heads = packed[:, :, model_width : 2 * model_width].reshape(
        batch_size, row_count, head_count, head_size
    )
    value_heads = packed[:, :, 2 * model_width :].reshape(
        batch_size, row_count, head_count, head_size
    )
    scores = jnp.einsum(
        "bqhd,bkhd->bhqk", queries, key_heads, preferred_element_type=jnp.float32
    ) * head_size ** (-0.5)
    if key_mask is not None:
        scores = jnp.where(key_mask[:, None, None, :], scores, -1e30)
    row_max = jnp.max(scores, axis=-1, keepdims=True)
    raised = jnp.exp(scores - row_max)
    attn_weights = raised / jnp.sum(raised, axis=-1, keepdims=True)
    attn_low = attn_weights.astype(jnp.bfloat16)
    mixed_heads = jnp.einsum(
        "bhqk,bkhd->bqhd", attn_low, value_heads, preferred_element_type=jnp.float32
    )
    mixed_heads = mixed_heads.reshape(batch_size, row_count, model_width).astype(jnp.bfloat16)
    return (mixed_heads, attn_weights, attn_low)


def attend_back(packed, attn_weights, attn_low, grad_mixed, head_count):
    batch_size, row_count, triple_width = packed.shape
    model_width = triple_width // 3
    head_size = model_width // head_count
    factor = head_size ** (-0.5)
    queries = packed[:, :, :model_width].reshape(batch_size, row_count, head_count, head_size)
    key_heads = packed[:, :, model_width : 2 * model_width].reshape(
        batch_size, row_count, head_count, head_size
    )
    value_heads = packed[:, :, 2 * model_width :].reshape(
        batch_size, row_count, head_count, head_size
    )
    grad_heads = grad_mixed.reshape(batch_size, row_count, head_count, head_size)
    grad_values = jnp.einsum(
        "bhqk,bqhd->bkhd", attn_low, grad_heads, preferred_element_type=jnp.float32
    )
    grad_attn = jnp.einsum(
        "bqhd,bkhd->bhqk", grad_heads, value_heads, preferred_element_type=jnp.float32
    )
    grad_scores = attn_weights * (
        grad_attn - jnp.sum(attn_weights * grad_attn, axis=-1, keepdims=True)
    )
    grad_scores = grad_scores.astype(jnp.bfloat16)
    grad_queries = (
        jnp.einsum("bhqk,bkhd->bqhd", grad_scores, key_heads, preferred_element_type=jnp.float32)
        * factor
    )
    grad_keys = (
        jnp.einsum("bhqk,bqhd->bkhd", grad_scores, queries, preferred_element_type=jnp.float32)
        * factor
    )
    grad_packed = jnp.concatenate(
        [
            grad_queries.reshape(batch_size, row_count, model_width),
            grad_keys.reshape(batch_size, row_count, model_width),
            grad_values.reshape(batch_size, row_count, model_width),
        ],
        axis=-1,
    )
    return grad_packed.astype(jnp.bfloat16)


def mlp_forward(middle, gain_two, up_weight, down_weight):
    normed_two, unit_two, inverse_two = layer_norm(middle, gain_two.astype(jnp.float32))
    second_low = normed_two.astype(jnp.bfloat16)
    pre_act = contract(second_low, up_weight)
    active_low = exact_gelu(pre_act).astype(jnp.bfloat16)
    result = middle + contract(active_low, down_weight)
    return (
        result,
        {
            "unit_two": unit_two,
            "inverse_two": inverse_two,
            "second_low": second_low,
            "pre_act": pre_act,
            "active_low": active_low,
        },
    )


def mlp_backward(grad_result, kept_values, gain_two, up_weight, down_weight):
    grad_branch = grad_result.astype(jnp.bfloat16)
    grad_down = outer_sum(kept_values["active_low"], grad_branch)
    grad_active = contract_back(grad_branch, down_weight)
    grad_pre = gelu_back(kept_values["pre_act"], grad_active).astype(jnp.bfloat16)
    grad_up = outer_sum(kept_values["second_low"], grad_pre)
    grad_second = contract_back(grad_pre, up_weight)
    grad_middle, grad_gain_two = layer_norm_back(
        grad_second,
        kept_values["unit_two"],
        kept_values["inverse_two"],
        gain_two.astype(jnp.float32),
    )
    return (grad_middle + grad_result, grad_gain_two, grad_up, grad_down)


def block_forward(stream, weights, head_count, key_mask):
    gain_one, qkv_weight, out_weight, gain_two, up_weight, down_weight = weights
    normed_one, unit_one, inverse_one = layer_norm(stream, gain_one.astype(jnp.float32))
    normed_low = normed_one.astype(jnp.bfloat16)
    packed = contract(normed_low, qkv_weight).astype(jnp.bfloat16)
    mixed_heads, attn_weights, attn_low = attend(packed, head_count, key_mask)
    middle = stream + contract(mixed_heads, out_weight)
    result, mlp_kept = mlp_forward(middle, gain_two, up_weight, down_weight)
    kept_values = {
        "unit_one": unit_one,
        "inverse_one": inverse_one,
        "normed_low": normed_low,
        "packed": packed,
        "attn_weights": attn_weights,
        "attn_low": attn_low,
        "mixed_heads": mixed_heads,
        "mlp": mlp_kept,
    }
    return (result, kept_values)


def block_backward(grad_result, kept_values, weights, head_count):
    gain_one, qkv_weight, out_weight, gain_two, up_weight, down_weight = weights
    grad_middle, grad_gain_two, grad_up, grad_down = mlp_backward(
        grad_result, kept_values["mlp"], gain_two, up_weight, down_weight
    )
    grad_attend = grad_middle.astype(jnp.bfloat16)
    grad_out = outer_sum(kept_values["mixed_heads"], grad_attend)
    grad_mixed = contract_back(grad_attend, out_weight).astype(jnp.bfloat16)
    grad_packed = attend_back(
        kept_values["packed"],
        kept_values["attn_weights"],
        kept_values["attn_low"],
        grad_mixed,
        head_count,
    )
    grad_qkv = outer_sum(kept_values["normed_low"], grad_packed)
    grad_normed = contract_back(grad_packed, qkv_weight)
    grad_stream, grad_gain_one = layer_norm_back(
        grad_normed,
        kept_values["unit_one"],
        kept_values["inverse_one"],
        gain_one.astype(jnp.float32),
    )
    return (
        grad_stream + grad_middle,
        grad_gain_one,
        grad_qkv,
        grad_out,
        grad_gain_two,
        grad_up,
        grad_down,
    )


def micro_step(
    enc_rows, counts, positions, cot_rows, enc_weights, embed_weight, mask_token, dec_weights
):
    slot_total = enc_rows.shape[1]
    live_slots = jnp.arange(slot_total)[None, :] < counts[:, None]
    encoded, enc_kept = block_forward(enc_rows.astype(jnp.float32), enc_weights, HEADS, live_slots)
    encoded_low = encoded.astype(jnp.bfloat16)
    embedded = contract(encoded_low, embed_weight)
    places = jnp.arange(PATCHES)
    matches = (positions[:, :, None] == places[None, None, :]) & live_slots[:, :, None]
    covered = jnp.any(matches, axis=1)
    slot_index = jnp.sum(jnp.where(matches, jnp.arange(slot_total)[None, :, None], 0), axis=1)
    picked = jnp.take_along_axis(embedded, slot_index[:, :, None], axis=1)
    filled = jnp.where(covered[:, :, None], picked, mask_token.astype(jnp.float32))
    filled = filled + position_table(PATCHES, embedded.shape[-1])
    filled_low = filled.astype(jnp.bfloat16)
    decoded, dec_kept = block_forward(filled_low.astype(jnp.float32), dec_weights, DHEADS, None)
    dec_piece = decoded.astype(jnp.bfloat16)
    dec_back = block_backward(cot_rows.astype(jnp.float32), dec_kept, dec_weights, DHEADS)
    dec_terms = dec_back[1:]
    grad_filled = dec_back[0].astype(jnp.bfloat16).astype(jnp.float32)
    mask_term = jnp.sum(
        jnp.where(covered[:, :, None], 0.0, grad_filled).reshape(-1, grad_filled.shape[-1]), axis=0
    )
    grad_embedded = jnp.take_along_axis(grad_filled, positions[:, :, None], axis=1)
    grad_embedded = jnp.where(live_slots[:, :, None], grad_embedded, 0.0).astype(jnp.bfloat16)
    embed_term = outer_sum(encoded_low, grad_embedded)
    grad_encoded = contract_back(grad_embedded, embed_weight)
    enc_back = block_backward(grad_encoded, enc_kept, enc_weights, HEADS)
    grad_input = enc_back[0]
    enc_terms = enc_back[1:] + (embed_term, mask_term)
    return (dec_piece, grad_input, tuple(enc_terms) + tuple(dec_terms))


def local(
    enc_input,
    keep_count,
    keep_positions,
    enc_gain_one,
    enc_qkv_weight,
    enc_out_weight,
    enc_gain_two,
    enc_up_weight,
    enc_down_weight,
    embed_weight,
    mask_token,
    dec_gain_one,
    dec_qkv_weight,
    dec_out_weight,
    dec_gain_two,
    dec_up_weight,
    dec_down_weight,
    cotangent,
):
    enc_weights = (
        enc_gain_one,
        enc_qkv_weight,
        enc_out_weight,
        enc_gain_two,
        enc_up_weight,
        enc_down_weight,
    )
    dec_weights = (
        dec_gain_one,
        dec_qkv_weight,
        dec_out_weight,
        dec_gain_two,
        dec_up_weight,
        dec_down_weight,
    )
    all_params = (
        enc_gain_one,
        enc_qkv_weight,
        enc_out_weight,
        enc_gain_two,
        enc_up_weight,
        enc_down_weight,
        embed_weight,
        mask_token,
        dec_gain_one,
        dec_qkv_weight,
        dec_out_weight,
        dec_gain_two,
        dec_up_weight,
        dec_down_weight,
    )
    dec_pieces, input_grads, totals = micro_step(
        enc_input, keep_count, keep_positions, cotangent, enc_weights, embed_weight, mask_token, dec_weights
    )
    totals = (
        lax.psum_scatter(totals[0], ("dp", "seq"), scatter_dimension=0, tiled=True),
        lax.psum_scatter(totals[1], ("dp", "seq"), scatter_dimension=0, tiled=True),
        lax.psum_scatter(totals[2], ("dp", "seq"), scatter_dimension=0, tiled=True),
        lax.psum_scatter(totals[3], ("dp", "seq"), scatter_dimension=0, tiled=True),
        lax.psum_scatter(totals[4], ("dp", "seq"), scatter_dimension=0, tiled=True),
        lax.psum_scatter(totals[5], ("dp", "seq"), scatter_dimension=0, tiled=True),
        lax.psum_scatter(totals[6], ("dp", "seq"), scatter_dimension=0, tiled=True),
        lax.psum_scatter(totals[7], ("dp", "seq"), scatter_dimension=0, tiled=True),
        lax.psum_scatter(totals[8], ("dp", "seq"), scatter_dimension=0, tiled=True),
        lax.psum_scatter(totals[9], ("dp", "seq"), scatter_dimension=0, tiled=True),
        lax.psum_scatter(totals[10], ("dp", "seq"), scatter_dimension=0, tiled=True),
        lax.psum_scatter(totals[11], ("dp", "seq"), scatter_dimension=0, tiled=True),
        lax.psum_scatter(totals[12], ("dp", "seq"), scatter_dimension=0, tiled=True),
        lax.psum_scatter(totals[13], ("dp", "seq"), scatter_dimension=0, tiled=True),
    )
    dec_output = dec_pieces.reshape(cotangent.shape)
    enc_input_grad = input_grads.reshape(enc_input.shape)
    return (
        dec_output,
        enc_input_grad,
        totals[0],
        totals[1],
        totals[2],
        totals[3],
        totals[4],
        totals[5],
        totals[6],
        totals[7],
        totals[8],
        totals[9],
        totals[10],
        totals[11],
        totals[12],
        totals[13],
    )


MESH = pl.DeviceIdType.MESH
BF = jnp.bfloat16
F32 = jnp.float32
LANES = 128
TILE = 256
CHUNK = 48
VMEM_BYTES = 62 * 2**20
STEP = 40
FLOWS = ((0, 16, "xyls"), (16, 16, "yxls"), (32, 8, "lsxy"))
COPIES = 4 * len(FLOWS) + 1
SLOTS = 8
LAG = 2
DIMS = "slyx"


def padded(count, multiple):
    return -(-count // multiple) * multiple


def nn(left, right):
    return lax.dot_general(left, right, (((1,), (0,)), ((), ())), preferred_element_type=F32)


def nt(left, right):
    return lax.dot_general(left, right, (((1,), (1,)), ((), ())), preferred_element_type=F32)


def tn(left, right):
    return lax.dot_general(left, right, (((0,), (0,)), ((), ())), preferred_element_type=F32)


def columns(tile):
    return pl.ds(pl.multiple_of(tile * TILE, TILE), TILE)


def each_pair(count, body):
    def both(index):
        body(2 * index)
        body(2 * index + 1)

    each(count // 2, both)
    if count % 2:
        body(count - 1)


def each(count, body):
    lax.fori_loop(0, count, lambda index, carry: (body(index), carry)[1], 0)


def gelu_pair(values):
    reach = jnp.abs(values)
    point = 1.0 / (1.0 + 0.23164189 * reach)
    decay = jnp.exp(-0.5 * values * values)
    tail = 0.5307027145 * point - 0.7265760135
    tail = tail * point + 0.710706870
    tail = tail * point - 0.142248368
    tail = tail * point + 0.127414796
    tail = tail * point * decay
    below = jnp.where(values < 0.0, tail, 1.0 - tail)
    return values * below, below + values * decay * 0.3989422804014327


def as_row(vector):
    return vector[...].astype(F32).reshape(1, vector.shape[0])


def norm_rows(total, source, gain, normed, inverse):
    width = gain.shape[-1]

    def body(chunk):
        rows = pl.ds(pl.multiple_of(chunk * CHUNK, CHUNK), CHUNK)
        stream = source[rows, :].astype(F32)
        centered = stream - jnp.sum(stream, axis=-1, keepdims=True) * (1.0 / width)
        scale = lax.rsqrt(jnp.sum(centered * centered, axis=-1, keepdims=True) * (1.0 / width) + eps)
        inverse[rows, :] = scale
        normed[rows, :] = (centered * scale * gain).astype(BF)

    each_pair(total // CHUNK, body)


def norm_back(total, grad_normed, normed, inverse, gain, added, emit, partial):
    width = gain.shape[-1]
    over = 1.0 / gain
    partial[...] = jnp.zeros_like(partial)

    def body(chunk):
        rows = pl.ds(pl.multiple_of(chunk * CHUNK, CHUNK), CHUNK)
        grad = grad_normed[rows, :]
        unit = normed[rows, :].astype(F32)
        both = grad * unit
        scaled = grad * gain
        first = jnp.sum(scaled, axis=-1, keepdims=True) * (1.0 / width)
        second = jnp.sum(both, axis=-1, keepdims=True) * (1.0 / width)
        emit(rows, inverse[rows, :] * (scaled - first - unit * over * second) + added[rows, :].astype(F32))
        partial[...] += jnp.sum(both.reshape(CHUNK // 8, 8, width), axis=0)

    each_pair(total // CHUNK, body)
    return jnp.sum(partial[...], axis=0, keepdims=True) * over


def head_masks(size):
    lane = lax.broadcasted_iota(jnp.int32, (1, LANES), 1)
    return [((lane >= h * size) & (lane < (h + 1) * size)).astype(F32) for h in range(LANES // size)]


def split_heads(block, masks):
    return jnp.concatenate([block * mask.astype(BF) for mask in masks], axis=0)


def merge_heads(stacked, masks, rows):
    total = stacked[:rows] * masks[0]
    for h in range(1, len(masks)):
        total = total + stacked[h * rows : (h + 1) * rows] * masks[h]
    return total


def attend_block(packed, width, rows, size, image, group, limit, kept, mixed):
    masks = head_masks(size)
    heads = len(masks)
    at = pl.ds(pl.multiple_of(image * rows, 16), rows)
    queries = packed[at, group * LANES : (group + 1) * LANES]
    keys = packed[at, width + group * LANES : width + (group + 1) * LANES]
    values = packed[at, 2 * width + group * LANES : 2 * width + (group + 1) * LANES]
    factor = size**-0.5 * 1.4426950408889634
    if isinstance(limit, int):
        first = limit // 16 * 16
        live = lax.broadcasted_iota(jnp.int32, (rows - first, 1), 0) < limit - first
        total = None
        for head, mask in enumerate(masks):
            scores = nt(keys * mask.astype(BF), queries)
            scores = jnp.concatenate([scores[:first], jnp.where(live, scores[first:], -1e30)], axis=0)
            raised = jnp.exp2((scores - jnp.max(scores, axis=0, keepdims=True)) * factor)
            low = (raised * (1.0 / jnp.sum(raised, axis=0, keepdims=True))).astype(BF)
            kept[image, group, head * rows : (head + 1) * rows, :] = low
            part = tn(low, values * mask.astype(BF))
            total = part if total is None else total + part
        mixed[at, group * LANES : (group + 1) * LANES] = total.astype(BF)
        return
    scores = nt(split_heads(keys, masks), queries).reshape(heads, rows, rows)
    live = lax.broadcasted_iota(jnp.int32, (1, rows, 1), 1) < limit
    scores = jnp.where(live, scores, -1e30)
    raised = jnp.exp2((scores - jnp.max(scores, axis=1, keepdims=True)) * factor)
    weights = raised * (1.0 / jnp.sum(raised, axis=1, keepdims=True))
    low = weights.reshape(heads * rows, rows).astype(BF)
    kept[image, group] = low
    mixed[at, group * LANES : (group + 1) * LANES] = tn(low, split_heads(values, masks)).astype(BF)


def attend_back_block(packed, width, rows, size, image, group, kept, grad_mixed, grad_packed):
    masks = head_masks(size)
    heads = len(masks)
    at = pl.ds(pl.multiple_of(image * rows, 16), rows)
    queries = packed[at, group * LANES : (group + 1) * LANES]
    keys = packed[at, width + group * LANES : width + (group + 1) * LANES]
    values = packed[at, 2 * width + group * LANES : 2 * width + (group + 1) * LANES]
    grad_out = grad_mixed[at, group * LANES : (group + 1) * LANES]
    low = kept[image, group]
    weights = low.astype(F32)
    both = weights * nt(split_heads(values, masks), grad_out)
    inner = jnp.sum(both.reshape(heads, rows, rows), axis=1, keepdims=True)
    grad_scores = both - (weights.reshape(heads, rows, rows) * inner).reshape(heads * rows, rows)
    grad_scores = grad_scores.astype(BF)
    grad_values = merge_heads(nn(low, grad_out), masks, rows)
    grad_keys = merge_heads(nn(grad_scores, queries), masks, rows) * size**-0.5
    flipped = keys.T
    parts = [nn(flipped[h * size : (h + 1) * size], grad_scores[h * rows : (h + 1) * rows]) for h in range(heads)]
    grad_queries = jnp.concatenate(parts, axis=0).T * size**-0.5
    grad_packed[at, group * LANES : (group + 1) * LANES] = grad_queries.astype(BF)
    grad_packed[at, width + group * LANES : width + (group + 1) * LANES] = grad_keys.astype(BF)
    grad_packed[at, 2 * width + group * LANES : 2 * width + (group + 1) * LANES] = grad_values.astype(BF)


def pad_images(source, target, rows):
    images, count = source.shape[0], source.shape[1]
    whole = count // 16 * 16
    for image in range(images):
        target[image * rows + whole : (image + 1) * rows, :] = jnp.zeros((rows - whole, target.shape[1]), target.dtype)
        target[image * rows : image * rows + count, :] = source[image]


def enc_forward_kernel(
    rows, counts, stream, gain_one, gain_two, qkv, out, up, down,
    normed_one_out, inverse_one_out, packed_out, kept_out, mixed_out, normed_two_out, inverse_two_out, active_out, slope_out, encoded_out,
    qkv_in, out_in, up_in, down_in, padded_in, middle,
    normed_one, inverse_one, packed, kept, mixed, normed_two, inverse_two, active, slope, encoded, in_sems, out_sems,
):
    images = stream.shape[0]
    total = images * rows
    width = stream.shape[-1]
    weights = [(qkv, qkv_in), (out, out_in), (up, up_in), (down, down_in)]
    loads = [pltpu.make_async_copy(source, target, in_sems.at[i]) for i, (source, target) in enumerate(weights)]
    for load in loads:
        load.start()
    results = [
        (normed_one, normed_one_out), (inverse_one, inverse_one_out), (packed, packed_out), (kept, kept_out), (mixed, mixed_out),
        (normed_two, normed_two_out), (inverse_two, inverse_two_out), (active, active_out), (slope, slope_out), (encoded, encoded_out),
    ]
    stores = [pltpu.make_async_copy(source, target, out_sems.at[i]) for i, (source, target) in enumerate(results)]
    pad_images(stream, padded_in, rows)
    norm_rows(total, padded_in, as_row(gain_one), normed_one, inverse_one)
    loads[0].wait()

    def project(tile):
        packed[:, columns(tile)] = nn(normed_one[...], qkv_in[:, columns(tile)]).astype(BF)

    each(qkv.shape[1] // TILE, project)
    for store in stores[:3]:
        store.start()

    def mix(image):
        for group in range(width // LANES):
            attend_block(packed, width, rows, width // HEADS, image, group, counts[image], kept, mixed)

    each(images, mix)
    for store in stores[3:5]:
        store.start()
    loads[1].wait()

    def add_out(tile):
        middle[:, columns(tile)] = padded_in[:, columns(tile)].astype(F32) + nn(mixed[...], out_in[:, columns(tile)])

    each(width // TILE, add_out)
    norm_rows(total, middle, as_row(gain_two), normed_two, inverse_two)
    loads[2].wait()
    feed_up(normed_two, up_in, active, slope)
    for store in stores[5:9]:
        store.start()
    loads[3].wait()

    def add_down(tile):
        encoded[:, columns(tile)] = (middle[:, columns(tile)] + nn(active[...], down_in[:, columns(tile)])).astype(BF)

    each(width // TILE, add_down)
    stores[9].start()
    for store in stores:
        store.wait()


def feed_up(normed, up, active, slope):
    def body(tile):
        value, derivative = gelu_pair(nn(normed[...], up[:, columns(tile)]))
        active[:, columns(tile)] = value.astype(BF)
        slope[:, columns(tile)] = derivative.astype(BF)

    each(up.shape[1] // TILE, body)


def feed_back(grad_low, down, slope, grad_pre, loop):
    def body(tile):
        grad = nt(grad_low[...], down[columns(tile), :]) * slope[:, columns(tile)].astype(F32)
        grad_pre[:, columns(tile)] = grad.astype(BF)

    loop(down.shape[0] // TILE, body)


def times_back(grad, matrix, result, loop):
    def body(tile):
        result[:, columns(tile)] = nt(grad[...], matrix[columns(tile), :]).astype(result.dtype)

    loop(matrix.shape[0] // TILE, body)


def one_hot(positions, image, limit, slots, places):
    place = lax.broadcasted_iota(jnp.int32, (places, slots), 0)
    slot = lax.broadcasted_iota(jnp.int32, (places, slots), 1)
    return jnp.where((positions[image : image + 1, :slots] == place) & (slot < limit), 1.0, 0.0)


def coords():
    seq, dp = lax.axis_index("seq"), lax.axis_index("dp")
    return {"s": dp // 4, "l": (dp // 2) % 2, "y": dp % 2, "x": seq // 2, "c": seq % 2}


def partner(here, dim):
    other = dict(here)
    other[dim] = 1 - here[dim]
    return (other["s"] * 4 + other["l"] * 2 + other["y"], other["x"] * 2 + other["c"])


class Reduction:
    def __init__(self, gathered, result, scratch):
        self.gathered, self.result = gathered, result
        self.steps = gathered.shape[1] // STEP
        self.stage, self.land = scratch[0], scratch[1]
        self.lands = [scratch[2 + 4 * f : 6 + 4 * f] for f in range(len(FLOWS))]
        self.send_sem, self.recv_sem, self.load_sem = scratch[-3:]
        self.here = coords()
        self.next, self.ready, self.coming, self.loaded, self.cored = 0, 0, 0, -1, -1
        self.calls, self.idle, self.resting = 0, [], 4 * LAG
        self.pending = []
        self.clock, self.period = 0.0, 4.6

    @staticmethod
    def scratch():
        shapes = [pltpu.VMEM((2, 2, 2, 2, 2, 2, STEP, TILE), F32), pltpu.VMEM((SLOTS, 2, 2, 2, 2, STEP, TILE), F32)]
        for _, rows, _ in FLOWS:
            for k in range(1, 5):
                shapes.append(pltpu.VMEM((SLOTS,) + (2,) * (4 - k) + (rows, TILE), F32))
        return shapes + [pltpu.SemaphoreType.DMA((SLOTS, COPIES)), pltpu.SemaphoreType.DMA((SLOTS, COPIES)), pltpu.SemaphoreType.DMA((2,))]

    def enter(self):
        barrier = pltpu.get_barrier_semaphore()
        for dim in "c" + DIMS:
            pl.semaphore_signal(barrier, inc=1, device_id=partner(self.here, dim), device_id_type=MESH)
        pl.semaphore_wait(barrier, 5)

    def load(self, t):
        rows = pl.ds(pl.multiple_of(t * STEP, 8), STEP)
        whole = self.gathered.reshape(2, 2, 2, 2, 2, self.gathered.shape[1], TILE)
        return pltpu.make_async_copy(whole.at[:, :, :, :, :, rows, :], self.stage.at[lax.rem(t, 2)], self.load_sem.at[lax.rem(t, 2)])

    def core_copy(self, t):
        slot = lax.rem(t, SLOTS)
        return pltpu.make_async_remote_copy(
            src_ref=self.stage.at[lax.rem(t, 2), :, :, :, :, 1 - self.here["c"]],
            dst_ref=self.land.at[slot],
            send_sem=self.send_sem.at[slot, COPIES - 1],
            recv_sem=self.recv_sem.at[slot, COPIES - 1],
            device_id=partner(self.here, "c"),
            device_id_type=MESH,
        )

    def half(self, t, flow, k, kept):
        first, rows, order = FLOWS[flow]
        left = [dim for dim in DIMS if dim not in order[:k]]
        side = self.here[order[k]] if kept else 1 - self.here[order[k]]
        at = (lax.rem(t, SLOTS),) + tuple(side if dim == order[k] else slice(None) for dim in left)
        if k == 0:
            return self.land.at[at + (pl.ds(first, rows),)]
        return self.lands[flow][k - 1].at[at]

    def copy(self, t, flow, k):
        slot = lax.rem(t, SLOTS)
        return pltpu.make_async_remote_copy(
            src_ref=self.half(t, flow, k, False),
            dst_ref=self.lands[flow][k].at[slot],
            send_sem=self.send_sem.at[slot, flow * 4 + k],
            recv_sem=self.recv_sem.at[slot, flow * 4 + k],
            device_id=partner(self.here, FLOWS[flow][2][k]),
            device_id_type=MESH,
        )

    def advance(self, k, t):
        slot = lax.rem(t, SLOTS)
        if k == 1:
            self.core_copy(t).wait()
            self.land[slot] += self.stage[lax.rem(t, 2), :, :, :, :, self.here["c"]]
            for flow in range(len(FLOWS)):
                self.copy(t, flow, 0).start()
            return
        for flow in range(len(FLOWS)):
            self.copy(t, flow, k - 2).wait()
            kept = self.half(t, flow, k - 2, True)
            if k < 5:
                self.lands[flow][k - 2][slot] += kept[...]
                self.copy(t, flow, k - 1).start()
            else:
                first, rows, _ = FLOWS[flow]
                at = pl.ds(pl.multiple_of(t * STEP + first, 8), rows)
                self.result[at, :] = self.lands[flow][3][slot] + kept[...]

    def entry(self, call):
        step, begun = call, call >= 0
        for idle in self.idle:
            step = step - jnp.where(call > idle, 1, 0)
            begun = begun & (call != idle)
        return step, begun

    def carry(self, call):
        for k in range(2, 6):
            t, begun = self.entry(call - LAG * (k - 1))

            @pl.when(begun & (t < self.steps))
            def _():
                self.advance(k, t)

    def call(self, call, fresh):
        t, _ = self.entry(call)

        @pl.when(t < self.steps)
        def _():
            self.advance(1, t)

        @pl.when(t + 1 < fresh)
        def _():
            self.load(t + 1).wait()
            self.core_copy(t + 1).start()

        @pl.when(t + 2 < fresh)
        def _():
            self.load(t + 2).start()

        self.carry(call)

    def settle(self):
        for wait in self.pending:
            wait()
        self.pending = []
        self.ready = self.coming

    def prime(self):
        first, last = self.next, self.ready // STEP - 1
        if first > last:
            return
        if self.cored < first:
            if self.loaded < first:
                self.load(first).start()
                self.loaded = first
            self.load(first).wait()
            self.core_copy(first).start()
            self.cored = first
        if self.loaded < min(first + 1, last):
            self.load(first + 1).start()
            self.loaded = first + 1

    def begun(self, calls):
        fresh = self.ready // STEP
        self.calls += calls
        self.next += calls
        self.cored, self.loaded = min(self.next, fresh - 1), min(self.next + 1, fresh - 1)
        self.resting = 0
        self.clock = 0.0

    def rested(self, calls):
        self.calls += calls
        self.resting += calls
        self.clock = 0.0

    def loop(self, count, body, spent):
        self.settle()
        every = max(1, round(self.period / spent))
        lead = max(1, math.ceil((self.period - self.clock) / spent))
        room = 1 + (count - lead) // every if count >= lead else 0
        start, fresh = self.calls, self.ready // STEP
        calls = min(room, fresh - self.next)
        idle = min(room, 4 * LAG - self.resting) if self.next >= fresh else 0
        spare = self.clock + count * spent
        if calls > 0:
            self.prime()
            step = lambda index: self.call(start + index, fresh)
            self.begun(calls)
        elif idle > 0:
            calls = idle
            self.idle.extend(range(start, start + calls))
            step = lambda index: self.carry(start + index)
            self.rested(calls)
        else:
            each(count, body)
            self.clock = spare
            return
        last = lead - 1 + (calls - 1) * every

        def one(index):
            body(index)

            @pl.when((index >= lead - 1) & (index <= last) & (lax.rem(index - (lead - 1), every) == 0))
            def _():
                step(lax.div(index - (lead - 1), every))

        each(count, one)
        self.clock = (count - 1 - last) * spent

    def tick(self, spent=0.0):
        self.clock += spent
        self.settle()
        last = self.ready // STEP - 1
        if self.next <= last:
            if self.cored < self.next:
                if self.loaded < self.next:
                    self.load(self.next).start()
                    self.loaded = self.next
                    return
                self.prime()
                return
            if self.clock >= self.period:
                self.prime()
                self.call(self.calls, last + 1)
                self.begun(1)
        elif self.resting < 4 * LAG and self.clock >= self.period:
            self.idle.append(self.calls)
            self.carry(self.calls)
            self.rested(1)

    def finish(self, beside):
        self.settle()
        first, fresh, start = self.next, self.ready // STEP, self.calls
        self.prime()

        def one(index):
            self.call(start + index, fresh)
            beside(index)

        each(max(self.steps - first + 4 * LAG, 6), one)

    def send(self, place, sems, tile, rows, count, spent, slots=2):
        self.settle()
        start = self.ready

        def copy(slot, at):
            return pltpu.make_async_copy(place(slot), self.gathered.at[:, pl.ds(at, rows), :], sems.at[slot])

        def body(n):
            slot = lax.rem(n, slots)

            @pl.when(n >= slots)
            def _():
                copy(slot, start).wait()

            place(slot)[...] = tile(n).reshape(32, rows, TILE)
            copy(slot, pl.multiple_of(start + n * rows, 8)).start()

        self.loop(count, body, spent)
        for n in range(max(count - slots, 0), count):
            self.pending.append(functools.partial(lambda slot: copy(slot, start).wait(), n % slots))
        self.coming = start + count * rows


def backward_kernel(
    erows, drows,
    counts, positions, enc_gain_one, enc_gain_two, token, dec_gain_one, dec_gain_two, table, encoded, embed, dec_qkv, dec_out, dec_up, dec_down, cotangent,
    enc_qkv, enc_out, enc_up, enc_down,
    enc_normed_one, enc_inverse_one, enc_packed, enc_kept, enc_mixed, enc_normed_two, enc_inverse_two, enc_active, enc_slope,
    result, input_grad, gathered, reduced, vector_sum,
    padded_positions, grad_embedded, vector_part, vector_land, vector_send, vector_recv, dec_sems, enc_sems, tile_sems, *scratch,
):
    images, places, dwidth = cotangent.shape
    slots, width = input_grad.shape[1:]
    dhidden, hidden = dec_up.shape[1], enc_up.shape[1]
    dtotal, etotal = images * drows, images * erows
    reduction = Reduction(gathered, reduced, scratch)
    mask_token, dec_gain_one, dec_gain_two = as_row(token), as_row(dec_gain_one), as_row(dec_gain_two)
    row = lax.broadcasted_iota(jnp.int32, (drows, 1), 0)
    padded_positions[:images, :slots] = positions[...]
    vector_part[...] = jnp.zeros_like(vector_part)

    def pick_of(image):
        place = lax.broadcasted_iota(jnp.int32, (drows, erows), 0)
        slot = lax.broadcasted_iota(jnp.int32, (drows, erows), 1)
        named = (padded_positions[image : image + 1, :erows] == place) & (slot < counts[image])
        return jnp.where(named, 1.0, 0.0)

    def beside(spent):
        return lambda count, body: reduction.loop(count, body, spent)

    def decoder(
        qkv, out, up, down, filled, normed_one, inverse_one, packed, kept, mixed, middle, normed_two, inverse_two, slope, wide_low, stage
    ):
        into_result = pltpu.make_async_copy(cotangent, result, dec_sems.at[0])
        weights = [(dec_qkv, qkv), (dec_out, out), (dec_up, up), (dec_down, down)]
        loads = [pltpu.make_async_copy(source, target, dec_sems.at[1 + i]) for i, (source, target) in enumerate(weights)]

        def fill(table_in, encoded_in, embed_in):
            starts = [(encoded, encoded_in), (embed, embed_in), (table, table_in)]
            starts = [pltpu.make_async_copy(source, target, dec_sems.at[5 + i]) for i, (source, target) in enumerate(starts)]
            for copy in starts + loads + [into_result]:
                copy.start()
            reduction.enter()
            starts[0].wait()
            starts[1].wait()
            high, rest = mixed, wide_low

            def embed_tile(tile):
                value = nn(encoded_in[...], embed_in[:, columns(tile)])
                top = value.astype(BF)
                high[pl.ds(0, etotal), columns(tile)] = top
                rest[pl.ds(0, etotal), columns(tile)] = (value - top.astype(F32)).astype(BF)

            each(dwidth // TILE, embed_tile)
            starts[2].wait()
            for image in range(images):
                pick = pick_of(image)
                low_pick = pick.astype(BF)
                at = pl.ds(image * erows, erows)
                picked = nn(low_pick, high[at, :]) + nn(low_pick, rest[at, :])
                covered = jnp.sum(pick, axis=1, keepdims=True) > 0.5
                value = jnp.where(covered, picked, mask_token) + table_in[...]
                filled[pl.ds(image * drows, drows), :] = jnp.where(row < places, value, 0.0).astype(BF)

        pl.run_scoped(
            fill, pltpu.VMEM(table.shape, F32), pltpu.VMEM(encoded.shape, BF), pltpu.VMEM(embed.shape, BF)
        )
        norm_rows(dtotal, filled, dec_gain_one, normed_one, inverse_one)
        loads[0].wait()

        def project(tile):
            packed[:, columns(tile)] = nn(normed_one[...], qkv[:, columns(tile)]).astype(BF)

        each(qkv.shape[1] // TILE, project)

        def mix(image):
            for group in range(dwidth // LANES):
                attend_block(packed, dwidth, drows, dwidth // DHEADS, image, group, places, kept, mixed)

        each(images, mix)
        loads[1].wait()

        def add_out(tile):
            middle[:, columns(tile)] = filled[:, columns(tile)].astype(F32) + nn(mixed[...], out[:, columns(tile)])

        each(dwidth // TILE, add_out)
        norm_rows(dtotal, middle, dec_gain_two, normed_two, inverse_two)
        loads[2].wait()
        grad_low = wide_low
        into_result.wait()
        pad_images(result, grad_low, drows)
        block = dwidth // 32

        def place(slot):
            return stage.at[:, pl.ds(pl.multiple_of(slot * block, 8), block), :]

        def feed(active):
            feed_up(normed_two, up, active, slope)
            for tile in range(dwidth // TILE):
                at = slice(tile * TILE, (tile + 1) * TILE)
                reduction.send(lambda slot: stage, tile_sems, lambda n: tn(active[...], grad_low[:, at]), dhidden // 32, 1, 1.9, slots=1)
                if tile == 0:
                    loads[3].wait()
                value = (middle[:, at] + nn(active[...], down[:, at])).astype(BF)
                for image in range(images):
                    result[image, :, at] = value[image * drows : image * drows + places]
                reduction.tick(1.9)
                reduction.tick()
            reduction.settle()

        pl.run_scoped(feed, pltpu.VMEM((dtotal, dhidden), BF))
        reduction.tick()
        feed_back(grad_low, down, slope, slope, beside(0.6))
        reduction.tick()
        half = dhidden // TILE // 2
        for part in range(2):
            reduction.send(place, tile_sems, lambda n: tn(normed_two[...], slope[:, columns(part * half + n)]), block, half, 0.65)
            reduction.tick()
        times_back(slope, up, middle, beside(1.8))
        reduction.tick()
        grad_attend = wide_low

        def keep_middle(at, grad):
            middle[at, :] = grad
            grad_attend[at, :] = grad.astype(BF)

        def late(wide, partial):
            vector_part[0, 4:5, :dwidth] = norm_back(
                dtotal, middle, normed_two, inverse_two, dec_gain_two, grad_low, keep_middle, partial
            )
            reduction.tick(2.2)
            reduction.send(place, tile_sems, lambda n: tn(mixed[...], grad_attend[:, columns(n)]), block, dwidth // TILE, 0.85)
            reduction.tick()
            grad_mixed = normed_two
            times_back(grad_attend, out, grad_mixed, beside(0.8))
            reduction.tick()
            groups = dwidth // LANES // 2
            half = dwidth // TILE // 2
            for part in range(2):
                def mix_back(image):
                    for group in range(part * groups, (part + 1) * groups):
                        attend_back_block(packed, dwidth, drows, dwidth // DHEADS, image, group, kept, grad_mixed, packed)

                reduction.loop(images, mix_back, 1.05)
                reduction.tick()
                tile = lambda n: tn(normed_one[...], packed[:, columns(lax.div(n, half) * 2 * half + part * half + lax.rem(n, half))])
                reduction.send(place, tile_sems, tile, block, 3 * half, 0.65)
                reduction.tick()
            times_back(packed, qkv, wide, beside(1.45))
            reduction.tick()

            def keep_filled(at, grad):
                filled[at, :] = grad.astype(BF)

            vector_part[0, 3:4, :dwidth] = norm_back(
                dtotal, wide, normed_one, inverse_one, dec_gain_one, middle, keep_filled, partial
            )
            reduction.tick(2.2)

        pl.run_scoped(late, pltpu.VMEM((dtotal, dwidth), F32), pltpu.VMEM((8, dwidth), F32))
        token_grad = jnp.zeros((1, dwidth), F32)
        for image in range(images):
            pick = pick_of(image)
            covered = jnp.sum(pick, axis=1, keepdims=True) > 0.5
            grad = filled[pl.ds(image * drows, drows), :]
            token_grad = token_grad + jnp.sum(jnp.where(covered | (row >= places), 0.0, grad.astype(F32)), axis=0, keepdims=True)
            grad_embedded[pl.ds(image * erows, erows), :] = tn(pick.astype(BF), grad).astype(BF)
        vector_part[0, 2:3, :dwidth] = token_grad
        reduction.tick(3.0)

    dgroups, dheads = dwidth // LANES, DHEADS * LANES // dwidth
    wide_shape = (dtotal, dwidth)
    pl.run_scoped(
        decoder,
        *[pltpu.VMEM(ref.shape, BF) for ref in (dec_qkv, dec_out, dec_up, dec_down)],
        pltpu.VMEM(wide_shape, BF), pltpu.VMEM(wide_shape, BF), pltpu.VMEM((dtotal, 1), F32), pltpu.VMEM((dtotal, 3 * dwidth), BF),
        pltpu.VMEM((images, dgroups, dheads * drows, drows), BF), pltpu.VMEM(wide_shape, BF), pltpu.VMEM(wide_shape, F32),
        pltpu.VMEM(wide_shape, BF), pltpu.VMEM((dtotal, 1), F32), pltpu.VMEM((dtotal, dhidden), BF), pltpu.VMEM(wide_shape, BF),
        pltpu.VMEM((32, dhidden // 32, TILE), F32),
    )

    def encoder(
        embed_in, out, weight, down, normed_one, inverse_one, packed, kept, mixed, normed_two, inverse_two, grad_pre,
        grad_low, grad_attend, middle, wide, stage,
    ):
        sources = [
            (embed, embed_in), (enc_down, down), (enc_slope, grad_pre), (enc_normed_two, normed_two), (enc_up, weight),
            (enc_inverse_two, inverse_two), (enc_out, out), (enc_mixed, mixed), (enc_packed, packed), (enc_kept, kept),
            (enc_normed_one, normed_one), (enc_inverse_one, inverse_one),
        ]
        loads = [pltpu.make_async_copy(source, target, enc_sems.at[i]) for i, (source, target) in enumerate(sources)]
        block = width // 32

        def place(slot):
            return stage.at[:, pl.ds(pl.multiple_of(slot * block, 8), block), :]

        def feed(active, encoded_in):
            starts = [(encoded, encoded_in), (enc_active, active)]
            starts = [pltpu.make_async_copy(source, target, enc_sems.at[len(loads) + i]) for i, (source, target) in enumerate(starts)]
            for copy in starts + loads:
                copy.start()
            starts[0].wait()
            reduction.send(place, tile_sems, lambda n: tn(encoded_in[...], grad_embedded[:, columns(n)]), block, dwidth // TILE, 1.0)
            loads[0].wait()
            reduction.tick()
            times_back(grad_embedded, embed_in, wide, beside(0.6))

            def low_chunk(chunk):
                at = pl.ds(pl.multiple_of(chunk * CHUNK, CHUNK), CHUNK)
                grad_low[at, :] = wide[at, :].astype(BF)

            each_pair(etotal // CHUNK, low_chunk)
            reduction.tick(0.4)
            starts[1].wait()
            for tile in range(width // TILE):
                at = slice(tile * TILE, (tile + 1) * TILE)
                reduction.send(lambda slot: stage, tile_sems, lambda n: tn(active[...], grad_low[:, at]), hidden // 32, 1, 1.7, slots=1)
                reduction.tick()
            reduction.settle()

        pl.run_scoped(feed, pltpu.VMEM(enc_active.shape, BF), pltpu.VMEM(encoded.shape, BF))
        reduction.period = 2.9
        reduction.tick()
        loads[1].wait()
        loads[2].wait()
        feed_back(grad_low, down, grad_pre, grad_pre, beside(0.52))
        reduction.tick()
        loads[3].wait()
        reduction.send(place, tile_sems, lambda n: tn(normed_two[...], grad_pre[:, columns(n)]), block, hidden // TILE, 0.58)
        reduction.tick()
        loads[4].wait()
        times_back(grad_pre, weight, middle, beside(1.5))
        reduction.tick()
        into_qkv = pltpu.make_async_copy(enc_qkv, weight.at[:, : enc_qkv.shape[1]], enc_sems.at[len(loads) + 2])
        into_qkv.start()
        loads[5].wait()

        def late(grad_mixed, partial, input_stage):
            def keep_middle(at, grad):
                middle[at, :] = grad
                grad_attend[at, :] = grad.astype(BF)

            vector_part[0, 1:2, :] = norm_back(etotal, middle, normed_two, inverse_two, as_row(enc_gain_two), wide, keep_middle, partial)
            loads[6].wait()
            loads[7].wait()
            reduction.tick(1.5)
            reduction.send(place, tile_sems, lambda n: tn(mixed[...], grad_attend[:, columns(n)]), block, width // TILE, 0.7)
            reduction.tick()
            times_back(grad_attend, out, grad_mixed, beside(0.65))
            for load in loads[8:]:
                load.wait()
            reduction.tick()

            def mix_back(image):
                for group in range(width // LANES):
                    attend_back_block(packed, width, erows, width // HEADS, image, group, kept, grad_mixed, packed)

            reduction.loop(images, mix_back, 1.4)
            reduction.tick()
            reduction.send(place, tile_sems, lambda n: tn(normed_one[...], packed[:, columns(n)]), block, 3 * width // TILE, 0.58)
            reduction.settle()
            left = gathered.shape[1] - reduction.ready
            if left:
                stage[:, :left, :] = jnp.zeros((32, left, TILE), F32)
                rest = pltpu.make_async_copy(
                    stage.at[:, pl.ds(0, left), :], gathered.at[:, pl.ds(reduction.ready, left), :], tile_sems.at[0]
                )
                rest.start()
                reduction.pending.append(rest.wait)
                reduction.coming += left
            into_qkv.wait()
            reduction.tick()
            times_back(packed, weight.at[:, : enc_qkv.shape[1]], wide, beside(1.2))
            reduction.tick()

            def keep_input(at, grad):
                wide[at, :] = grad

            vector_part[0, 0:1, :] = norm_back(etotal, wide, normed_one, inverse_one, as_row(enc_gain_one), middle, keep_input, partial)
            reduction.tick(1.5)
            for image in range(images):
                input_stage[image] = wide[image * erows : image * erows + slots, :]
            store = pltpu.make_async_copy(input_stage, input_grad, tile_sems.at[0])
            store.start()
            reduction.tick(1.5)
            store.wait()

        pl.run_scoped(
            late, pltpu.VMEM((etotal, width), BF), pltpu.VMEM((8, width), F32), pltpu.VMEM(input_grad.shape, F32)
        )

    pl.run_scoped(
        encoder,
        pltpu.VMEM(embed.shape, BF), pltpu.VMEM(enc_out.shape, BF), pltpu.VMEM(enc_up.shape, BF), pltpu.VMEM(enc_down.shape, BF),
        pltpu.VMEM(enc_normed_one.shape, BF), pltpu.VMEM(enc_inverse_one.shape, F32), pltpu.VMEM(enc_packed.shape, BF),
        pltpu.VMEM(enc_kept.shape, BF), pltpu.VMEM(enc_mixed.shape, BF), pltpu.VMEM(enc_normed_two.shape, BF),
        pltpu.VMEM(enc_inverse_two.shape, F32), pltpu.VMEM(enc_slope.shape, BF),
        pltpu.VMEM((etotal, width), BF), pltpu.VMEM((etotal, width), BF), pltpu.VMEM((etotal, width), F32), pltpu.VMEM((etotal, width), F32),
        pltpu.VMEM((32, hidden // 32, TILE), F32),
    )
    order = "c" + DIMS

    def vector_copy(k):
        return pltpu.make_async_remote_copy(
            src_ref=vector_part.at[k],
            dst_ref=vector_land.at[k],
            send_sem=vector_send.at[k],
            recv_sem=vector_recv.at[k],
            device_id=partner(reduction.here, order[k]),
            device_id_type=MESH,
        )

    def vector_step(index):
        for k in range(6):
            @pl.when(index == k)
            def _():
                if k:
                    vector_copy(k - 1).wait()
                    vector_part[k] = vector_part[k - 1] + vector_land[k - 1]
                if k < 5:
                    vector_copy(k).start()

    reduction.finish(vector_step)
    vector_sum[...] = vector_part[5]


def unpack_kernel(halved, source, vector_sum, result_in, grad_in, *targets):
    *targets, result, grad, sems = targets
    matrices, vectors = targets[:9], targets[9:]
    copies = [pltpu.make_async_copy(result_in, result, sems.at[0]), pltpu.make_async_copy(grad_in, grad, sems.at[1])]
    for copy in copies:
        copy.start()
    index = lax.axis_index("dp") * lax.axis_size("seq") + lax.axis_index("seq")
    width = vector_sum.shape[1]
    for row, vector in enumerate(vectors):
        size = vector.shape[0]
        own = pltpu.roll(vector_sum[...], lax.rem(width - index * size, width), 1)
        vector[...] = own[row, :size]
    at = 0
    for index, target in enumerate(matrices):
        block, width = target.shape
        tiles = list(range(width // TILE))
        if index == halved:
            half = len(tiles) // 6
            tiles = [n // half * 2 * half + part * half + n % half for part in range(2) for n in range(3 * half)]
        for n in tiles:
            target[:, n * TILE : (n + 1) * TILE] = source[at : at + block, :]
            at += block
    for copy in copies:
        copy.wait()


def vmem(count):
    return [pl.BlockSpec(memory_space=pltpu.VMEM)] * count


def anywhere(count):
    return [pl.BlockSpec(memory_space=pl.ANY)] * count


def shapes(*pairs):
    return [jax.ShapeDtypeStruct(shape, dtype) for shape, dtype in pairs]


def scratches(*pairs):
    return [pltpu.VMEM(shape, dtype) for shape, dtype in pairs]


def fast_local(
    enc_input, keep_count, keep_positions,
    enc_gain_one, enc_qkv_weight, enc_out_weight, enc_gain_two, enc_up_weight, enc_down_weight,
    embed_weight, mask_token,
    dec_gain_one, dec_qkv_weight, dec_out_weight, dec_gain_two, dec_up_weight, dec_down_weight,
    cotangent,
):
    images, slots, width = enc_input.shape
    places, dwidth = cotangent.shape[1:]
    hidden, dhidden = enc_up_weight.shape[1], dec_up_weight.shape[1]
    erows, drows = padded(slots, 16), padded(places, 16)
    etotal, dtotal = images * erows, images * drows
    egroups, dgroups = width // LANES, dwidth // LANES
    eheads, dheads = HEADS // egroups, DHEADS // dgroups
    smem = [pl.BlockSpec(memory_space=pltpu.SMEM)]
    settings = functools.partial(pltpu.CompilerParams, vmem_limit_bytes=VMEM_BYTES)
    vectors = (enc_gain_one, enc_gain_two, mask_token, dec_gain_one, dec_gain_two)

    saved = shapes(
        ((etotal, width), BF), ((etotal, 1), F32), ((etotal, 3 * width), BF), ((images, egroups, eheads * erows, erows), BF),
        ((etotal, width), BF), ((etotal, width), BF), ((etotal, 1), F32), ((etotal, hidden), BF), ((etotal, hidden), BF), ((etotal, width), BF),
    )
    normed_one, inverse_one, packed, kept, mixed, normed_two, inverse_two, active, slope, encoded = pl.pallas_call(
        functools.partial(enc_forward_kernel, erows),
        name="enc_forward",
        out_shape=saved,
        in_specs=smem + vmem(3) + anywhere(4),
        out_specs=anywhere(10),
        scratch_shapes=scratches(
            *((weight.shape, BF) for weight in (enc_qkv_weight, enc_out_weight, enc_up_weight, enc_down_weight)),
            ((etotal, width), BF), ((etotal, width), F32), *((array.shape, array.dtype) for array in saved),
        ) + [pltpu.SemaphoreType.DMA((4,)), pltpu.SemaphoreType.DMA((10,))],
        compiler_params=settings(),
    )(keep_count, enc_input, enc_gain_one, enc_gain_two, enc_qkv_weight, enc_out_weight, enc_up_weight, enc_down_weight)

    table = jnp.asarray(position_rows(places, dwidth, drows))
    block = dwidth // 32
    eblock = width // 32
    layout = (
        (dhidden // 32, dwidth), (block, dhidden), (block, dwidth), (block, 3 * dwidth), (eblock, dwidth),
        (hidden // 32, width), (eblock, hidden), (eblock, width), (eblock, 3 * width),
    )
    share_rows = padded(sum(rows * columns // TILE for rows, columns in layout), STEP)
    dec_output, input_grad, _, reduced, vector_sum = pl.pallas_call(
        functools.partial(backward_kernel, erows, drows),
        name="backward",
        out_shape=shapes(
            (cotangent.shape, BF), (enc_input.shape, F32), ((32, share_rows, TILE), F32), ((share_rows, TILE), F32), ((8, width), F32),
        ),
        in_specs=smem + vmem(6) + anywhere(21),
        out_specs=vmem(1) + anywhere(2) + vmem(2),
        scratch_shapes=scratches(
            ((8, LANES), jnp.int32), ((etotal, dwidth), BF), ((6, 8, width), F32), ((5, 8, width), F32),
        ) + [pltpu.SemaphoreType.DMA((count,)) for count in (5, 5, 8, 15, 2)] + Reduction.scratch(),
        compiler_params=settings(collective_id=0, has_side_effects=True),
    )(
        keep_count, keep_positions, *vectors, table, encoded, embed_weight, dec_qkv_weight, dec_out_weight, dec_up_weight, dec_down_weight,
        cotangent, enc_qkv_weight, enc_out_weight, enc_up_weight, enc_down_weight,
        normed_one, inverse_one, packed, kept, mixed, normed_two, inverse_two, active, slope,
    )
    dec_down, dec_up, dec_out, dec_qkv, embed, enc_down, enc_up, enc_out, enc_qkv, *cuts, dec_output, input_grad = pl.pallas_call(
        functools.partial(unpack_kernel, 3),
        name="unpack",
        out_shape=shapes(
            *((shape, F32) for shape in layout), *(((vector.shape[0] // 32,), F32) for vector in vectors),
            (cotangent.shape, BF), (enc_input.shape, F32),
        ),
        in_specs=vmem(2) + anywhere(2),
        out_specs=vmem(11 + len(vectors)),
        scratch_shapes=[pltpu.SemaphoreType.DMA((2,))],
    )(reduced, vector_sum, dec_output, input_grad)
    return (
        dec_output, input_grad, cuts[0], enc_qkv, enc_out, cuts[1], enc_up, enc_down, embed, cuts[2],
        cuts[3], dec_qkv, dec_out, cuts[4], dec_up, dec_down,
    )


def position_rows(places, width, rows):
    side = math.isqrt(places)
    quarter = width // 4
    place = np.arange(places)
    rate = 1.0 / 10000.0 ** (np.arange(quarter) / quarter)
    across, down = place[:, None] % side * rate, place[:, None] // side * rate
    table = np.concatenate([np.sin(across), np.cos(across), np.sin(down), np.cos(down)], axis=1)
    return np.pad(table, ((0, rows - places), (0, 0))).astype(np.float32)


def solution(mesh):
    placed = (
        P(("dp", "seq"), None, None),
        P(("dp", "seq")),
        P(("dp", "seq"), None),
        P(),
        P(),
        P(),
        P(),
        P(),
        P(),
        P(),
        P(),
        P(),
        P(),
        P(),
        P(),
        P(),
        P(),
        P(("dp", "seq"), None, None),
    )
    fast = (mesh.shape["dp"], mesh.shape["seq"]) == (8, 4)
    return jax.shard_map(
        fast_local if fast else local,
        mesh=mesh,
        in_specs=placed,
        out_specs=(
            P(("dp", "seq"), None, None),
            P(("dp", "seq"), None, None),
            P(("dp", "seq")),
            P(("dp", "seq"), None),
            P(("dp", "seq"), None),
            P(("dp", "seq")),
            P(("dp", "seq"), None),
            P(("dp", "seq"), None),
            P(("dp", "seq"), None),
            P(("dp", "seq")),
            P(("dp", "seq")),
            P(("dp", "seq"), None),
            P(("dp", "seq"), None),
            P(("dp", "seq")),
            P(("dp", "seq"), None),
            P(("dp", "seq"), None),
        ),
        check_vma=False,
    )
```

```python
import functools
import math

import jax
import jax.numpy as jnp
import numpy as np
from jax import lax
from jax.experimental import pallas as pl
from jax.experimental.pallas import tpu as pltpu
from jax.sharding import PartitionSpec as P

HEADS = 12
DHEADS = 16
PATCHES = 196


eps = 1e-06


def position_table(count, model_width):
    grid_side = math.isqrt(count)
    quarter = model_width // 4
    places = jnp.arange(count)
    across = (places % grid_side).astype(jnp.float32)
    row_place = (places // grid_side).astype(jnp.float32)
    frequency = 1.0 / 10000.0 ** (jnp.arange(quarter).astype(jnp.float32) / quarter)
    return jnp.concatenate(
        [
            jnp.sin(across[:, None] * frequency),
            jnp.cos(across[:, None] * frequency),
            jnp.sin(row_place[:, None] * frequency),
            jnp.cos(row_place[:, None] * frequency),
        ],
        axis=1,
    )


def contract(operand, matrix):
    return jnp.einsum("...i,ij->...j", operand, matrix, preferred_element_type=jnp.float32)


def contract_back(gradient, matrix):
    return jnp.einsum("...j,ij->...i", gradient, matrix, preferred_element_type=jnp.float32)


def outer_sum(operand, gradient):
    flat_left = operand.reshape(-1, operand.shape[-1])
    flat_right = gradient.reshape(-1, gradient.shape[-1])
    return lax.dot_general(
        flat_left, flat_right, (((0,), (0,)), ((), ())), preferred_element_type=jnp.float32
    )


def exact_gelu(values):
    return jax.nn.gelu(values, approximate=False)


def gelu_back(pre_act, grad_active):
    unused, pullback = jax.vjp(exact_gelu, pre_act)
    return pullback(grad_active)[0]


def layer_norm(stream, gain_vec):
    row_mean = jnp.mean(stream, axis=-1, keepdims=True)
    centered = stream - row_mean
    inverse = lax.rsqrt(jnp.mean(centered * centered, axis=-1, keepdims=True) + eps)
    unit_rows = centered * inverse
    return (unit_rows * gain_vec, unit_rows, inverse)


def layer_norm_back(grad_normed, unit_rows, inverse, gain_vec):
    grad_gain = jnp.sum((grad_normed * unit_rows).reshape(-1, unit_rows.shape[-1]), axis=0)
    grad_unit = grad_normed * gain_vec
    grad_stream = inverse * (
        grad_unit
        - jnp.mean(grad_unit, axis=-1, keepdims=True)
        - unit_rows * jnp.mean(grad_unit * unit_rows, axis=-1, keepdims=True)
    )
    return (grad_stream, grad_gain)


def attend(packed, head_count, key_mask):
    batch_size, row_count, triple_width = packed.shape
    model_width = triple_width // 3
    head_size = model_width // head_count
    queries = packed[:, :, :model_width].reshape(batch_size, row_count, head_count, head_size)
    key_heads = packed[:, :, model_width : 2 * model_width].reshape(
        batch_size, row_count, head_count, head_size
    )
    value_heads = packed[:, :, 2 * model_width :].reshape(
        batch_size, row_count, head_count, head_size
    )
    scores = jnp.einsum(
        "bqhd,bkhd->bhqk", queries, key_heads, preferred_element_type=jnp.float32
    ) * head_size ** (-0.5)
    if key_mask is not None:
        scores = jnp.where(key_mask[:, None, None, :], scores, -1e30)
    row_max = jnp.max(scores, axis=-1, keepdims=True)
    raised = jnp.exp(scores - row_max)
    attn_weights = raised / jnp.sum(raised, axis=-1, keepdims=True)
    attn_low = attn_weights.astype(jnp.bfloat16)
    mixed_heads = jnp.einsum(
        "bhqk,bkhd->bqhd", attn_low, value_heads, preferred_element_type=jnp.float32
    )
    mixed_heads = mixed_heads.reshape(batch_size, row_count, model_width).astype(jnp.bfloat16)
    return (mixed_heads, attn_weights, attn_low)


def attend_back(packed, attn_weights, attn_low, grad_mixed, head_count):
    batch_size, row_count, triple_width = packed.shape
    model_width = triple_width // 3
    head_size = model_width // head_count
    factor = head_size ** (-0.5)
    queries = packed[:, :, :model_width].reshape(batch_size, row_count, head_count, head_size)
    key_heads = packed[:, :, model_width : 2 * model_width].reshape(
        batch_size, row_count, head_count, head_size
    )
    value_heads = packed[:, :, 2 * model_width :].reshape(
        batch_size, row_count, head_count, head_size
    )
    grad_heads = grad_mixed.reshape(batch_size, row_count, head_count, head_size)
    grad_values = jnp.einsum(
        "bhqk,bqhd->bkhd", attn_low, grad_heads, preferred_element_type=jnp.float32
    )
    grad_attn = jnp.einsum(
        "bqhd,bkhd->bhqk", grad_heads, value_heads, preferred_element_type=jnp.float32
    )
    grad_scores = attn_weights * (
        grad_attn - jnp.sum(attn_weights * grad_attn, axis=-1, keepdims=True)
    )
    grad_scores = grad_scores.astype(jnp.bfloat16)
    grad_queries = (
        jnp.einsum("bhqk,bkhd->bqhd", grad_scores, key_heads, preferred_element_type=jnp.float32)
        * factor
    )
    grad_keys = (
        jnp.einsum("bhqk,bqhd->bkhd", grad_scores, queries, preferred_element_type=jnp.float32)
        * factor
    )
    grad_packed = jnp.concatenate(
        [
            grad_queries.reshape(batch_size, row_count, model_width),
            grad_keys.reshape(batch_size, row_count, model_width),
            grad_values.reshape(batch_size, row_count, model_width),
        ],
        axis=-1,
    )
    return grad_packed.astype(jnp.bfloat16)


def mlp_forward(middle, gain_two, up_weight, down_weight):
    normed_two, unit_two, inverse_two = layer_norm(middle, gain_two.astype(jnp.float32))
    second_low = normed_two.astype(jnp.bfloat16)
    pre_act = contract(second_low, up_weight)
    active_low = exact_gelu(pre_act).astype(jnp.bfloat16)
    result = middle + contract(active_low, down_weight)
    return (
        result,
        {
            "unit_two": unit_two,
            "inverse_two": inverse_two,
            "second_low": second_low,
            "pre_act": pre_act,
            "active_low": active_low,
        },
    )


def mlp_backward(grad_result, kept_values, gain_two, up_weight, down_weight):
    grad_branch = grad_result.astype(jnp.bfloat16)
    grad_down = outer_sum(kept_values["active_low"], grad_branch)
    grad_active = contract_back(grad_branch, down_weight)
    grad_pre = gelu_back(kept_values["pre_act"], grad_active).astype(jnp.bfloat16)
    grad_up = outer_sum(kept_values["second_low"], grad_pre)
    grad_second = contract_back(grad_pre, up_weight)
    grad_middle, grad_gain_two = layer_norm_back(
        grad_second,
        kept_values["unit_two"],
        kept_values["inverse_two"],
        gain_two.astype(jnp.float32),
    )
    return (grad_middle + grad_result, grad_gain_two, grad_up, grad_down)


def block_forward(stream, weights, head_count, key_mask):
    gain_one, qkv_weight, out_weight, gain_two, up_weight, down_weight = weights
    normed_one, unit_one, inverse_one = layer_norm(stream, gain_one.astype(jnp.float32))
    normed_low = normed_one.astype(jnp.bfloat16)
    packed = contract(normed_low, qkv_weight).astype(jnp.bfloat16)
    mixed_heads, attn_weights, attn_low = attend(packed, head_count, key_mask)
    middle = stream + contract(mixed_heads, out_weight)
    result, mlp_kept = mlp_forward(middle, gain_two, up_weight, down_weight)
    kept_values = {
        "unit_one": unit_one,
        "inverse_one": inverse_one,
        "normed_low": normed_low,
        "packed": packed,
        "attn_weights": attn_weights,
        "attn_low": attn_low,
        "mixed_heads": mixed_heads,
        "mlp": mlp_kept,
    }
    return (result, kept_values)


def block_backward(grad_result, kept_values, weights, head_count):
    gain_one, qkv_weight, out_weight, gain_two, up_weight, down_weight = weights
    grad_middle, grad_gain_two, grad_up, grad_down = mlp_backward(
        grad_result, kept_values["mlp"], gain_two, up_weight, down_weight
    )
    grad_attend = grad_middle.astype(jnp.bfloat16)
    grad_out = outer_sum(kept_values["mixed_heads"], grad_attend)
    grad_mixed = contract_back(grad_attend, out_weight).astype(jnp.bfloat16)
    grad_packed = attend_back(
        kept_values["packed"],
        kept_values["attn_weights"],
        kept_values["attn_low"],
        grad_mixed,
        head_count,
    )
    grad_qkv = outer_sum(kept_values["normed_low"], grad_packed)
    grad_normed = contract_back(grad_packed, qkv_weight)
    grad_stream, grad_gain_one = layer_norm_back(
        grad_normed,
        kept_values["unit_one"],
        kept_values["inverse_one"],
        gain_one.astype(jnp.float32),
    )
    return (
        grad_stream + grad_middle,
        grad_gain_one,
        grad_qkv,
        grad_out,
        grad_gain_two,
        grad_up,
        grad_down,
    )


def micro_step(
    enc_rows, counts, positions, cot_rows, enc_weights, embed_weight, mask_token, dec_weights
):
    slot_total = enc_rows.shape[1]
    live_slots = jnp.arange(slot_total)[None, :] < counts[:, None]
    encoded, enc_kept = block_forward(enc_rows.astype(jnp.float32), enc_weights, HEADS, live_slots)
    encoded_low = encoded.astype(jnp.bfloat16)
    embedded = contract(encoded_low, embed_weight)
    places = jnp.arange(PATCHES)
    matches = (positions[:, :, None] == places[None, None, :]) & live_slots[:, :, None]
    covered = jnp.any(matches, axis=1)
    slot_index = jnp.sum(jnp.where(matches, jnp.arange(slot_total)[None, :, None], 0), axis=1)
    picked = jnp.take_along_axis(embedded, slot_index[:, :, None], axis=1)
    filled = jnp.where(covered[:, :, None], picked, mask_token.astype(jnp.float32))
    filled = filled + position_table(PATCHES, embedded.shape[-1])
    filled_low = filled.astype(jnp.bfloat16)
    decoded, dec_kept = block_forward(filled_low.astype(jnp.float32), dec_weights, DHEADS, None)
    dec_piece = decoded.astype(jnp.bfloat16)
    dec_back = block_backward(cot_rows.astype(jnp.float32), dec_kept, dec_weights, DHEADS)
    dec_terms = dec_back[1:]
    grad_filled = dec_back[0].astype(jnp.bfloat16).astype(jnp.float32)
    mask_term = jnp.sum(
        jnp.where(covered[:, :, None], 0.0, grad_filled).reshape(-1, grad_filled.shape[-1]), axis=0
    )
    grad_embedded = jnp.take_along_axis(grad_filled, positions[:, :, None], axis=1)
    grad_embedded = jnp.where(live_slots[:, :, None], grad_embedded, 0.0).astype(jnp.bfloat16)
    embed_term = outer_sum(encoded_low, grad_embedded)
    grad_encoded = contract_back(grad_embedded, embed_weight)
    enc_back = block_backward(grad_encoded, enc_kept, enc_weights, HEADS)
    grad_input = enc_back[0]
    enc_terms = enc_back[1:] + (embed_term, mask_term)
    return (dec_piece, grad_input, tuple(enc_terms) + tuple(dec_terms))


def local(
    enc_input,
    keep_count,
    keep_positions,
    enc_gain_one,
    enc_qkv_weight,
    enc_out_weight,
    enc_gain_two,
    enc_up_weight,
    enc_down_weight,
    embed_weight,
    mask_token,
    dec_gain_one,
    dec_qkv_weight,
    dec_out_weight,
    dec_gain_two,
    dec_up_weight,
    dec_down_weight,
    cotangent,
):
    enc_weights = (
        enc_gain_one,
        enc_qkv_weight,
        enc_out_weight,
        enc_gain_two,
        enc_up_weight,
        enc_down_weight,
    )
    dec_weights = (
        dec_gain_one,
        dec_qkv_weight,
        dec_out_weight,
        dec_gain_two,
        dec_up_weight,
        dec_down_weight,
    )
    all_params = (
        enc_gain_one,
        enc_qkv_weight,
        enc_out_weight,
        enc_gain_two,
        enc_up_weight,
        enc_down_weight,
        embed_weight,
        mask_token,
        dec_gain_one,
        dec_qkv_weight,
        dec_out_weight,
        dec_gain_two,
        dec_up_weight,
        dec_down_weight,
    )
    dec_pieces, input_grads, totals = micro_step(
        enc_input, keep_count, keep_positions, cotangent, enc_weights, embed_weight, mask_token, dec_weights
    )
    totals = (
        lax.psum_scatter(totals[0], ("dp", "seq"), scatter_dimension=0, tiled=True),
        lax.psum_scatter(totals[1], ("dp", "seq"), scatter_dimension=0, tiled=True),
        lax.psum_scatter(totals[2], ("dp", "seq"), scatter_dimension=0, tiled=True),
        lax.psum_scatter(totals[3], ("dp", "seq"), scatter_dimension=0, tiled=True),
        lax.psum_scatter(totals[4], ("dp", "seq"), scatter_dimension=0, tiled=True),
        lax.psum_scatter(totals[5], ("dp", "seq"), scatter_dimension=0, tiled=True),
        lax.psum_scatter(totals[6], ("dp", "seq"), scatter_dimension=0, tiled=True),
        lax.psum_scatter(totals[7], ("dp", "seq"), scatter_dimension=0, tiled=True),
        lax.psum_scatter(totals[8], ("dp", "seq"), scatter_dimension=0, tiled=True),
        lax.psum_scatter(totals[9], ("dp", "seq"), scatter_dimension=0, tiled=True),
        lax.psum_scatter(totals[10], ("dp", "seq"), scatter_dimension=0, tiled=True),
        lax.psum_scatter(totals[11], ("dp", "seq"), scatter_dimension=0, tiled=True),
        lax.psum_scatter(totals[12], ("dp", "seq"), scatter_dimension=0, tiled=True),
        lax.psum_scatter(totals[13], ("dp", "seq"), scatter_dimension=0, tiled=True),
    )
    dec_output = dec_pieces.reshape(cotangent.shape)
    enc_input_grad = input_grads.reshape(enc_input.shape)
    return (
        dec_output,
        enc_input_grad,
        totals[0],
        totals[1],
        totals[2],
        totals[3],
        totals[4],
        totals[5],
        totals[6],
        totals[7],
        totals[8],
        totals[9],
        totals[10],
        totals[11],
        totals[12],
        totals[13],
    )


MESH = pl.DeviceIdType.MESH
BF = jnp.bfloat16
F32 = jnp.float32
LANES = 128
TILE = 256
CHUNK = 48
VMEM_BYTES = 62 * 2**20
STEP = 40
FLOWS = ((0, 16, "xyls"), (16, 16, "yxls"), (32, 8, "lsxy"))
COPIES = 4 * len(FLOWS) + 1
SLOTS = 8
LAG = 2
DIMS = "slyx"


def padded(count, multiple):
    return -(-count // multiple) * multiple


def nn(left, right):
    return lax.dot_general(left, right, (((1,), (0,)), ((), ())), preferred_element_type=F32)


def nt(left, right):
    return lax.dot_general(left, right, (((1,), (1,)), ((), ())), preferred_element_type=F32)


def tn(left, right):
    return lax.dot_general(left, right, (((0,), (0,)), ((), ())), preferred_element_type=F32)


def columns(tile):
    return pl.ds(pl.multiple_of(tile * TILE, TILE), TILE)


def wide_of(rows, count):
    return next(wide for wide in ((768, 512, TILE) if rows < 1000 else (512, TILE)) if count % wide == 0)


def span(tile, wide):
    return pl.ds(pl.multiple_of(tile * wide, wide), wide)


def each_pair(count, body):
    def both(index):
        body(2 * index)
        body(2 * index + 1)

    each(count // 2, both)
    if count % 2:
        body(count - 1)


def each(count, body):
    lax.fori_loop(0, count, lambda index, carry: (body(index), carry)[1], 0)


def gelu_pair(values):
    reach = jnp.abs(values)
    point = 1.0 / (1.0 + 0.23164189 * reach)
    decay = jnp.exp(-0.5 * values * values)
    tail = 0.5307027145 * point - 0.7265760135
    tail = tail * point + 0.710706870
    tail = tail * point - 0.142248368
    tail = tail * point + 0.127414796
    tail = tail * point * decay
    below = jnp.where(values < 0.0, tail, 1.0 - tail)
    return values * below, below + values * decay * 0.3989422804014327


def as_row(vector):
    return vector[...].astype(F32).reshape(1, vector.shape[0])


def norm_rows(total, source, gain, normed, inverse):
    width = gain.shape[-1]

    def body(chunk):
        rows = pl.ds(pl.multiple_of(chunk * CHUNK, CHUNK), CHUNK)
        stream = source[rows, :].astype(F32)
        centered = stream - jnp.sum(stream, axis=-1, keepdims=True) * (1.0 / width)
        scale = lax.rsqrt(jnp.sum(centered * centered, axis=-1, keepdims=True) * (1.0 / width) + eps)
        inverse[rows, :] = scale
        normed[rows, :] = (centered * scale * gain).astype(BF)

    each_pair(total // CHUNK, body)


def norm_back(total, grad_normed, normed, inverse, gain, added, emit, partial):
    width = gain.shape[-1]
    over = 1.0 / gain
    partial[...] = jnp.zeros_like(partial)

    def body(chunk):
        rows = pl.ds(pl.multiple_of(chunk * CHUNK, CHUNK), CHUNK)
        grad = grad_normed[rows, :]
        unit = normed[rows, :].astype(F32)
        both = grad * unit
        scaled = grad * gain
        first = jnp.sum(scaled, axis=-1, keepdims=True) * (1.0 / width)
        second = jnp.sum(both, axis=-1, keepdims=True) * (1.0 / width)
        emit(rows, inverse[rows, :] * (scaled - first - unit * over * second) + added[rows, :].astype(F32))
        partial[...] += jnp.sum(both.reshape(CHUNK // 8, 8, width), axis=0)

    each_pair(total // CHUNK, body)
    return jnp.sum(partial[...], axis=0, keepdims=True) * over


def head_masks(size):
    lane = lax.broadcasted_iota(jnp.int32, (1, LANES), 1)
    return [((lane >= h * size) & (lane < (h + 1) * size)).astype(F32) for h in range(LANES // size)]


def split_heads(block, masks):
    return jnp.concatenate([block * mask.astype(BF) for mask in masks], axis=0)


def merge_heads(stacked, masks, rows):
    total = stacked[:rows] * masks[0]
    for h in range(1, len(masks)):
        total = total + stacked[h * rows : (h + 1) * rows] * masks[h]
    return total


def attend_block(packed, width, rows, size, image, group, limit, kept, mixed):
    masks = head_masks(size)
    heads = len(masks)
    at = pl.ds(pl.multiple_of(image * rows, 16), rows)
    queries = packed[at, group * LANES : (group + 1) * LANES]
    keys = packed[at, width + group * LANES : width + (group + 1) * LANES]
    values = packed[at, 2 * width + group * LANES : 2 * width + (group + 1) * LANES]
    factor = size**-0.5 * 1.4426950408889634
    if isinstance(limit, int):
        first = limit // 16 * 16
        live = lax.broadcasted_iota(jnp.int32, (rows - first, 1), 0) < limit - first
        total = None
        for head, mask in enumerate(masks):
            scores = nt(keys * mask.astype(BF), queries)
            scores = jnp.concatenate([scores[:first], jnp.where(live, scores[first:], -1e30)], axis=0)
            raised = jnp.exp2((scores - jnp.max(scores, axis=0, keepdims=True)) * factor)
            low = (raised * (1.0 / jnp.sum(raised, axis=0, keepdims=True))).astype(BF)
            kept[image, group, head * rows : (head + 1) * rows, :] = low
            part = tn(low, values * mask.astype(BF))
            total = part if total is None else total + part
        mixed[at, group * LANES : (group + 1) * LANES] = total.astype(BF)
        return
    scores = nt(split_heads(keys, masks), queries).reshape(heads, rows, rows)
    live = lax.broadcasted_iota(jnp.int32, (1, rows, 1), 1) < limit
    scores = jnp.where(live, scores, -1e30)
    raised = jnp.exp2((scores - jnp.max(scores, axis=1, keepdims=True)) * factor)
    weights = raised * (1.0 / jnp.sum(raised, axis=1, keepdims=True))
    low = weights.reshape(heads * rows, rows).astype(BF)
    kept[image, group] = low
    mixed[at, group * LANES : (group + 1) * LANES] = tn(low, split_heads(values, masks)).astype(BF)


def attend_back_block(packed, width, rows, size, image, group, kept, grad_mixed, grad_packed):
    masks = head_masks(size)
    heads = len(masks)
    at = pl.ds(pl.multiple_of(image * rows, 16), rows)
    queries = packed[at, group * LANES : (group + 1) * LANES]
    keys = packed[at, width + group * LANES : width + (group + 1) * LANES]
    values = packed[at, 2 * width + group * LANES : 2 * width + (group + 1) * LANES]
    grad_out = grad_mixed[at, group * LANES : (group + 1) * LANES]
    low = kept[image, group]
    weights = low.astype(F32)
    both = weights * nt(split_heads(values, masks), grad_out)
    inner = jnp.sum(both.reshape(heads, rows, rows), axis=1, keepdims=True)
    grad_scores = both - (weights.reshape(heads, rows, rows) * inner).reshape(heads * rows, rows)
    grad_scores = grad_scores.astype(BF)
    grad_values = merge_heads(nn(low, grad_out), masks, rows)
    grad_keys = merge_heads(nn(grad_scores, queries), masks, rows) * size**-0.5
    flipped = keys.T
    parts = [nn(flipped[h * size : (h + 1) * size], grad_scores[h * rows : (h + 1) * rows]) for h in range(heads)]
    grad_queries = jnp.concatenate(parts, axis=0).T * size**-0.5
    grad_packed[at, group * LANES : (group + 1) * LANES] = grad_queries.astype(BF)
    grad_packed[at, width + group * LANES : width + (group + 1) * LANES] = grad_keys.astype(BF)
    grad_packed[at, 2 * width + group * LANES : 2 * width + (group + 1) * LANES] = grad_values.astype(BF)


def pad_images(source, target, rows):
    images, count = source.shape[0], source.shape[1]
    whole = count // 16 * 16
    for image in range(images):
        target[image * rows + whole : (image + 1) * rows, :] = jnp.zeros((rows - whole, target.shape[1]), target.dtype)
        target[image * rows : image * rows + count, :] = source[image]


def enc_forward_kernel(
    rows, counts, stream, gain_one, gain_two, qkv, out, up, down,
    normed_one_out, inverse_one_out, packed_out, kept_out, mixed_out, normed_two_out, inverse_two_out, active_out, slope_out, encoded_out,
    qkv_in, out_in, up_in, down_in, padded_in, middle,
    normed_one, inverse_one, packed, kept, mixed, normed_two, inverse_two, active, slope, encoded, in_sems, out_sems,
):
    images = stream.shape[0]
    total = images * rows
    width = stream.shape[-1]
    weights = [(qkv, qkv_in), (out, out_in), (up, up_in), (down, down_in)]
    loads = [pltpu.make_async_copy(source, target, in_sems.at[i]) for i, (source, target) in enumerate(weights)]
    for load in loads:
        load.start()
    results = [
        (normed_one, normed_one_out), (inverse_one, inverse_one_out), (packed, packed_out), (kept, kept_out), (mixed, mixed_out),
        (normed_two, normed_two_out), (inverse_two, inverse_two_out), (active, active_out), (slope, slope_out), (encoded, encoded_out),
    ]
    stores = [pltpu.make_async_copy(source, target, out_sems.at[i]) for i, (source, target) in enumerate(results)]
    pad_images(stream, padded_in, rows)
    norm_rows(total, padded_in, as_row(gain_one), normed_one, inverse_one)
    loads[0].wait()

    project(normed_one, qkv_in, packed)
    for store in stores[:3]:
        store.start()

    def mix(image):
        for group in range(width // LANES):
            attend_block(packed, width, rows, width // HEADS, image, group, counts[image], kept, mixed)

    each(images, mix)
    for store in stores[3:5]:
        store.start()
    loads[1].wait()

    middle[...] = padded_in[...].astype(F32) + nn(mixed[...], out_in[...])
    norm_rows(total, middle, as_row(gain_two), normed_two, inverse_two)
    loads[2].wait()
    feed_up(normed_two, up_in, active, slope)
    for store in stores[5:9]:
        store.start()
    loads[3].wait()

    encoded[...] = (middle[...] + nn(active[...], down_in[...])).astype(BF)
    stores[9].start()
    for store in stores:
        store.wait()


def project(normed, weight, packed):
    wide = wide_of(normed.shape[0], weight.shape[1])

    def body(tile):
        packed[:, span(tile, wide)] = nn(normed[...], weight[:, span(tile, wide)]).astype(BF)

    each(weight.shape[1] // wide, body)


def feed_up(normed, up, active, slope):
    wide = wide_of(normed.shape[0], up.shape[1])

    def body(tile):
        value, derivative = gelu_pair(nn(normed[...], up[:, span(tile, wide)]))
        active[:, span(tile, wide)] = value.astype(BF)
        slope[:, span(tile, wide)] = derivative.astype(BF)

    each(up.shape[1] // wide, body)


def feed_back(grad_low, down, slope, grad_pre, beside, spent):
    wide = wide_of(grad_low.shape[0], down.shape[0])
    count = down.shape[0] // wide

    def body(tile):
        grad = nt(grad_low[...], down[span(tile, wide), :]) * slope[:, span(tile, wide)].astype(F32)
        grad_pre[:, span(tile, wide)] = grad.astype(BF)

    beside(count, body, spent / count)


def times_back(grad, matrix, result, beside, spent):
    wide = wide_of(grad.shape[0], matrix.shape[0])
    count = matrix.shape[0] // wide

    def body(tile):
        result[:, span(tile, wide)] = nt(grad[...], matrix[span(tile, wide), :]).astype(result.dtype)

    beside(count, body, spent / count)


def one_hot(positions, image, limit, slots, places):
    place = lax.broadcasted_iota(jnp.int32, (places, slots), 0)
    slot = lax.broadcasted_iota(jnp.int32, (places, slots), 1)
    return jnp.where((positions[image : image + 1, :slots] == place) & (slot < limit), 1.0, 0.0)


def coords():
    seq, dp = lax.axis_index("seq"), lax.axis_index("dp")
    return {"s": dp // 4, "l": (dp // 2) % 2, "y": dp % 2, "x": seq // 2, "c": seq % 2}


def partner(here, dim):
    other = dict(here)
    other[dim] = 1 - here[dim]
    return (other["s"] * 4 + other["l"] * 2 + other["y"], other["x"] * 2 + other["c"])


class Reduction:
    def __init__(self, gathered, result, scratch, used):
        self.gathered, self.result = gathered, result
        self.steps = gathered.shape[1] // STEP
        self.tail = used - (self.steps - 1) * STEP
        self.stage, self.land = scratch[0], scratch[1]
        self.lands = [scratch[2 + 4 * f : 6 + 4 * f] for f in range(len(FLOWS))]
        self.send_sem, self.recv_sem, self.load_sem = scratch[-3:]
        self.here = coords()
        self.next, self.ready, self.coming, self.loaded, self.cored = 0, 0, 0, -1, -1
        self.calls, self.idle, self.resting = 0, [], 4 * LAG
        self.pending = []
        self.clock, self.period = 0.0, 3.4

    @staticmethod
    def scratch():
        shapes = [pltpu.VMEM((2, 2, 2, 2, 2, 2, STEP, TILE), F32), pltpu.VMEM((SLOTS, 2, 2, 2, 2, STEP, TILE), F32)]
        for _, rows, _ in FLOWS:
            for k in range(1, 5):
                shapes.append(pltpu.VMEM((SLOTS,) + (2,) * (4 - k) + (rows, TILE), F32))
        return shapes + [pltpu.SemaphoreType.DMA((SLOTS, COPIES)), pltpu.SemaphoreType.DMA((SLOTS, COPIES)), pltpu.SemaphoreType.DMA((2,))]

    def enter(self):
        barrier = pltpu.get_barrier_semaphore()
        for dim in "c" + DIMS:
            pl.semaphore_signal(barrier, inc=1, device_id=partner(self.here, dim), device_id_type=MESH)
        pl.semaphore_wait(barrier, 5)

    def load(self, t):
        rows = pl.ds(pl.multiple_of(t * STEP, 8), STEP)
        whole = self.gathered.reshape(2, 2, 2, 2, 2, self.gathered.shape[1], TILE)
        return pltpu.make_async_copy(whole.at[:, :, :, :, :, rows, :], self.stage.at[lax.rem(t, 2)], self.load_sem.at[lax.rem(t, 2)])

    def core_copy(self, t):
        slot = lax.rem(t, SLOTS)
        return pltpu.make_async_remote_copy(
            src_ref=self.stage.at[lax.rem(t, 2), :, :, :, :, 1 - self.here["c"]],
            dst_ref=self.land.at[slot],
            send_sem=self.send_sem.at[slot, COPIES - 1],
            recv_sem=self.recv_sem.at[slot, COPIES - 1],
            device_id=partner(self.here, "c"),
            device_id_type=MESH,
        )

    def half(self, t, flow, k, kept):
        first, rows, order = FLOWS[flow]
        left = [dim for dim in DIMS if dim not in order[:k]]
        side = self.here[order[k]] if kept else 1 - self.here[order[k]]
        at = (lax.rem(t, SLOTS),) + tuple(side if dim == order[k] else slice(None) for dim in left)
        if k == 0:
            return self.land.at[at + (pl.ds(first, rows),)]
        return self.lands[flow][k - 1].at[at]

    def copy(self, t, flow, k):
        slot = lax.rem(t, SLOTS)
        return pltpu.make_async_remote_copy(
            src_ref=self.half(t, flow, k, False),
            dst_ref=self.lands[flow][k].at[slot],
            send_sem=self.send_sem.at[slot, flow * 4 + k],
            recv_sem=self.recv_sem.at[slot, flow * 4 + k],
            device_id=partner(self.here, FLOWS[flow][2][k]),
            device_id_type=MESH,
        )

    def advance(self, k, t):
        slot = lax.rem(t, SLOTS)
        if k == 1:
            self.core_copy(t).wait()
            self.land[slot] += self.stage[lax.rem(t, 2), :, :, :, :, self.here["c"]]
        always = [flow for flow in range(len(FLOWS)) if FLOWS[flow][0] < self.tail]
        others = [flow for flow in range(len(FLOWS)) if FLOWS[flow][0] >= self.tail]
        self.exchange(k, t, slot, always)
        if others:
            @pl.when(t < self.steps - 1)
            def _():
                self.exchange(k, t, slot, others)

    def exchange(self, k, t, slot, flows):
        if k == 1:
            for flow in flows:
                self.copy(t, flow, 0).start()
            return
        for flow in flows:
            self.copy(t, flow, k - 2).wait()
            kept = self.half(t, flow, k - 2, True)
            if k < 5:
                self.lands[flow][k - 2][slot] += kept[...]
                self.copy(t, flow, k - 1).start()
            else:
                first, rows, _ = FLOWS[flow]
                at = pl.ds(pl.multiple_of(t * STEP + first, 8), rows)
                self.result[at, :] = self.lands[flow][3][slot] + kept[...]

    def entry(self, call):
        step, begun = call, call >= 0
        for idle in self.idle:
            step = step - jnp.where(call > idle, 1, 0)
            begun = begun & (call != idle)
        return step, begun

    def carry(self, call):
        for k in range(2, 6):
            t, begun = self.entry(call - LAG * (k - 1))

            @pl.when(begun & (t < self.steps))
            def _():
                self.advance(k, t)

    def call(self, call, fresh):
        t, _ = self.entry(call)

        @pl.when(t < self.steps)
        def _():
            self.advance(1, t)

        @pl.when(t + 1 < fresh)
        def _():
            self.load(t + 1).wait()
            self.core_copy(t + 1).start()

        @pl.when(t + 2 < fresh)
        def _():
            self.load(t + 2).start()

        self.carry(call)

    def settle(self):
        for wait in self.pending:
            wait()
        self.pending = []
        self.ready = self.coming
        self.fetch()

    def fetch(self):
        for t in (self.next, self.next + 1):
            if self.loaded < t < self.ready // STEP:
                self.load(t).start()
                self.loaded = t

    def prime(self):
        first = self.next
        if first >= self.ready // STEP:
            return
        self.fetch()
        if self.cored < first:
            self.load(first).wait()
            self.core_copy(first).start()
            self.cored = first

    def begun(self, calls):
        fresh = self.ready // STEP
        self.calls += calls
        self.next += calls
        self.cored, self.loaded = min(self.next, fresh - 1), min(self.next + 1, fresh - 1)
        self.resting = 0
        self.clock = 0.0

    def rested(self, calls):
        self.calls += calls
        self.resting += calls
        self.clock = 0.0

    def loop(self, count, body, spent):
        every = max(1, round(self.period / spent))
        lead = max(1, math.ceil((self.period - self.clock) / spent))
        room = 1 + (count - lead) // every if count >= lead else 0
        start, fresh = self.calls, self.ready // STEP
        calls = min(room, fresh - self.next)
        idle = min(room, 4 * LAG - self.resting) if self.next >= fresh else 0
        spare = self.clock + count * spent
        if calls > 0:
            self.prime()
            step = lambda index: self.call(start + index, fresh)
            self.begun(calls)
        elif idle > 0:
            calls = idle
            self.idle.extend(range(start, start + calls))
            step = lambda index: self.carry(start + index)
            self.rested(calls)
        else:
            each(count, body)
            self.settle()
            self.clock = spare
            return
        last = lead - 1 + (calls - 1) * every

        def one(index):
            body(index)

            @pl.when((index >= lead - 1) & (index <= last) & (lax.rem(index - (lead - 1), every) == 0))
            def _():
                step(lax.div(index - (lead - 1), every))

        each(count, one)
        self.settle()
        self.clock = (count - 1 - last) * spent

    def tick(self, spent=0.0):
        self.clock += spent
        if spent > 0.0:
            self.settle()
        last = self.ready // STEP - 1
        if self.next <= last:
            if self.cored < self.next:
                self.prime()
                return
            if self.clock >= self.period:
                self.prime()
                self.call(self.calls, last + 1)
                self.begun(1)
        elif self.resting < 4 * LAG and self.clock >= self.period:
            self.idle.append(self.calls)
            self.carry(self.calls)
            self.rested(1)

    def finish(self, beside):
        self.settle()
        first, fresh, start = self.next, self.ready // STEP, self.calls
        self.prime()

        def one(index):
            self.call(start + index, fresh)
            beside(index)

        each(max(self.steps - first + 4 * LAG, 6), one)

    def send(self, place, sems, tile, rows, count, spent, slots=2, group=1):
        self.settle()
        start = self.ready

        def copy(slot, at):
            return pltpu.make_async_copy(place(slot), self.gathered.at[:, pl.ds(at, group * rows), :], sems.at[slot])

        def body(n):
            slot = lax.rem(n, slots)

            @pl.when(n >= slots)
            def _():
                copy(slot, start).wait()

            value = tile(n)
            for block in range(group):
                part = value[:, block * TILE : (block + 1) * TILE].reshape(32, rows, TILE)
                place(slot).at[:, pl.ds(block * rows, rows), :][...] = part
            copy(slot, pl.multiple_of(start + n * group * rows, 8)).start()

        self.loop(count, body, spent)
        for n in range(max(count - slots, 0), count):
            self.pending.append(functools.partial(lambda slot: copy(slot, start).wait(), n % slots))
        self.coming = start + count * group * rows


def backward_kernel(
    erows, drows, used,
    counts, positions, enc_gain_one, enc_gain_two, token, dec_gain_one, dec_gain_two, table, encoded, embed, dec_qkv, dec_out, dec_up, dec_down, cotangent,
    enc_qkv, enc_out, enc_up, enc_down,
    enc_normed_one, enc_inverse_one, enc_packed, enc_kept, enc_mixed, enc_normed_two, enc_inverse_two, enc_active, enc_slope,
    result, input_grad, gathered, kept_active, kept_middle, reduced, vector_sum,
    padded_positions, grad_embedded, filled, vector_part, vector_land, vector_send, vector_recv, dec_sems, enc_sems, tile_sems, *scratch,
):
    images, places, dwidth = cotangent.shape
    slots, width = input_grad.shape[1:]
    dhidden, hidden = dec_up.shape[1], enc_up.shape[1]
    dtotal, etotal = images * drows, images * erows
    reduction = Reduction(gathered, reduced, scratch, used)
    mask_token, dec_gain_one, dec_gain_two = as_row(token), as_row(dec_gain_one), as_row(dec_gain_two)
    row = lax.broadcasted_iota(jnp.int32, (drows, 1), 0)
    padded_positions[:images, :slots] = positions[...]
    vector_part[...] = jnp.zeros_like(vector_part)

    def pick_of(image):
        place = lax.broadcasted_iota(jnp.int32, (drows, erows), 0)
        slot = lax.broadcasted_iota(jnp.int32, (drows, erows), 1)
        named = (padded_positions[image : image + 1, :erows] == place) & (slot < counts[image])
        return jnp.where(named, 1.0, 0.0)

    beside = reduction.loop

    def decoder(
        qkv, out, up, down, normed_one, inverse_one, packed, kept, mixed, middle, normed_two, inverse_two, slope, wide_low, stage
    ):
        into_result = pltpu.make_async_copy(cotangent, result, dec_sems.at[0])
        weights = [(dec_qkv, qkv), (dec_out, out), (dec_up, up), (dec_down, down)]
        loads = [pltpu.make_async_copy(source, target, dec_sems.at[1 + i]) for i, (source, target) in enumerate(weights)]

        def fill(table_in, encoded_in, embed_in):
            starts = [(encoded, encoded_in), (embed, embed_in), (table, table_in)]
            starts = [pltpu.make_async_copy(source, target, dec_sems.at[5 + i]) for i, (source, target) in enumerate(starts)]
            for copy in starts + loads + [into_result]:
                copy.start()
            starts[0].wait()
            starts[1].wait()
            high, rest = mixed, wide_low

            def embed_tile(tile):
                value = nn(encoded_in[...], embed_in[:, columns(tile)])
                top = value.astype(BF)
                high[pl.ds(0, etotal), columns(tile)] = top
                rest[pl.ds(0, etotal), columns(tile)] = (value - top.astype(F32)).astype(BF)

            each(dwidth // TILE, embed_tile)
            starts[2].wait()
            for image in range(images):
                pick = pick_of(image)
                low_pick = pick.astype(BF)
                at = pl.ds(image * erows, erows)
                picked = nn(low_pick, high[at, :]) + nn(low_pick, rest[at, :])
                covered = jnp.sum(pick, axis=1, keepdims=True) > 0.5
                value = jnp.where(covered, picked, mask_token) + table_in[...]
                filled[pl.ds(image * drows, drows), :] = jnp.where(row < places, value, 0.0).astype(BF)

        pl.run_scoped(
            fill, pltpu.VMEM(table.shape, F32), pltpu.VMEM(encoded.shape, BF), pltpu.VMEM(embed.shape, BF)
        )
        norm_rows(dtotal, filled, dec_gain_one, normed_one, inverse_one)
        loads[0].wait()

        project(normed_one, qkv, packed)

        def mix(image):
            for group in range(dwidth // LANES):
                attend_block(packed, dwidth, drows, dwidth // DHEADS, image, group, places, kept, mixed)

        each(images, mix)
        loads[1].wait()

        middle[...] = filled[...].astype(F32) + nn(mixed[...], out[...])
        norm_rows(dtotal, middle, dec_gain_two, normed_two, inverse_two)
        loads[2].wait()
        grad_low = wide_low
        into_result.wait()
        pad_images(result, grad_low, drows)
        block = dwidth // 32

        def place(slot):
            return stage.at[:, pl.ds(pl.multiple_of(slot * block, 8), block), :]

        def place_two(slot):
            return stage.at[:, pl.ds(pl.multiple_of(slot * 2 * block, 8), 2 * block), :]

        def feed(active):
            feed_up(normed_two, up, active, slope)
            keep = [(active, kept_active, dec_sems.at[0]), (middle, kept_middle, dec_sems.at[1])]
            keep = [pltpu.make_async_copy(*copy) for copy in keep]
            for copy in keep:
                copy.start()
            reduction.enter()
            loads[3].wait()
            for tile in range(dwidth // TILE):
                at = slice(tile * TILE, (tile + 1) * TILE)
                reduction.send(lambda slot: stage, tile_sems, lambda n: tn(active[...], grad_low[:, at]), dhidden // 32, 1, 1.9, slots=1)
                if tile == 0:
                    feed_back(grad_low, down, slope, slope, beside, 4.0)
                    reduction.tick()
            for copy in keep:
                copy.wait()

        pl.run_scoped(feed, pltpu.VMEM((dtotal, dhidden), BF))
        reduction.tick()
        half = dhidden // 512 // 2
        for part in range(2):
            reduction.send(place_two, tile_sems, lambda n: tn(normed_two[...], slope[:, span(part * half + n, 512)]), block, half, 1.0, group=2)
            reduction.tick()
        times_back(slope, up, middle, beside, 3.3)
        reduction.tick()
        grad_attend = wide_low

        def keep_middle(at, grad):
            middle[at, :] = grad
            grad_attend[at, :] = grad.astype(BF)

        def late(wide, partial):
            vector_part[0, 4:5, :dwidth] = norm_back(
                dtotal, middle, normed_two, inverse_two, dec_gain_two, grad_low, keep_middle, partial
            )
            reduction.tick(2.2)
            reduction.send(place_two, tile_sems, lambda n: tn(mixed[...], grad_attend[...]), block, 1, 1.4, group=dwidth // TILE)
            reduction.tick()
            grad_mixed = normed_two
            times_back(grad_attend, out, grad_mixed, beside, 1.4)
            reduction.tick()
            groups = dwidth // LANES // 2
            half = dwidth // TILE // 2
            for part in range(2):
                def mix_back(image):
                    for group in range(part * groups, (part + 1) * groups):
                        attend_back_block(packed, dwidth, drows, dwidth // DHEADS, image, group, kept, grad_mixed, packed)

                reduction.loop(images, mix_back, 1.05)
                reduction.tick()
                tile = lambda n: tn(normed_one[...], packed[:, columns(lax.div(n, half) * 2 * half + part * half + lax.rem(n, half))])
                reduction.send(place, tile_sems, tile, block, 3 * half, 0.65)
                reduction.tick()
            times_back(packed, qkv, wide, beside, 2.7)
            reduction.tick()

            def keep_filled(at, grad):
                filled[at, :] = grad.astype(BF)

            vector_part[0, 3:4, :dwidth] = norm_back(
                dtotal, wide, normed_one, inverse_one, dec_gain_one, middle, keep_filled, partial
            )
            reduction.tick(2.2)

        pl.run_scoped(late, pltpu.VMEM((dtotal, dwidth), F32), pltpu.VMEM((8, dwidth), F32))
    dgroups, dheads = dwidth // LANES, DHEADS * LANES // dwidth
    wide_shape = (dtotal, dwidth)
    pl.run_scoped(
        decoder,
        *[pltpu.VMEM(ref.shape, BF) for ref in (dec_qkv, dec_out, dec_up, dec_down)],
        pltpu.VMEM(wide_shape, BF), pltpu.VMEM((dtotal, 1), F32), pltpu.VMEM((dtotal, 3 * dwidth), BF),
        pltpu.VMEM((images, dgroups, dheads * drows, drows), BF), pltpu.VMEM(wide_shape, BF), pltpu.VMEM(wide_shape, F32),
        pltpu.VMEM(wide_shape, BF), pltpu.VMEM((dtotal, 1), F32), pltpu.VMEM((dtotal, dhidden), BF), pltpu.VMEM(wide_shape, BF),
        pltpu.VMEM((32, dhidden // 32, TILE), F32),
    )

    def encoder(
        embed_in, out, weight, down, normed_one, inverse_one, packed, kept, mixed, normed_two, inverse_two, grad_pre,
        grad_low, grad_attend, middle, wide, stage,
    ):
        sources = [
            (embed, embed_in), (enc_down, down), (enc_slope, grad_pre), (enc_normed_two, normed_two), (enc_up, weight),
            (enc_inverse_two, inverse_two), (enc_out, out), (enc_mixed, mixed), (enc_packed, packed), (enc_kept, kept),
            (enc_normed_one, normed_one), (enc_inverse_one, inverse_one),
        ]
        loads = [pltpu.make_async_copy(source, target, enc_sems.at[i]) for i, (source, target) in enumerate(sources)]
        block = width // 32

        def place(slot):
            return stage.at[:, pl.ds(pl.multiple_of(slot * block, 8), block), :]

        def place_two(slot):
            return stage.at[:, pl.ds(pl.multiple_of(slot * 2 * block, 8), 2 * block), :]

        def feed(active, encoded_in):
            starts = [(encoded, encoded_in), (enc_active, active)]
            starts = [pltpu.make_async_copy(source, target, enc_sems.at[len(loads) + i]) for i, (source, target) in enumerate(starts)]
            for copy in starts + loads:
                copy.start()
            for image in range(images):
                grad = filled[pl.ds(image * drows, drows), :]
                grad_embedded[pl.ds(image * erows, erows), :] = tn(pick_of(image).astype(BF), grad).astype(BF)
            reduction.tick(2.0)
            starts[0].wait()
            reduction.send(place_two, tile_sems, lambda n: tn(encoded_in[...], grad_embedded[...]), block, 1, 1.8, group=dwidth // TILE)
            loads[0].wait()
            reduction.tick()
            value = nt(grad_embedded[...], embed_in[...])
            wide[...] = value
            grad_low[...] = value.astype(BF)
            reduction.tick(1.2)
            starts[1].wait()
            for tile in range(width // TILE):
                at = slice(tile * TILE, (tile + 1) * TILE)
                reduction.send(lambda slot: stage, tile_sems, lambda n: tn(active[...], grad_low[:, at]), hidden // 32, 1, 1.7, slots=1)
                reduction.tick()
            reduction.settle()

        pl.run_scoped(feed, pltpu.VMEM(enc_active.shape, BF), pltpu.VMEM(encoded.shape, BF))
        reduction.period = 2.5
        reduction.tick()
        loads[1].wait()
        loads[2].wait()
        feed_back(grad_low, down, grad_pre, grad_pre, beside, 4.6)
        reduction.tick()
        loads[3].wait()
        reduction.send(place_two, tile_sems, lambda n: tn(normed_two[...], grad_pre[:, span(n, 512)]), block, hidden // 512, 1.0, group=2)
        reduction.tick()
        loads[4].wait()
        times_back(grad_pre, weight, middle, beside, 3.9)
        reduction.tick()
        into_qkv = pltpu.make_async_copy(enc_qkv, weight.at[:, : enc_qkv.shape[1]], enc_sems.at[len(loads) + 2])
        into_qkv.start()
        loads[5].wait()

        def late(grad_mixed, partial, input_stage):
            def keep_middle(at, grad):
                middle[at, :] = grad
                grad_attend[at, :] = grad.astype(BF)

            vector_part[0, 1:2, :] = norm_back(etotal, middle, normed_two, inverse_two, as_row(enc_gain_two), wide, keep_middle, partial)
            loads[6].wait()
            loads[7].wait()
            reduction.tick(1.5)
            reduction.send(place, tile_sems, lambda n: tn(mixed[...], grad_attend[:, columns(n)]), block, width // TILE, 0.7)
            reduction.tick()
            times_back(grad_attend, out, grad_mixed, beside, 1.5)
            for load in loads[8:]:
                load.wait()
            reduction.tick()

            def mix_back(image):
                for group in range(width // LANES):
                    attend_back_block(packed, width, erows, width // HEADS, image, group, kept, grad_mixed, packed)

            reduction.loop(images, mix_back, 1.4)
            reduction.tick()
            reduction.send(place, tile_sems, lambda n: tn(normed_one[...], packed[:, columns(n)]), block, 3 * width // TILE, 0.58)
            reduction.settle()
            left = gathered.shape[1] - reduction.ready
            if left:
                stage[:, :left, :] = jnp.zeros((32, left, TILE), F32)
                rest = pltpu.make_async_copy(
                    stage.at[:, pl.ds(0, left), :], gathered.at[:, pl.ds(reduction.ready, left), :], tile_sems.at[0]
                )
                rest.start()
                reduction.pending.append(rest.wait)
                reduction.coming += left
            into_qkv.wait()
            reduction.tick()
            times_back(packed, weight.at[:, : enc_qkv.shape[1]], wide, beside, 3.1)
            reduction.tick()

            def keep_input(at, grad):
                wide[at, :] = grad

            vector_part[0, 0:1, :] = norm_back(etotal, wide, normed_one, inverse_one, as_row(enc_gain_one), middle, keep_input, partial)
            reduction.tick(1.5)
            for image in range(images):
                input_stage[image] = wide[image * erows : image * erows + slots, :]
            store = pltpu.make_async_copy(input_stage, input_grad, tile_sems.at[0])
            store.start()
            reduction.tick(1.5)
            store.wait()

        pl.run_scoped(
            late, pltpu.VMEM((etotal, width), BF), pltpu.VMEM((8, width), F32), pltpu.VMEM(input_grad.shape, F32)
        )

    pl.run_scoped(
        encoder,
        pltpu.VMEM(embed.shape, BF), pltpu.VMEM(enc_out.shape, BF), pltpu.VMEM(enc_up.shape, BF), pltpu.VMEM(enc_down.shape, BF),
        pltpu.VMEM(enc_normed_one.shape, BF), pltpu.VMEM(enc_inverse_one.shape, F32), pltpu.VMEM(enc_packed.shape, BF),
        pltpu.VMEM(enc_kept.shape, BF), pltpu.VMEM(enc_mixed.shape, BF), pltpu.VMEM(enc_normed_two.shape, BF),
        pltpu.VMEM(enc_inverse_two.shape, F32), pltpu.VMEM(enc_slope.shape, BF),
        pltpu.VMEM((etotal, width), BF), pltpu.VMEM((etotal, width), BF), pltpu.VMEM((etotal, width), F32), pltpu.VMEM((etotal, width), F32),
        pltpu.VMEM((32, hidden // 32, TILE), F32),
    )
    def finish_decoder(active, middle, down):
        loads = [(kept_active, active), (kept_middle, middle), (dec_down, down)]
        loads = [pltpu.make_async_copy(source, target, dec_sems.at[i]) for i, (source, target) in enumerate(loads)]
        for load in loads:
            load.start()
        reduction.tick()
        for load in loads:
            load.wait()
        for tile in range(dwidth // TILE):
            at = slice(tile * TILE, (tile + 1) * TILE)
            value = (middle[:, at] + nn(active[...], down[:, at])).astype(BF)
            for image in range(images):
                result[image, :, at] = value[image * drows : image * drows + places]
            reduction.tick(1.75)
        token_grad = jnp.zeros((1, dwidth), F32)
        for image in range(images):
            covered = jnp.sum(pick_of(image), axis=1, keepdims=True) > 0.5
            grad = filled[pl.ds(image * drows, drows), :]
            token_grad = token_grad + jnp.sum(jnp.where(covered | (row >= places), 0.0, grad.astype(F32)), axis=0, keepdims=True)
        vector_part[0, 2:3, :dwidth] = token_grad
        reduction.tick(1.5)

    pl.run_scoped(
        finish_decoder, pltpu.VMEM((dtotal, dhidden), BF), pltpu.VMEM((dtotal, dwidth), F32), pltpu.VMEM(dec_down.shape, BF)
    )
    order = "c" + DIMS

    def vector_copy(k):
        return pltpu.make_async_remote_copy(
            src_ref=vector_part.at[k],
            dst_ref=vector_land.at[k],
            send_sem=vector_send.at[k],
            recv_sem=vector_recv.at[k],
            device_id=partner(reduction.here, order[k]),
            device_id_type=MESH,
        )

    def vector_step(index):
        for k in range(6):
            @pl.when(index == k)
            def _():
                if k:
                    vector_copy(k - 1).wait()
                    vector_part[k] = vector_part[k - 1] + vector_land[k - 1]
                if k < 5:
                    vector_copy(k).start()

    reduction.finish(vector_step)
    vector_sum[...] = vector_part[5]


def unpack_kernel(halved, source, vector_sum, result_in, grad_in, *targets):
    *targets, result, grad, sems = targets
    matrices, vectors = targets[:9], targets[9:]
    copies = [pltpu.make_async_copy(result_in, result, sems.at[0]), pltpu.make_async_copy(grad_in, grad, sems.at[1])]
    for copy in copies:
        copy.start()
    index = lax.axis_index("dp") * lax.axis_size("seq") + lax.axis_index("seq")
    width = vector_sum.shape[1]
    for row, vector in enumerate(vectors):
        size = vector.shape[0]
        own = pltpu.roll(vector_sum[...], lax.rem(width - index * size, width), 1)
        vector[...] = own[row, :size]
    at = 0
    for index, target in enumerate(matrices):
        block, width = target.shape
        tiles = list(range(width // TILE))
        if index == halved:
            half = len(tiles) // 6
            tiles = [n // half * 2 * half + part * half + n % half for part in range(2) for n in range(3 * half)]
        for n in tiles:
            target[:, n * TILE : (n + 1) * TILE] = source[at : at + block, :]
            at += block
    for copy in copies:
        copy.wait()


def vmem(count):
    return [pl.BlockSpec(memory_space=pltpu.VMEM)] * count


def anywhere(count):
    return [pl.BlockSpec(memory_space=pl.ANY)] * count


def shapes(*pairs):
    return [jax.ShapeDtypeStruct(shape, dtype) for shape, dtype in pairs]


def scratches(*pairs):
    return [pltpu.VMEM(shape, dtype) for shape, dtype in pairs]


def fast_local(
    enc_input, keep_count, keep_positions,
    enc_gain_one, enc_qkv_weight, enc_out_weight, enc_gain_two, enc_up_weight, enc_down_weight,
    embed_weight, mask_token,
    dec_gain_one, dec_qkv_weight, dec_out_weight, dec_gain_two, dec_up_weight, dec_down_weight,
    cotangent,
):
    images, slots, width = enc_input.shape
    places, dwidth = cotangent.shape[1:]
    hidden, dhidden = enc_up_weight.shape[1], dec_up_weight.shape[1]
    erows, drows = padded(slots, 16), padded(places, 16)
    etotal, dtotal = images * erows, images * drows
    egroups, dgroups = width // LANES, dwidth // LANES
    eheads, dheads = HEADS // egroups, DHEADS // dgroups
    smem = [pl.BlockSpec(memory_space=pltpu.SMEM)]
    settings = functools.partial(pltpu.CompilerParams, vmem_limit_bytes=VMEM_BYTES)
    vectors = (enc_gain_one, enc_gain_two, mask_token, dec_gain_one, dec_gain_two)

    saved = shapes(
        ((etotal, width), BF), ((etotal, 1), F32), ((etotal, 3 * width), BF), ((images, egroups, eheads * erows, erows), BF),
        ((etotal, width), BF), ((etotal, width), BF), ((etotal, 1), F32), ((etotal, hidden), BF), ((etotal, hidden), BF), ((etotal, width), BF),
    )
    normed_one, inverse_one, packed, kept, mixed, normed_two, inverse_two, active, slope, encoded = pl.pallas_call(
        functools.partial(enc_forward_kernel, erows),
        name="enc_forward",
        out_shape=saved,
        in_specs=smem + vmem(3) + anywhere(4),
        out_specs=anywhere(10),
        scratch_shapes=scratches(
            *((weight.shape, BF) for weight in (enc_qkv_weight, enc_out_weight, enc_up_weight, enc_down_weight)),
            ((etotal, width), BF), ((etotal, width), F32), *((array.shape, array.dtype) for array in saved),
        ) + [pltpu.SemaphoreType.DMA((4,)), pltpu.SemaphoreType.DMA((10,))],
        compiler_params=settings(),
    )(keep_count, enc_input, enc_gain_one, enc_gain_two, enc_qkv_weight, enc_out_weight, enc_up_weight, enc_down_weight)

    table = jnp.asarray(position_rows(places, dwidth, drows))
    block = dwidth // 32
    eblock = width // 32
    layout = (
        (dhidden // 32, dwidth), (block, dhidden), (block, dwidth), (block, 3 * dwidth), (eblock, dwidth),
        (hidden // 32, width), (eblock, hidden), (eblock, width), (eblock, 3 * width),
    )
    used = sum(rows * columns // TILE for rows, columns in layout)
    share_rows = padded(used, STEP)
    dec_output, input_grad, _, _, _, reduced, vector_sum = pl.pallas_call(
        functools.partial(backward_kernel, erows, drows, used),
        name="backward",
        out_shape=shapes(
            (cotangent.shape, BF), (enc_input.shape, F32), ((32, share_rows, TILE), F32), ((dtotal, dhidden), BF), ((dtotal, dwidth), F32),
            ((share_rows, TILE), F32), ((8, width), F32),
        ),
        in_specs=smem + vmem(6) + anywhere(21),
        out_specs=vmem(1) + anywhere(4) + vmem(2),
        scratch_shapes=scratches(
            ((8, LANES), jnp.int32), ((etotal, dwidth), BF), ((dtotal, dwidth), BF), ((6, 8, width), F32), ((5, 8, width), F32),
        ) + [pltpu.SemaphoreType.DMA((count,)) for count in (5, 5, 8, 15, 2)] + Reduction.scratch(),
        compiler_params=settings(collective_id=0, has_side_effects=True),
    )(
        keep_count, keep_positions, *vectors, table, encoded, embed_weight, dec_qkv_weight, dec_out_weight, dec_up_weight, dec_down_weight,
        cotangent, enc_qkv_weight, enc_out_weight, enc_up_weight, enc_down_weight,
        normed_one, inverse_one, packed, kept, mixed, normed_two, inverse_two, active, slope,
    )
    dec_down, dec_up, dec_out, dec_qkv, embed, enc_down, enc_up, enc_out, enc_qkv, *cuts, dec_output, input_grad = pl.pallas_call(
        functools.partial(unpack_kernel, 3),
        name="unpack",
        out_shape=shapes(
            *((shape, F32) for shape in layout), *(((vector.shape[0] // 32,), F32) for vector in vectors),
            (cotangent.shape, BF), (enc_input.shape, F32),
        ),
        in_specs=vmem(2) + anywhere(2),
        out_specs=vmem(11 + len(vectors)),
        scratch_shapes=[pltpu.SemaphoreType.DMA((2,))],
    )(reduced, vector_sum, dec_output, input_grad)
    return (
        dec_output, input_grad, cuts[0], enc_qkv, enc_out, cuts[1], enc_up, enc_down, embed, cuts[2],
        cuts[3], dec_qkv, dec_out, cuts[4], dec_up, dec_down,
    )


def position_rows(places, width, rows):
    side = math.isqrt(places)
    quarter = width // 4
    place = np.arange(places)
    rate = 1.0 / 10000.0 ** (np.arange(quarter) / quarter)
    across, down = place[:, None] % side * rate, place[:, None] // side * rate
    table = np.concatenate([np.sin(across), np.cos(across), np.sin(down), np.cos(down)], axis=1)
    return np.pad(table, ((0, rows - places), (0, 0))).astype(np.float32)


def solution(mesh):
    placed = (
        P(("dp", "seq"), None, None),
        P(("dp", "seq")),
        P(("dp", "seq"), None),
        P(),
        P(),
        P(),
        P(),
        P(),
        P(),
        P(),
        P(),
        P(),
        P(),
        P(),
        P(),
        P(),
        P(),
        P(("dp", "seq"), None, None),
    )
    fast = (mesh.shape["dp"], mesh.shape["seq"]) == (8, 4)
    return jax.shard_map(
        fast_local if fast else local,
        mesh=mesh,
        in_specs=placed,
        out_specs=(
            P(("dp", "seq"), None, None),
            P(("dp", "seq"), None, None),
            P(("dp", "seq")),
            P(("dp", "seq"), None),
            P(("dp", "seq"), None),
            P(("dp", "seq")),
            P(("dp", "seq"), None),
            P(("dp", "seq"), None),
            P(("dp", "seq"), None),
            P(("dp", "seq")),
            P(("dp", "seq")),
            P(("dp", "seq"), None),
            P(("dp", "seq"), None),
            P(("dp", "seq")),
            P(("dp", "seq"), None),
            P(("dp", "seq"), None),
        ),
        check_vma=False,
    )
```

```python
import functools
import math

import jax
import jax.numpy as jnp
import numpy as np
from jax import lax
from jax.experimental import pallas as pl
from jax.experimental.pallas import tpu as pltpu
from jax.sharding import PartitionSpec as P

HEADS = 12
DHEADS = 16
PATCHES = 196


eps = 1e-06


def position_table(count, model_width):
    grid_side = math.isqrt(count)
    quarter = model_width // 4
    places = jnp.arange(count)
    across = (places % grid_side).astype(jnp.float32)
    row_place = (places // grid_side).astype(jnp.float32)
    frequency = 1.0 / 10000.0 ** (jnp.arange(quarter).astype(jnp.float32) / quarter)
    return jnp.concatenate(
        [
            jnp.sin(across[:, None] * frequency),
            jnp.cos(across[:, None] * frequency),
            jnp.sin(row_place[:, None] * frequency),
            jnp.cos(row_place[:, None] * frequency),
        ],
        axis=1,
    )


def contract(operand, matrix):
    return jnp.einsum("...i,ij->...j", operand, matrix, preferred_element_type=jnp.float32)


def contract_back(gradient, matrix):
    return jnp.einsum("...j,ij->...i", gradient, matrix, preferred_element_type=jnp.float32)


def outer_sum(operand, gradient):
    flat_left = operand.reshape(-1, operand.shape[-1])
    flat_right = gradient.reshape(-1, gradient.shape[-1])
    return lax.dot_general(
        flat_left, flat_right, (((0,), (0,)), ((), ())), preferred_element_type=jnp.float32
    )


def exact_gelu(values):
    return jax.nn.gelu(values, approximate=False)


def gelu_back(pre_act, grad_active):
    unused, pullback = jax.vjp(exact_gelu, pre_act)
    return pullback(grad_active)[0]


def layer_norm(stream, gain_vec):
    row_mean = jnp.mean(stream, axis=-1, keepdims=True)
    centered = stream - row_mean
    inverse = lax.rsqrt(jnp.mean(centered * centered, axis=-1, keepdims=True) + eps)
    unit_rows = centered * inverse
    return (unit_rows * gain_vec, unit_rows, inverse)


def layer_norm_back(grad_normed, unit_rows, inverse, gain_vec):
    grad_gain = jnp.sum((grad_normed * unit_rows).reshape(-1, unit_rows.shape[-1]), axis=0)
    grad_unit = grad_normed * gain_vec
    grad_stream = inverse * (
        grad_unit
        - jnp.mean(grad_unit, axis=-1, keepdims=True)
        - unit_rows * jnp.mean(grad_unit * unit_rows, axis=-1, keepdims=True)
    )
    return (grad_stream, grad_gain)


def attend(packed, head_count, key_mask):
    batch_size, row_count, triple_width = packed.shape
    model_width = triple_width // 3
    head_size = model_width // head_count
    queries = packed[:, :, :model_width].reshape(batch_size, row_count, head_count, head_size)
    key_heads = packed[:, :, model_width : 2 * model_width].reshape(
        batch_size, row_count, head_count, head_size
    )
    value_heads = packed[:, :, 2 * model_width :].reshape(
        batch_size, row_count, head_count, head_size
    )
    scores = jnp.einsum(
        "bqhd,bkhd->bhqk", queries, key_heads, preferred_element_type=jnp.float32
    ) * head_size ** (-0.5)
    if key_mask is not None:
        scores = jnp.where(key_mask[:, None, None, :], scores, -1e30)
    row_max = jnp.max(scores, axis=-1, keepdims=True)
    raised = jnp.exp(scores - row_max)
    attn_weights = raised / jnp.sum(raised, axis=-1, keepdims=True)
    attn_low = attn_weights.astype(jnp.bfloat16)
    mixed_heads = jnp.einsum(
        "bhqk,bkhd->bqhd", attn_low, value_heads, preferred_element_type=jnp.float32
    )
    mixed_heads = mixed_heads.reshape(batch_size, row_count, model_width).astype(jnp.bfloat16)
    return (mixed_heads, attn_weights, attn_low)


def attend_back(packed, attn_weights, attn_low, grad_mixed, head_count):
    batch_size, row_count, triple_width = packed.shape
    model_width = triple_width // 3
    head_size = model_width // head_count
    factor = head_size ** (-0.5)
    queries = packed[:, :, :model_width].reshape(batch_size, row_count, head_count, head_size)
    key_heads = packed[:, :, model_width : 2 * model_width].reshape(
        batch_size, row_count, head_count, head_size
    )
    value_heads = packed[:, :, 2 * model_width :].reshape(
        batch_size, row_count, head_count, head_size
    )
    grad_heads = grad_mixed.reshape(batch_size, row_count, head_count, head_size)
    grad_values = jnp.einsum(
        "bhqk,bqhd->bkhd", attn_low, grad_heads, preferred_element_type=jnp.float32
    )
    grad_attn = jnp.einsum(
        "bqhd,bkhd->bhqk", grad_heads, value_heads, preferred_element_type=jnp.float32
    )
    grad_scores = attn_weights * (
        grad_attn - jnp.sum(attn_weights * grad_attn, axis=-1, keepdims=True)
    )
    grad_scores = grad_scores.astype(jnp.bfloat16)
    grad_queries = (
        jnp.einsum("bhqk,bkhd->bqhd", grad_scores, key_heads, preferred_element_type=jnp.float32)
        * factor
    )
    grad_keys = (
        jnp.einsum("bhqk,bqhd->bkhd", grad_scores, queries, preferred_element_type=jnp.float32)
        * factor
    )
    grad_packed = jnp.concatenate(
        [
            grad_queries.reshape(batch_size, row_count, model_width),
            grad_keys.reshape(batch_size, row_count, model_width),
            grad_values.reshape(batch_size, row_count, model_width),
        ],
        axis=-1,
    )
    return grad_packed.astype(jnp.bfloat16)


def mlp_forward(middle, gain_two, up_weight, down_weight):
    normed_two, unit_two, inverse_two = layer_norm(middle, gain_two.astype(jnp.float32))
    second_low = normed_two.astype(jnp.bfloat16)
    pre_act = contract(second_low, up_weight)
    active_low = exact_gelu(pre_act).astype(jnp.bfloat16)
    result = middle + contract(active_low, down_weight)
    return (
        result,
        {
            "unit_two": unit_two,
            "inverse_two": inverse_two,
            "second_low": second_low,
            "pre_act": pre_act,
            "active_low": active_low,
        },
    )


def mlp_backward(grad_result, kept_values, gain_two, up_weight, down_weight):
    grad_branch = grad_result.astype(jnp.bfloat16)
    grad_down = outer_sum(kept_values["active_low"], grad_branch)
    grad_active = contract_back(grad_branch, down_weight)
    grad_pre = gelu_back(kept_values["pre_act"], grad_active).astype(jnp.bfloat16)
    grad_up = outer_sum(kept_values["second_low"], grad_pre)
    grad_second = contract_back(grad_pre, up_weight)
    grad_middle, grad_gain_two = layer_norm_back(
        grad_second,
        kept_values["unit_two"],
        kept_values["inverse_two"],
        gain_two.astype(jnp.float32),
    )
    return (grad_middle + grad_result, grad_gain_two, grad_up, grad_down)


def block_forward(stream, weights, head_count, key_mask):
    gain_one, qkv_weight, out_weight, gain_two, up_weight, down_weight = weights
    normed_one, unit_one, inverse_one = layer_norm(stream, gain_one.astype(jnp.float32))
    normed_low = normed_one.astype(jnp.bfloat16)
    packed = contract(normed_low, qkv_weight).astype(jnp.bfloat16)
    mixed_heads, attn_weights, attn_low = attend(packed, head_count, key_mask)
    middle = stream + contract(mixed_heads, out_weight)
    result, mlp_kept = mlp_forward(middle, gain_two, up_weight, down_weight)
    kept_values = {
        "unit_one": unit_one,
        "inverse_one": inverse_one,
        "normed_low": normed_low,
        "packed": packed,
        "attn_weights": attn_weights,
        "attn_low": attn_low,
        "mixed_heads": mixed_heads,
        "mlp": mlp_kept,
    }
    return (result, kept_values)


def block_backward(grad_result, kept_values, weights, head_count):
    gain_one, qkv_weight, out_weight, gain_two, up_weight, down_weight = weights
    grad_middle, grad_gain_two, grad_up, grad_down = mlp_backward(
        grad_result, kept_values["mlp"], gain_two, up_weight, down_weight
    )
    grad_attend = grad_middle.astype(jnp.bfloat16)
    grad_out = outer_sum(kept_values["mixed_heads"], grad_attend)
    grad_mixed = contract_back(grad_attend, out_weight).astype(jnp.bfloat16)
    grad_packed = attend_back(
        kept_values["packed"],
        kept_values["attn_weights"],
        kept_values["attn_low"],
        grad_mixed,
        head_count,
    )
    grad_qkv = outer_sum(kept_values["normed_low"], grad_packed)
    grad_normed = contract_back(grad_packed, qkv_weight)
    grad_stream, grad_gain_one = layer_norm_back(
        grad_normed,
        kept_values["unit_one"],
        kept_values["inverse_one"],
        gain_one.astype(jnp.float32),
    )
    return (
        grad_stream + grad_middle,
        grad_gain_one,
        grad_qkv,
        grad_out,
        grad_gain_two,
        grad_up,
        grad_down,
    )


def micro_step(
    enc_rows, counts, positions, cot_rows, enc_weights, embed_weight, mask_token, dec_weights
):
    slot_total = enc_rows.shape[1]
    live_slots = jnp.arange(slot_total)[None, :] < counts[:, None]
    encoded, enc_kept = block_forward(enc_rows.astype(jnp.float32), enc_weights, HEADS, live_slots)
    encoded_low = encoded.astype(jnp.bfloat16)
    embedded = contract(encoded_low, embed_weight)
    places = jnp.arange(PATCHES)
    matches = (positions[:, :, None] == places[None, None, :]) & live_slots[:, :, None]
    covered = jnp.any(matches, axis=1)
    slot_index = jnp.sum(jnp.where(matches, jnp.arange(slot_total)[None, :, None], 0), axis=1)
    picked = jnp.take_along_axis(embedded, slot_index[:, :, None], axis=1)
    filled = jnp.where(covered[:, :, None], picked, mask_token.astype(jnp.float32))
    filled = filled + position_table(PATCHES, embedded.shape[-1])
    filled_low = filled.astype(jnp.bfloat16)
    decoded, dec_kept = block_forward(filled_low.astype(jnp.float32), dec_weights, DHEADS, None)
    dec_piece = decoded.astype(jnp.bfloat16)
    dec_back = block_backward(cot_rows.astype(jnp.float32), dec_kept, dec_weights, DHEADS)
    dec_terms = dec_back[1:]
    grad_filled = dec_back[0].astype(jnp.bfloat16).astype(jnp.float32)
    mask_term = jnp.sum(
        jnp.where(covered[:, :, None], 0.0, grad_filled).reshape(-1, grad_filled.shape[-1]), axis=0
    )
    grad_embedded = jnp.take_along_axis(grad_filled, positions[:, :, None], axis=1)
    grad_embedded = jnp.where(live_slots[:, :, None], grad_embedded, 0.0).astype(jnp.bfloat16)
    embed_term = outer_sum(encoded_low, grad_embedded)
    grad_encoded = contract_back(grad_embedded, embed_weight)
    enc_back = block_backward(grad_encoded, enc_kept, enc_weights, HEADS)
    grad_input = enc_back[0]
    enc_terms = enc_back[1:] + (embed_term, mask_term)
    return (dec_piece, grad_input, tuple(enc_terms) + tuple(dec_terms))


def local(
    enc_input,
    keep_count,
    keep_positions,
    enc_gain_one,
    enc_qkv_weight,
    enc_out_weight,
    enc_gain_two,
    enc_up_weight,
    enc_down_weight,
    embed_weight,
    mask_token,
    dec_gain_one,
    dec_qkv_weight,
    dec_out_weight,
    dec_gain_two,
    dec_up_weight,
    dec_down_weight,
    cotangent,
):
    enc_weights = (
        enc_gain_one,
        enc_qkv_weight,
        enc_out_weight,
        enc_gain_two,
        enc_up_weight,
        enc_down_weight,
    )
    dec_weights = (
        dec_gain_one,
        dec_qkv_weight,
        dec_out_weight,
        dec_gain_two,
        dec_up_weight,
        dec_down_weight,
    )
    all_params = (
        enc_gain_one,
        enc_qkv_weight,
        enc_out_weight,
        enc_gain_two,
        enc_up_weight,
        enc_down_weight,
        embed_weight,
        mask_token,
        dec_gain_one,
        dec_qkv_weight,
        dec_out_weight,
        dec_gain_two,
        dec_up_weight,
        dec_down_weight,
    )
    dec_pieces, input_grads, totals = micro_step(
        enc_input, keep_count, keep_positions, cotangent, enc_weights, embed_weight, mask_token, dec_weights
    )
    totals = (
        lax.psum_scatter(totals[0], ("dp", "seq"), scatter_dimension=0, tiled=True),
        lax.psum_scatter(totals[1], ("dp", "seq"), scatter_dimension=0, tiled=True),
        lax.psum_scatter(totals[2], ("dp", "seq"), scatter_dimension=0, tiled=True),
        lax.psum_scatter(totals[3], ("dp", "seq"), scatter_dimension=0, tiled=True),
        lax.psum_scatter(totals[4], ("dp", "seq"), scatter_dimension=0, tiled=True),
        lax.psum_scatter(totals[5], ("dp", "seq"), scatter_dimension=0, tiled=True),
        lax.psum_scatter(totals[6], ("dp", "seq"), scatter_dimension=0, tiled=True),
        lax.psum_scatter(totals[7], ("dp", "seq"), scatter_dimension=0, tiled=True),
        lax.psum_scatter(totals[8], ("dp", "seq"), scatter_dimension=0, tiled=True),
        lax.psum_scatter(totals[9], ("dp", "seq"), scatter_dimension=0, tiled=True),
        lax.psum_scatter(totals[10], ("dp", "seq"), scatter_dimension=0, tiled=True),
        lax.psum_scatter(totals[11], ("dp", "seq"), scatter_dimension=0, tiled=True),
        lax.psum_scatter(totals[12], ("dp", "seq"), scatter_dimension=0, tiled=True),
        lax.psum_scatter(totals[13], ("dp", "seq"), scatter_dimension=0, tiled=True),
    )
    dec_output = dec_pieces.reshape(cotangent.shape)
    enc_input_grad = input_grads.reshape(enc_input.shape)
    return (
        dec_output,
        enc_input_grad,
        totals[0],
        totals[1],
        totals[2],
        totals[3],
        totals[4],
        totals[5],
        totals[6],
        totals[7],
        totals[8],
        totals[9],
        totals[10],
        totals[11],
        totals[12],
        totals[13],
    )


MESH = pl.DeviceIdType.MESH
BF = jnp.bfloat16
F32 = jnp.float32
LANES = 128
TILE = 256
CHUNK = 48
VMEM_BYTES = 62 * 2**20
STEP = 40
FLOWS = ((0, 16, "xyls"), (16, 16, "yxls"), (32, 8, "lsxy"))
COPIES = 4 * len(FLOWS) + 1
SLOTS = 8
LAG = 2
DIMS = "slyx"


def padded(count, multiple):
    return -(-count // multiple) * multiple


def nn(left, right):
    return lax.dot_general(left, right, (((1,), (0,)), ((), ())), preferred_element_type=F32)


def nt(left, right):
    return lax.dot_general(left, right, (((1,), (1,)), ((), ())), preferred_element_type=F32)


def tn(left, right):
    return lax.dot_general(left, right, (((0,), (0,)), ((), ())), preferred_element_type=F32)


def columns(tile):
    return pl.ds(pl.multiple_of(tile * TILE, TILE), TILE)


def wide_of(rows, count):
    return next(wide for wide in ((768, 512, TILE) if rows < 1000 else (512, TILE)) if count % wide == 0)


def span(tile, wide):
    return pl.ds(pl.multiple_of(tile * wide, wide), wide)


def each_pair(count, body):
    def both(index):
        body(2 * index)
        body(2 * index + 1)

    each(count // 2, both)
    if count % 2:
        body(count - 1)


def each(count, body):
    lax.fori_loop(0, count, lambda index, carry: (body(index), carry)[1], 0)


def gelu_pair(values):
    reach = jnp.abs(values)
    point = 1.0 / (1.0 + 0.23164189 * reach)
    decay = jnp.exp(-0.5 * values * values)
    tail = 0.5307027145 * point - 0.7265760135
    tail = tail * point + 0.710706870
    tail = tail * point - 0.142248368
    tail = tail * point + 0.127414796
    tail = tail * point * decay
    below = jnp.where(values < 0.0, tail, 1.0 - tail)
    return values * below, below + values * decay * 0.3989422804014327


def as_row(vector):
    return vector[...].astype(F32).reshape(1, vector.shape[0])


def norm_rows(total, source, gain, normed, inverse):
    width = gain.shape[-1]

    def body(chunk):
        rows = pl.ds(pl.multiple_of(chunk * CHUNK, CHUNK), CHUNK)
        stream = source[rows, :].astype(F32)
        centered = stream - jnp.sum(stream, axis=-1, keepdims=True) * (1.0 / width)
        scale = lax.rsqrt(jnp.sum(centered * centered, axis=-1, keepdims=True) * (1.0 / width) + eps)
        inverse[rows, :] = scale
        normed[rows, :] = (centered * scale * gain).astype(BF)

    each_pair(total // CHUNK, body)


def norm_back(total, grad_normed, normed, inverse, gain, added, emit, partial):
    width = gain.shape[-1]
    over = 1.0 / gain
    partial[...] = jnp.zeros_like(partial)

    def body(chunk):
        rows = pl.ds(pl.multiple_of(chunk * CHUNK, CHUNK), CHUNK)
        grad = grad_normed[rows, :]
        unit = normed[rows, :].astype(F32)
        both = grad * unit
        scaled = grad * gain
        first = jnp.sum(scaled, axis=-1, keepdims=True) * (1.0 / width)
        second = jnp.sum(both, axis=-1, keepdims=True) * (1.0 / width)
        emit(rows, inverse[rows, :] * (scaled - first - unit * over * second) + added[rows, :].astype(F32))
        partial[...] += jnp.sum(both.reshape(CHUNK // 8, 8, width), axis=0)

    each_pair(total // CHUNK, body)
    return jnp.sum(partial[...], axis=0, keepdims=True) * over


def head_masks(size):
    lane = lax.broadcasted_iota(jnp.int32, (1, LANES), 1)
    return [((lane >= h * size) & (lane < (h + 1) * size)).astype(F32) for h in range(LANES // size)]


def split_heads(block, masks):
    return jnp.concatenate([block * mask.astype(BF) for mask in masks], axis=0)


def merge_heads(stacked, masks, rows):
    total = stacked[:rows] * masks[0]
    for h in range(1, len(masks)):
        total = total + stacked[h * rows : (h + 1) * rows] * masks[h]
    return total


def attend_block(packed, width, rows, size, image, group, limit, kept, mixed):
    masks = head_masks(size)
    heads = len(masks)
    at = pl.ds(pl.multiple_of(image * rows, 16), rows)
    queries = packed[at, group * LANES : (group + 1) * LANES]
    keys = packed[at, width + group * LANES : width + (group + 1) * LANES]
    values = packed[at, 2 * width + group * LANES : 2 * width + (group + 1) * LANES]
    factor = size**-0.5 * 1.4426950408889634
    if isinstance(limit, int):
        first = limit // 16 * 16
        live = lax.broadcasted_iota(jnp.int32, (rows - first, 1), 0) < limit - first
        total = None
        for head, mask in enumerate(masks):
            scores = nt(keys * mask.astype(BF), queries)
            scores = jnp.concatenate([scores[:first], jnp.where(live, scores[first:], -1e30)], axis=0)
            raised = jnp.exp2((scores - jnp.max(scores, axis=0, keepdims=True)) * factor)
            low = (raised * (1.0 / jnp.sum(raised, axis=0, keepdims=True))).astype(BF)
            kept[image, group, head * rows : (head + 1) * rows, :] = low
            part = tn(low, values * mask.astype(BF))
            total = part if total is None else total + part
        mixed[at, group * LANES : (group + 1) * LANES] = total.astype(BF)
        return
    scores = nt(split_heads(keys, masks), queries).reshape(heads, rows, rows)
    live = lax.broadcasted_iota(jnp.int32, (1, rows, 1), 1) < limit
    scores = jnp.where(live, scores, -1e30)
    raised = jnp.exp2((scores - jnp.max(scores, axis=1, keepdims=True)) * factor)
    weights = raised * (1.0 / jnp.sum(raised, axis=1, keepdims=True))
    low = weights.reshape(heads * rows, rows).astype(BF)
    kept[image, group] = low
    mixed[at, group * LANES : (group + 1) * LANES] = tn(low, split_heads(values, masks)).astype(BF)


def attend_back_block(packed, width, rows, size, image, group, kept, grad_mixed, grad_packed):
    masks = head_masks(size)
    heads = len(masks)
    at = pl.ds(pl.multiple_of(image * rows, 16), rows)
    queries = packed[at, group * LANES : (group + 1) * LANES]
    keys = packed[at, width + group * LANES : width + (group + 1) * LANES]
    values = packed[at, 2 * width + group * LANES : 2 * width + (group + 1) * LANES]
    grad_out = grad_mixed[at, group * LANES : (group + 1) * LANES]
    low = kept[image, group]
    weights = low.astype(F32)
    both = weights * nt(split_heads(values, masks), grad_out)
    inner = jnp.sum(both.reshape(heads, rows, rows), axis=1, keepdims=True)
    grad_scores = both - (weights.reshape(heads, rows, rows) * inner).reshape(heads * rows, rows)
    grad_scores = grad_scores.astype(BF)
    grad_values = merge_heads(nn(low, grad_out), masks, rows)
    grad_keys = merge_heads(nn(grad_scores, queries), masks, rows) * size**-0.5
    flipped = keys.T
    parts = [nn(flipped[h * size : (h + 1) * size], grad_scores[h * rows : (h + 1) * rows]) for h in range(heads)]
    grad_queries = jnp.concatenate(parts, axis=0).T * size**-0.5
    grad_packed[at, group * LANES : (group + 1) * LANES] = grad_queries.astype(BF)
    grad_packed[at, width + group * LANES : width + (group + 1) * LANES] = grad_keys.astype(BF)
    grad_packed[at, 2 * width + group * LANES : 2 * width + (group + 1) * LANES] = grad_values.astype(BF)


def pad_images(source, target, rows):
    images, count = source.shape[0], source.shape[1]
    whole = count // 16 * 16
    for image in range(images):
        target[image * rows + whole : (image + 1) * rows, :] = jnp.zeros((rows - whole, target.shape[1]), target.dtype)
        target[image * rows : image * rows + count, :] = source[image]


def enc_forward_kernel(
    rows, counts, stream, gain_one, gain_two, qkv, out, up, down,
    normed_one_out, inverse_one_out, packed_out, kept_out, mixed_out, normed_two_out, inverse_two_out, active_out, slope_out, encoded_out,
    qkv_in, out_in, up_in, down_in, padded_in, middle,
    normed_one, inverse_one, packed, kept, mixed, normed_two, inverse_two, active, slope, encoded, in_sems, out_sems,
):
    images = stream.shape[0]
    total = images * rows
    width = stream.shape[-1]
    weights = [(qkv, qkv_in), (out, out_in), (up, up_in), (down, down_in)]
    loads = [pltpu.make_async_copy(source, target, in_sems.at[i]) for i, (source, target) in enumerate(weights)]
    for load in loads:
        load.start()
    results = [
        (normed_one, normed_one_out), (inverse_one, inverse_one_out), (packed, packed_out), (kept, kept_out), (mixed, mixed_out),
        (normed_two, normed_two_out), (inverse_two, inverse_two_out), (active, active_out), (slope, slope_out), (encoded, encoded_out),
    ]
    stores = [pltpu.make_async_copy(source, target, out_sems.at[i]) for i, (source, target) in enumerate(results)]
    pad_images(stream, padded_in, rows)
    norm_rows(total, padded_in, as_row(gain_one), normed_one, inverse_one)
    loads[0].wait()

    project(normed_one, qkv_in, packed)
    for store in stores[:3]:
        store.start()

    def mix(image):
        for group in range(width // LANES):
            attend_block(packed, width, rows, width // HEADS, image, group, counts[image], kept, mixed)

    each(images, mix)
    for store in stores[3:5]:
        store.start()
    loads[1].wait()

    middle[...] = padded_in[...].astype(F32) + nn(mixed[...], out_in[...])
    norm_rows(total, middle, as_row(gain_two), normed_two, inverse_two)
    loads[2].wait()
    feed_up(normed_two, up_in, active, slope)
    for store in stores[5:9]:
        store.start()
    loads[3].wait()

    encoded[...] = (middle[...] + nn(active[...], down_in[...])).astype(BF)
    stores[9].start()
    for store in stores:
        store.wait()


def project(normed, weight, packed):
    wide = wide_of(normed.shape[0], weight.shape[1])

    def body(tile):
        packed[:, span(tile, wide)] = nn(normed[...], weight[:, span(tile, wide)]).astype(BF)

    each(weight.shape[1] // wide, body)


def feed_up(normed, up, active, slope):
    wide = wide_of(normed.shape[0], up.shape[1])

    def body(tile):
        value, derivative = gelu_pair(nn(normed[...], up[:, span(tile, wide)]))
        active[:, span(tile, wide)] = value.astype(BF)
        slope[:, span(tile, wide)] = derivative.astype(BF)

    each(up.shape[1] // wide, body)


def feed_back(grad_low, down, slope, grad_pre, beside, spent):
    wide = wide_of(grad_low.shape[0], down.shape[0])
    count = down.shape[0] // wide

    def body(tile):
        grad = nt(grad_low[...], down[span(tile, wide), :]) * slope[:, span(tile, wide)].astype(F32)
        grad_pre[:, span(tile, wide)] = grad.astype(BF)

    beside(count, body, spent / count)


def times_back(grad, matrix, result, beside, spent):
    wide = wide_of(grad.shape[0], matrix.shape[0])
    count = matrix.shape[0] // wide

    def body(tile):
        result[:, span(tile, wide)] = nt(grad[...], matrix[span(tile, wide), :]).astype(result.dtype)

    beside(count, body, spent / count)


def one_hot(positions, image, limit, slots, places):
    place = lax.broadcasted_iota(jnp.int32, (places, slots), 0)
    slot = lax.broadcasted_iota(jnp.int32, (places, slots), 1)
    return jnp.where((positions[image : image + 1, :slots] == place) & (slot < limit), 1.0, 0.0)


def coords():
    seq, dp = lax.axis_index("seq"), lax.axis_index("dp")
    return {"s": dp // 4, "l": (dp // 2) % 2, "y": dp % 2, "x": seq // 2, "c": seq % 2}


def partner(here, dim):
    other = dict(here)
    other[dim] = 1 - here[dim]
    return (other["s"] * 4 + other["l"] * 2 + other["y"], other["x"] * 2 + other["c"])


class Reduction:
    def __init__(self, gathered, result, scratch, used):
        self.gathered, self.result = gathered, result
        self.steps = gathered.shape[1] // STEP
        self.tail = used - (self.steps - 1) * STEP
        self.stage, self.land = scratch[0], scratch[1]
        self.lands = [scratch[2 + 4 * f : 6 + 4 * f] for f in range(len(FLOWS))]
        self.send_sem, self.recv_sem, self.load_sem = scratch[-3:]
        self.here = coords()
        self.next, self.ready, self.coming, self.loaded, self.cored = 0, 0, 0, -1, -1
        self.calls, self.idle, self.resting = 0, [], 4 * LAG
        self.pending = []
        self.clock, self.period = 0.0, 3.4

    @staticmethod
    def scratch():
        shapes = [pltpu.VMEM((2, 2, 2, 2, 2, 2, STEP, TILE), F32), pltpu.VMEM((SLOTS, 2, 2, 2, 2, STEP, TILE), F32)]
        for _, rows, _ in FLOWS:
            for k in range(1, 5):
                shapes.append(pltpu.VMEM((SLOTS,) + (2,) * (4 - k) + (rows, TILE), F32))
        return shapes + [pltpu.SemaphoreType.DMA((SLOTS, COPIES)), pltpu.SemaphoreType.DMA((SLOTS, COPIES)), pltpu.SemaphoreType.DMA((2,))]

    def enter(self):
        barrier = pltpu.get_barrier_semaphore()
        for dim in "c" + DIMS:
            pl.semaphore_signal(barrier, inc=1, device_id=partner(self.here, dim), device_id_type=MESH)
        pl.semaphore_wait(barrier, 5)

    def load(self, t):
        rows = pl.ds(pl.multiple_of(t * STEP, 8), STEP)
        whole = self.gathered.reshape(2, 2, 2, 2, 2, self.gathered.shape[1], TILE)
        return pltpu.make_async_copy(whole.at[:, :, :, :, :, rows, :], self.stage.at[lax.rem(t, 2)], self.load_sem.at[lax.rem(t, 2)])

    def core_copy(self, t):
        slot = lax.rem(t, SLOTS)
        return pltpu.make_async_remote_copy(
            src_ref=self.stage.at[lax.rem(t, 2), :, :, :, :, 1 - self.here["c"]],
            dst_ref=self.land.at[slot],
            send_sem=self.send_sem.at[slot, COPIES - 1],
            recv_sem=self.recv_sem.at[slot, COPIES - 1],
            device_id=partner(self.here, "c"),
            device_id_type=MESH,
        )

    def half(self, t, flow, k, kept):
        first, rows, order = FLOWS[flow]
        left = [dim for dim in DIMS if dim not in order[:k]]
        side = self.here[order[k]] if kept else 1 - self.here[order[k]]
        at = (lax.rem(t, SLOTS),) + tuple(side if dim == order[k] else slice(None) for dim in left)
        if k == 0:
            return self.land.at[at + (pl.ds(first, rows),)]
        return self.lands[flow][k - 1].at[at]

    def copy(self, t, flow, k):
        slot = lax.rem(t, SLOTS)
        return pltpu.make_async_remote_copy(
            src_ref=self.half(t, flow, k, False),
            dst_ref=self.lands[flow][k].at[slot],
            send_sem=self.send_sem.at[slot, flow * 4 + k],
            recv_sem=self.recv_sem.at[slot, flow * 4 + k],
            device_id=partner(self.here, FLOWS[flow][2][k]),
            device_id_type=MESH,
        )

    def advance(self, k, t):
        slot = lax.rem(t, SLOTS)
        if k == 1:
            self.core_copy(t).wait()
            self.land[slot] += self.stage[lax.rem(t, 2), :, :, :, :, self.here["c"]]
        always = [flow for flow in range(len(FLOWS)) if FLOWS[flow][0] < self.tail]
        others = [flow for flow in range(len(FLOWS)) if FLOWS[flow][0] >= self.tail]
        self.exchange(k, t, slot, always)
        if others:
            @pl.when(t < self.steps - 1)
            def _():
                self.exchange(k, t, slot, others)

    def exchange(self, k, t, slot, flows):
        if k == 1:
            for flow in flows:
                self.copy(t, flow, 0).start()
            return
        for flow in flows:
            self.copy(t, flow, k - 2).wait()
            kept = self.half(t, flow, k - 2, True)
            if k < 5:
                self.lands[flow][k - 2][slot] += kept[...]
                self.copy(t, flow, k - 1).start()
            else:
                first, rows, _ = FLOWS[flow]
                at = pl.ds(pl.multiple_of(t * STEP + first, 8), rows)
                self.result[at, :] = self.lands[flow][3][slot] + kept[...]

    def entry(self, call):
        step, begun = call, call >= 0
        for idle in self.idle:
            step = step - jnp.where(call > idle, 1, 0)
            begun = begun & (call != idle)
        return step, begun

    def carry(self, call):
        for k in range(2, 6):
            t, begun = self.entry(call - LAG * (k - 1))

            @pl.when(begun & (t < self.steps))
            def _():
                self.advance(k, t)

    def call(self, call, fresh):
        t, _ = self.entry(call)

        @pl.when(t < self.steps)
        def _():
            self.advance(1, t)

        @pl.when(t + 1 < fresh)
        def _():
            self.load(t + 1).wait()
            self.core_copy(t + 1).start()

        @pl.when(t + 2 < fresh)
        def _():
            self.load(t + 2).start()

        self.carry(call)

    def settle(self):
        for wait in self.pending:
            wait()
        self.pending = []
        self.ready = self.coming
        self.fetch()

    def fetch(self):
        for t in (self.next, self.next + 1):
            if self.loaded < t < self.ready // STEP:
                self.load(t).start()
                self.loaded = t

    def prime(self):
        first = self.next
        if first >= self.ready // STEP:
            return
        self.fetch()
        if self.cored < first:
            self.load(first).wait()
            self.core_copy(first).start()
            self.cored = first

    def begun(self, calls):
        fresh = self.ready // STEP
        self.calls += calls
        self.next += calls
        self.cored, self.loaded = min(self.next, fresh - 1), min(self.next + 1, fresh - 1)
        self.resting = 0
        self.clock = 0.0

    def rested(self, calls):
        self.calls += calls
        self.resting += calls
        self.clock = 0.0

    def loop(self, count, body, spent):
        every = max(1, round(self.period / spent))
        lead = max(1, math.ceil((self.period - self.clock) / spent))
        room = 1 + (count - lead) // every if count >= lead else 0
        start, fresh = self.calls, self.ready // STEP
        calls = min(room, fresh - self.next)
        idle = min(room, 4 * LAG - self.resting) if self.next >= fresh else 0
        spare = self.clock + count * spent
        if calls > 0:
            self.prime()
            step = lambda index: self.call(start + index, fresh)
            self.begun(calls)
        elif idle > 0:
            calls = idle
            self.idle.extend(range(start, start + calls))
            step = lambda index: self.carry(start + index)
            self.rested(calls)
        else:
            each(count, body)
            self.settle()
            self.clock = spare
            return
        last = lead - 1 + (calls - 1) * every

        def one(index):
            body(index)

            @pl.when((index >= lead - 1) & (index <= last) & (lax.rem(index - (lead - 1), every) == 0))
            def _():
                step(lax.div(index - (lead - 1), every))

        each(count, one)
        self.settle()
        self.clock = (count - 1 - last) * spent

    def tick(self, spent=0.0):
        self.clock += spent
        if spent > 0.0:
            self.settle()
        last = self.ready // STEP - 1
        if self.next <= last:
            if self.cored < self.next:
                self.prime()
                return
            if self.clock >= self.period:
                self.prime()
                self.call(self.calls, last + 1)
                self.begun(1)
        elif self.resting < 4 * LAG and self.clock >= self.period:
            self.idle.append(self.calls)
            self.carry(self.calls)
            self.rested(1)

    def finish(self, beside):
        self.settle()
        first, fresh, start = self.next, self.ready // STEP, self.calls
        self.prime()

        def one(index):
            self.call(start + index, fresh)
            beside(index)

        each(max(self.steps - first + 4 * LAG, 6), one)

    def send(self, place, sems, tile, rows, count, spent, slots=2, group=1):
        self.settle()
        start = self.ready

        def copy(slot, at):
            return pltpu.make_async_copy(place(slot), self.gathered.at[:, pl.ds(at, group * rows), :], sems.at[slot])

        def body(n):
            slot = lax.rem(n, slots)

            @pl.when(n >= slots)
            def _():
                copy(slot, start).wait()

            value = tile(n)
            for block in range(group):
                part = value[:, block * TILE : (block + 1) * TILE].reshape(32, rows, TILE)
                place(slot).at[:, pl.ds(block * rows, rows), :][...] = part
            copy(slot, pl.multiple_of(start + n * group * rows, 8)).start()

        self.loop(count, body, spent)
        for n in range(max(count - slots, 0), count):
            self.pending.append(functools.partial(lambda slot: copy(slot, start).wait(), n % slots))
        self.coming = start + count * group * rows


def backward_kernel(
    erows, drows, used,
    counts, positions, enc_gain_one, enc_gain_two, token, dec_gain_one, dec_gain_two, table, encoded, embed, dec_qkv, dec_out, dec_up, dec_down, cotangent,
    enc_qkv, enc_out, enc_up, enc_down,
    enc_normed_one, enc_inverse_one, enc_packed, enc_kept, enc_mixed, enc_normed_two, enc_inverse_two, enc_active, enc_slope,
    result, input_grad, gathered, kept_active, kept_middle, reduced, vector_sum,
    padded_positions, grad_embedded, filled, vector_part, vector_land, vector_send, vector_recv, dec_sems, enc_sems, tile_sems, *scratch,
):
    images, places, dwidth = cotangent.shape
    slots, width = input_grad.shape[1:]
    dhidden, hidden = dec_up.shape[1], enc_up.shape[1]
    dtotal, etotal = images * drows, images * erows
    reduction = Reduction(gathered, reduced, scratch, used)
    mask_token, dec_gain_one, dec_gain_two = as_row(token), as_row(dec_gain_one), as_row(dec_gain_two)
    row = lax.broadcasted_iota(jnp.int32, (drows, 1), 0)
    padded_positions[:images, :slots] = positions[...]
    vector_part[...] = jnp.zeros_like(vector_part)

    def pick_of(image):
        place = lax.broadcasted_iota(jnp.int32, (drows, erows), 0)
        slot = lax.broadcasted_iota(jnp.int32, (drows, erows), 1)
        named = (padded_positions[image : image + 1, :erows] == place) & (slot < counts[image])
        return jnp.where(named, 1.0, 0.0)

    beside = reduction.loop

    def decoder(
        qkv, out, up, down, normed_one, inverse_one, packed, kept, mixed, middle, normed_two, inverse_two, slope, wide_low, stage
    ):
        into_result = pltpu.make_async_copy(cotangent, result, dec_sems.at[0])
        weights = [(dec_qkv, qkv), (dec_out, out), (dec_up, up), (dec_down, down)]
        loads = [pltpu.make_async_copy(source, target, dec_sems.at[1 + i]) for i, (source, target) in enumerate(weights)]

        def fill(table_in, encoded_in, embed_in):
            starts = [(encoded, encoded_in), (embed, embed_in), (table, table_in)]
            starts = [pltpu.make_async_copy(source, target, dec_sems.at[5 + i]) for i, (source, target) in enumerate(starts)]
            for copy in starts + loads + [into_result]:
                copy.start()
            starts[0].wait()
            starts[1].wait()
            high, rest = mixed, wide_low

            def embed_tile(tile):
                value = nn(encoded_in[...], embed_in[:, columns(tile)])
                top = value.astype(BF)
                high[pl.ds(0, etotal), columns(tile)] = top
                rest[pl.ds(0, etotal), columns(tile)] = (value - top.astype(F32)).astype(BF)

            each(dwidth // TILE, embed_tile)
            starts[2].wait()
            for image in range(images):
                pick = pick_of(image)
                low_pick = pick.astype(BF)
                at = pl.ds(image * erows, erows)
                picked = nn(low_pick, high[at, :]) + nn(low_pick, rest[at, :])
                covered = jnp.sum(pick, axis=1, keepdims=True) > 0.5
                value = jnp.where(covered, picked, mask_token) + table_in[...]
                filled[pl.ds(image * drows, drows), :] = jnp.where(row < places, value, 0.0).astype(BF)

        pl.run_scoped(
            fill, pltpu.VMEM(table.shape, F32), pltpu.VMEM(encoded.shape, BF), pltpu.VMEM(embed.shape, BF)
        )
        norm_rows(dtotal, filled, dec_gain_one, normed_one, inverse_one)
        loads[0].wait()

        project(normed_one, qkv, packed)

        def mix(image):
            for group in range(dwidth // LANES):
                attend_block(packed, dwidth, drows, dwidth // DHEADS, image, group, places, kept, mixed)

        each(images, mix)
        loads[1].wait()

        middle[...] = filled[...].astype(F32) + nn(mixed[...], out[...])
        norm_rows(dtotal, middle, dec_gain_two, normed_two, inverse_two)
        loads[2].wait()
        grad_low = wide_low
        into_result.wait()
        pad_images(result, grad_low, drows)
        block = dwidth // 32

        def place(slot):
            return stage.at[:, pl.ds(pl.multiple_of(slot * block, 8), block), :]

        def place_two(slot):
            return stage.at[:, pl.ds(pl.multiple_of(slot * 2 * block, 8), 2 * block), :]

        def feed(active):
            feed_up(normed_two, up, active, slope)
            keep = [(active, kept_active, dec_sems.at[0]), (middle, kept_middle, dec_sems.at[1])]
            keep = [pltpu.make_async_copy(*copy) for copy in keep]
            for copy in keep:
                copy.start()
            reduction.enter()
            loads[3].wait()
            for tile in range(dwidth // TILE):
                at = slice(tile * TILE, (tile + 1) * TILE)
                reduction.send(lambda slot: stage, tile_sems, lambda n: tn(active[...], grad_low[:, at]), dhidden // 32, 1, 1.9, slots=1)
                if tile == 0:
                    feed_back(grad_low, down, slope, slope, beside, 4.0)
                    reduction.tick()
            for copy in keep:
                copy.wait()

        pl.run_scoped(feed, pltpu.VMEM((dtotal, dhidden), BF))
        reduction.tick()
        half = dhidden // 512 // 2
        for part in range(2):
            reduction.send(place_two, tile_sems, lambda n: tn(normed_two[...], slope[:, span(part * half + n, 512)]), block, half, 1.0, group=2)
            reduction.tick()
        times_back(slope, up, middle, beside, 3.3)
        reduction.tick()
        grad_attend = wide_low

        def keep_middle(at, grad):
            middle[at, :] = grad
            grad_attend[at, :] = grad.astype(BF)

        def late(wide, partial):
            vector_part[0, 4:5, :dwidth] = norm_back(
                dtotal, middle, normed_two, inverse_two, dec_gain_two, grad_low, keep_middle, partial
            )
            reduction.tick(2.2)
            reduction.send(place_two, tile_sems, lambda n: tn(mixed[...], grad_attend[...]), block, 1, 1.4, group=dwidth // TILE)
            reduction.tick()
            grad_mixed = normed_two
            times_back(grad_attend, out, grad_mixed, beside, 1.4)
            reduction.tick()
            groups = dwidth // LANES // 2
            half = dwidth // TILE // 2
            for part in range(2):
                def mix_back(image):
                    for group in range(part * groups, (part + 1) * groups):
                        attend_back_block(packed, dwidth, drows, dwidth // DHEADS, image, group, kept, grad_mixed, packed)

                reduction.loop(images, mix_back, 1.05)
                reduction.tick()
                tile = lambda n: tn(normed_one[...], packed[:, columns(lax.div(n, half) * 2 * half + part * half + lax.rem(n, half))])
                reduction.send(place, tile_sems, tile, block, 3 * half, 0.65)
                reduction.tick()
            times_back(packed, qkv, wide, beside, 2.7)
            reduction.tick()

            def keep_filled(at, grad):
                filled[at, :] = grad.astype(BF)

            vector_part[0, 3:4, :dwidth] = norm_back(
                dtotal, wide, normed_one, inverse_one, dec_gain_one, middle, keep_filled, partial
            )
            reduction.tick(2.2)

        pl.run_scoped(late, pltpu.VMEM((dtotal, dwidth), F32), pltpu.VMEM((8, dwidth), F32))
    dgroups, dheads = dwidth // LANES, DHEADS * LANES // dwidth
    wide_shape = (dtotal, dwidth)
    pl.run_scoped(
        decoder,
        *[pltpu.VMEM(ref.shape, BF) for ref in (dec_qkv, dec_out, dec_up, dec_down)],
        pltpu.VMEM(wide_shape, BF), pltpu.VMEM((dtotal, 1), F32), pltpu.VMEM((dtotal, 3 * dwidth), BF),
        pltpu.VMEM((images, dgroups, dheads * drows, drows), BF), pltpu.VMEM(wide_shape, BF), pltpu.VMEM(wide_shape, F32),
        pltpu.VMEM(wide_shape, BF), pltpu.VMEM((dtotal, 1), F32), pltpu.VMEM((dtotal, dhidden), BF), pltpu.VMEM(wide_shape, BF),
        pltpu.VMEM((32, dhidden // 32, TILE), F32),
    )

    def encoder(
        embed_in, out, weight, down, normed_one, inverse_one, packed, kept, mixed, normed_two, inverse_two, grad_pre,
        grad_low, grad_attend, middle, wide, stage,
    ):
        sources = [
            (embed, embed_in), (enc_down, down), (enc_slope, grad_pre), (enc_normed_two, normed_two), (enc_up, weight),
            (enc_inverse_two, inverse_two), (enc_out, out), (enc_mixed, mixed), (enc_packed, packed), (enc_kept, kept),
            (enc_normed_one, normed_one), (enc_inverse_one, inverse_one),
        ]
        loads = [pltpu.make_async_copy(source, target, enc_sems.at[i]) for i, (source, target) in enumerate(sources)]
        block = width // 32

        def place(slot):
            return stage.at[:, pl.ds(pl.multiple_of(slot * block, 8), block), :]

        def place_two(slot):
            return stage.at[:, pl.ds(pl.multiple_of(slot * 2 * block, 8), 2 * block), :]

        def feed(active, encoded_in):
            starts = [(encoded, encoded_in), (enc_active, active)]
            starts = [pltpu.make_async_copy(source, target, enc_sems.at[len(loads) + i]) for i, (source, target) in enumerate(starts)]
            for copy in starts + loads:
                copy.start()
            for image in range(images):
                grad = filled[pl.ds(image * drows, drows), :]
                grad_embedded[pl.ds(image * erows, erows), :] = tn(pick_of(image).astype(BF), grad).astype(BF)
            reduction.tick(2.0)
            loads[0].wait()
            reduction.tick()
            value = nt(grad_embedded[...], embed_in[...])
            wide[...] = value
            grad_low[...] = value.astype(BF)
            reduction.tick(1.2)
            starts[1].wait()
            for tile in range(width // TILE):
                at = slice(tile * TILE, (tile + 1) * TILE)
                reduction.send(lambda slot: stage, tile_sems, lambda n: tn(active[...], grad_low[:, at]), hidden // 32, 1, 1.7, slots=1)
                reduction.tick()
            starts[0].wait()
            reduction.send(place_two, tile_sems, lambda n: tn(encoded_in[...], grad_embedded[...]), block, 1, 1.8, group=dwidth // TILE)
            reduction.tick()
            reduction.settle()

        pl.run_scoped(feed, pltpu.VMEM(enc_active.shape, BF), pltpu.VMEM(encoded.shape, BF))
        reduction.period = 2.5
        reduction.tick()
        loads[1].wait()
        loads[2].wait()
        feed_back(grad_low, down, grad_pre, grad_pre, beside, 4.6)
        reduction.tick()
        loads[3].wait()
        reduction.send(place_two, tile_sems, lambda n: tn(normed_two[...], grad_pre[:, span(n, 512)]), block, hidden // 512, 1.0, group=2)
        reduction.tick()
        loads[4].wait()
        times_back(grad_pre, weight, middle, beside, 3.9)
        reduction.tick()
        into_qkv = pltpu.make_async_copy(enc_qkv, weight.at[:, : enc_qkv.shape[1]], enc_sems.at[len(loads) + 2])
        into_qkv.start()
        loads[5].wait()

        def late(grad_mixed, partial, input_stage):
            def keep_middle(at, grad):
                middle[at, :] = grad
                grad_attend[at, :] = grad.astype(BF)

            vector_part[0, 1:2, :] = norm_back(etotal, middle, normed_two, inverse_two, as_row(enc_gain_two), wide, keep_middle, partial)
            loads[6].wait()
            loads[7].wait()
            reduction.tick(1.5)
            reduction.send(place, tile_sems, lambda n: tn(mixed[...], grad_attend[:, columns(n)]), block, width // TILE, 0.7)
            reduction.tick()
            times_back(grad_attend, out, grad_mixed, beside, 1.5)
            for load in loads[8:]:
                load.wait()
            reduction.tick()

            def mix_back(image):
                for group in range(width // LANES):
                    attend_back_block(packed, width, erows, width // HEADS, image, group, kept, grad_mixed, packed)

            reduction.loop(images, mix_back, 1.4)
            reduction.tick()
            reduction.send(place, tile_sems, lambda n: tn(normed_one[...], packed[:, columns(n)]), block, 3 * width // TILE, 0.58)
            reduction.settle()
            left = gathered.shape[1] - reduction.ready
            if left:
                stage[:, :left, :] = jnp.zeros((32, left, TILE), F32)
                rest = pltpu.make_async_copy(
                    stage.at[:, pl.ds(0, left), :], gathered.at[:, pl.ds(reduction.ready, left), :], tile_sems.at[0]
                )
                rest.start()
                reduction.pending.append(rest.wait)
                reduction.coming += left
            into_qkv.wait()
            reduction.tick()
            times_back(packed, weight.at[:, : enc_qkv.shape[1]], wide, beside, 3.1)
            reduction.tick()

            def keep_input(at, grad):
                wide[at, :] = grad

            vector_part[0, 0:1, :] = norm_back(etotal, wide, normed_one, inverse_one, as_row(enc_gain_one), middle, keep_input, partial)
            reduction.tick(1.5)
            for image in range(images):
                input_stage[image] = wide[image * erows : image * erows + slots, :]
            store = pltpu.make_async_copy(input_stage, input_grad, tile_sems.at[0])
            store.start()
            reduction.tick(1.5)
            store.wait()

        pl.run_scoped(
            late, pltpu.VMEM((etotal, width), BF), pltpu.VMEM((8, width), F32), pltpu.VMEM(input_grad.shape, F32)
        )

    pl.run_scoped(
        encoder,
        pltpu.VMEM(embed.shape, BF), pltpu.VMEM(enc_out.shape, BF), pltpu.VMEM(enc_up.shape, BF), pltpu.VMEM(enc_down.shape, BF),
        pltpu.VMEM(enc_normed_one.shape, BF), pltpu.VMEM(enc_inverse_one.shape, F32), pltpu.VMEM(enc_packed.shape, BF),
        pltpu.VMEM(enc_kept.shape, BF), pltpu.VMEM(enc_mixed.shape, BF), pltpu.VMEM(enc_normed_two.shape, BF),
        pltpu.VMEM(enc_inverse_two.shape, F32), pltpu.VMEM(enc_slope.shape, BF),
        pltpu.VMEM((etotal, width), BF), pltpu.VMEM((etotal, width), BF), pltpu.VMEM((etotal, width), F32), pltpu.VMEM((etotal, width), F32),
        pltpu.VMEM((32, hidden // 32, TILE), F32),
    )
    def finish_decoder(active, middle, down):
        loads = [(kept_active, active), (kept_middle, middle), (dec_down, down)]
        loads = [pltpu.make_async_copy(source, target, dec_sems.at[i]) for i, (source, target) in enumerate(loads)]
        for load in loads:
            load.start()
        reduction.tick()
        for load in loads:
            load.wait()
        for tile in range(dwidth // TILE):
            at = slice(tile * TILE, (tile + 1) * TILE)
            value = (middle[:, at] + nn(active[...], down[:, at])).astype(BF)
            for image in range(images):
                result[image, :, at] = value[image * drows : image * drows + places]
            reduction.tick(1.75)
        token_grad = jnp.zeros((1, dwidth), F32)
        for image in range(images):
            covered = jnp.sum(pick_of(image), axis=1, keepdims=True) > 0.5
            grad = filled[pl.ds(image * drows, drows), :]
            token_grad = token_grad + jnp.sum(jnp.where(covered | (row >= places), 0.0, grad.astype(F32)), axis=0, keepdims=True)
        vector_part[0, 2:3, :dwidth] = token_grad
        reduction.tick(1.5)

    pl.run_scoped(
        finish_decoder, pltpu.VMEM((dtotal, dhidden), BF), pltpu.VMEM((dtotal, dwidth), F32), pltpu.VMEM(dec_down.shape, BF)
    )
    order = "c" + DIMS

    def vector_copy(k):
        return pltpu.make_async_remote_copy(
            src_ref=vector_part.at[k],
            dst_ref=vector_land.at[k],
            send_sem=vector_send.at[k],
            recv_sem=vector_recv.at[k],
            device_id=partner(reduction.here, order[k]),
            device_id_type=MESH,
        )

    def vector_step(index):
        for k in range(6):
            @pl.when(index == k)
            def _():
                if k:
                    vector_copy(k - 1).wait()
                    vector_part[k] = vector_part[k - 1] + vector_land[k - 1]
                if k < 5:
                    vector_copy(k).start()

    reduction.finish(vector_step)
    vector_sum[...] = vector_part[5]


def unpack_kernel(halved, source, vector_sum, result_in, grad_in, *targets):
    *targets, result, grad, sems = targets
    matrices, vectors = targets[:9], targets[9:]
    copies = [pltpu.make_async_copy(result_in, result, sems.at[0]), pltpu.make_async_copy(grad_in, grad, sems.at[1])]
    for copy in copies:
        copy.start()
    index = lax.axis_index("dp") * lax.axis_size("seq") + lax.axis_index("seq")
    width = vector_sum.shape[1]
    for row, vector in enumerate(vectors):
        size = vector.shape[0]
        own = pltpu.roll(vector_sum[...], lax.rem(width - index * size, width), 1)
        vector[...] = own[row, :size]
    at = 0
    for index, target in enumerate(matrices):
        block, width = target.shape
        tiles = list(range(width // TILE))
        if index == halved:
            half = len(tiles) // 6
            tiles = [n // half * 2 * half + part * half + n % half for part in range(2) for n in range(3 * half)]
        for n in tiles:
            target[:, n * TILE : (n + 1) * TILE] = source[at : at + block, :]
            at += block
    for copy in copies:
        copy.wait()


def vmem(count):
    return [pl.BlockSpec(memory_space=pltpu.VMEM)] * count


def anywhere(count):
    return [pl.BlockSpec(memory_space=pl.ANY)] * count


def shapes(*pairs):
    return [jax.ShapeDtypeStruct(shape, dtype) for shape, dtype in pairs]


def scratches(*pairs):
    return [pltpu.VMEM(shape, dtype) for shape, dtype in pairs]


def fast_local(
    enc_input, keep_count, keep_positions,
    enc_gain_one, enc_qkv_weight, enc_out_weight, enc_gain_two, enc_up_weight, enc_down_weight,
    embed_weight, mask_token,
    dec_gain_one, dec_qkv_weight, dec_out_weight, dec_gain_two, dec_up_weight, dec_down_weight,
    cotangent,
):
    images, slots, width = enc_input.shape
    places, dwidth = cotangent.shape[1:]
    hidden, dhidden = enc_up_weight.shape[1], dec_up_weight.shape[1]
    erows, drows = padded(slots, 16), padded(places, 16)
    etotal, dtotal = images * erows, images * drows
    egroups, dgroups = width // LANES, dwidth // LANES
    eheads, dheads = HEADS // egroups, DHEADS // dgroups
    smem = [pl.BlockSpec(memory_space=pltpu.SMEM)]
    settings = functools.partial(pltpu.CompilerParams, vmem_limit_bytes=VMEM_BYTES)
    vectors = (enc_gain_one, enc_gain_two, mask_token, dec_gain_one, dec_gain_two)

    saved = shapes(
        ((etotal, width), BF), ((etotal, 1), F32), ((etotal, 3 * width), BF), ((images, egroups, eheads * erows, erows), BF),
        ((etotal, width), BF), ((etotal, width), BF), ((etotal, 1), F32), ((etotal, hidden), BF), ((etotal, hidden), BF), ((etotal, width), BF),
    )
    normed_one, inverse_one, packed, kept, mixed, normed_two, inverse_two, active, slope, encoded = pl.pallas_call(
        functools.partial(enc_forward_kernel, erows),
        name="enc_forward",
        out_shape=saved,
        in_specs=smem + vmem(3) + anywhere(4),
        out_specs=anywhere(10),
        scratch_shapes=scratches(
            *((weight.shape, BF) for weight in (enc_qkv_weight, enc_out_weight, enc_up_weight, enc_down_weight)),
            ((etotal, width), BF), ((etotal, width), F32), *((array.shape, array.dtype) for array in saved),
        ) + [pltpu.SemaphoreType.DMA((4,)), pltpu.SemaphoreType.DMA((10,))],
        compiler_params=settings(),
    )(keep_count, enc_input, enc_gain_one, enc_gain_two, enc_qkv_weight, enc_out_weight, enc_up_weight, enc_down_weight)

    table = jnp.asarray(position_rows(places, dwidth, drows))
    block = dwidth // 32
    eblock = width // 32
    layout = (
        (dhidden // 32, dwidth), (block, dhidden), (block, dwidth), (block, 3 * dwidth), (hidden // 32, width),
        (eblock, dwidth), (eblock, hidden), (eblock, width), (eblock, 3 * width),
    )
    used = sum(rows * columns // TILE for rows, columns in layout)
    share_rows = padded(used, STEP)
    dec_output, input_grad, _, _, _, reduced, vector_sum = pl.pallas_call(
        functools.partial(backward_kernel, erows, drows, used),
        name="backward",
        out_shape=shapes(
            (cotangent.shape, BF), (enc_input.shape, F32), ((32, share_rows, TILE), F32), ((dtotal, dhidden), BF), ((dtotal, dwidth), F32),
            ((share_rows, TILE), F32), ((8, width), F32),
        ),
        in_specs=smem + vmem(6) + anywhere(21),
        out_specs=vmem(1) + anywhere(4) + vmem(2),
        scratch_shapes=scratches(
            ((8, LANES), jnp.int32), ((etotal, dwidth), BF), ((dtotal, dwidth), BF), ((6, 8, width), F32), ((5, 8, width), F32),
        ) + [pltpu.SemaphoreType.DMA((count,)) for count in (5, 5, 8, 15, 2)] + Reduction.scratch(),
        compiler_params=settings(collective_id=0, has_side_effects=True),
    )(
        keep_count, keep_positions, *vectors, table, encoded, embed_weight, dec_qkv_weight, dec_out_weight, dec_up_weight, dec_down_weight,
        cotangent, enc_qkv_weight, enc_out_weight, enc_up_weight, enc_down_weight,
        normed_one, inverse_one, packed, kept, mixed, normed_two, inverse_two, active, slope,
    )
    dec_down, dec_up, dec_out, dec_qkv, enc_down, embed, enc_up, enc_out, enc_qkv, *cuts, dec_output, input_grad = pl.pallas_call(
        functools.partial(unpack_kernel, 3),
        name="unpack",
        out_shape=shapes(
            *((shape, F32) for shape in layout), *(((vector.shape[0] // 32,), F32) for vector in vectors),
            (cotangent.shape, BF), (enc_input.shape, F32),
        ),
        in_specs=vmem(2) + anywhere(2),
        out_specs=vmem(11 + len(vectors)),
        scratch_shapes=[pltpu.SemaphoreType.DMA((2,))],
    )(reduced, vector_sum, dec_output, input_grad)
    return (
        dec_output, input_grad, cuts[0], enc_qkv, enc_out, cuts[1], enc_up, enc_down, embed, cuts[2],
        cuts[3], dec_qkv, dec_out, cuts[4], dec_up, dec_down,
    )


def position_rows(places, width, rows):
    side = math.isqrt(places)
    quarter = width // 4
    place = np.arange(places)
    rate = 1.0 / 10000.0 ** (np.arange(quarter) / quarter)
    across, down = place[:, None] % side * rate, place[:, None] // side * rate
    table = np.concatenate([np.sin(across), np.cos(across), np.sin(down), np.cos(down)], axis=1)
    return np.pad(table, ((0, rows - places), (0, 0))).astype(np.float32)


def solution(mesh):
    placed = (
        P(("dp", "seq"), None, None),
        P(("dp", "seq")),
        P(("dp", "seq"), None),
        P(),
        P(),
        P(),
        P(),
        P(),
        P(),
        P(),
        P(),
        P(),
        P(),
        P(),
        P(),
        P(),
        P(),
        P(("dp", "seq"), None, None),
    )
    fast = (mesh.shape["dp"], mesh.shape["seq"]) == (8, 4)
    return jax.shard_map(
        fast_local if fast else local,
        mesh=mesh,
        in_specs=placed,
        out_specs=(
            P(("dp", "seq"), None, None),
            P(("dp", "seq"), None, None),
            P(("dp", "seq")),
            P(("dp", "seq"), None),
            P(("dp", "seq"), None),
            P(("dp", "seq")),
            P(("dp", "seq"), None),
            P(("dp", "seq"), None),
            P(("dp", "seq"), None),
            P(("dp", "seq")),
            P(("dp", "seq")),
            P(("dp", "seq"), None),
            P(("dp", "seq"), None),
            P(("dp", "seq")),
            P(("dp", "seq"), None),
            P(("dp", "seq"), None),
        ),
        check_vma=False,
    )
```
